128 devices in a mesh: group: 8 (over x_lo, z), tp: 16 (over x_hi, y, core).
Axes of the slice: x: 4 (x_hi: 2, x_lo: 2; x = x_hi * 2 + x_lo), y: 4, z: 4, core: 2. Of those that a mesh axis runs over, the one named last changes fastest.
Arguments:
- layer_input: bfloat16 [8, 256, 8192], P('group', None, 'tp'), may hold values from -6 to 6
- query_weight: bfloat16 [8192, 4096], P(None, 'tp'), may hold values from -0.1875 to 0.1875
- kv_weight: bfloat16 [8192, 2048], P(None, 'tp'), may hold values from -0.1875 to 0.1875
- out_weight: bfloat16 [4096, 8192], P('tp'), may hold values from -0.125 to 0.125
- cache_keys: bfloat16 [8, 64, 4096, 128], P('group', None, 'tp'), may hold values from -480 to 480
- cache_values: bfloat16 [8, 64, 4096, 128], P('group', None, 'tp'), may hold values from -6 to 6
- lengths: int32 [8, 64], P('group'), may hold values from 1 to 512, as said below
- placement: int32 [16, 2], replicated, may hold values from 0 to 7, as said below
Outputs:
- projected: bfloat16 [8, 256, 8192], P('group', None, 'tp')
- incoming: bfloat16 [8, 4, 128, 256], P('group', None, 'tp')
The draws below stay inside these ranges and needn't reach their ends.
Inputs may be any that keep to these rules, and one draw needn't show every extreme that they name: `lengths`: each group has a row of length 512. `placement`: column 0 is a decode group from 1 to 7 and column 1 a slot below 4; no two blocks share a group and slot; some group receives 4 blocks, and the group whose index is half of 8, rounded down, receives at least one.
All inputs are finite; a program needn't handle non-finite values.
Results may differ from the reference program's by a relative error of at most 0.03.
Values may be sent and summed in bfloat16 or wider, within the bound.
No kernel may reach another device: no remote copies, remote signals or barrier semaphores. Data moves between devices by JAX's collectives and lax.ppermute only.
A program may use at most 128 MiB of HBM per device.

```python
import jax
import jax.numpy as jnp
from jax import lax

D = 8192
HD = 128
QH = 32
KVH = 8
STEPS = 4
NPR = 2
BS = 16
R = 64
L = 512
GQ = 4
KVW = 1024
TOK = 256
CH = 128
RP = 32
NBLK = 16
GROUPS = 8
SLOTS = 4


def draw_cache_keys(key, part):
    key = jax.random.fold_in(key, 11)
    first = jax.random.fold_in(key, 0)
    shape = (GROUPS, R, KVH * L, HD)
    values = 1.5 * jax.random.truncated_normal(first, -4.0, 4.0, shape, jnp.float32)
    return values.astype(jnp.bfloat16)


def draw_lengths(key, part):
    key = jax.random.fold_in(key, 5)
    first, second = jax.random.split(key)
    drawn = jax.random.randint(first, (GROUPS, R), 1, L + 1)
    full_row = jax.random.randint(second, (GROUPS, 1), 0, R)
    return jnp.where(jnp.arange(R)[None, :] == full_row, L, drawn).astype(jnp.int32)


def draw_placement(key, part):
    key = jax.random.fold_in(key, 7)
    first, second, third = jax.random.split(key, 3)
    cell_count = (GROUPS - 1) * SLOTS
    full_group = jax.random.randint(first, (), 1, GROUPS)
    shuffled = jax.random.permutation(second, cell_count)
    cell_group = 1 + shuffled // SLOTS
    order_index = jnp.arange(cell_count, dtype=jnp.int32)
    first_middle = jnp.argmax(cell_group == GROUPS // 2).astype(jnp.int32)
    ranking = jnp.where(cell_group == full_group, 0, jnp.where(order_index == first_middle, cell_count, 2 * cell_count)) + order_index
    chosen = shuffled[jnp.argsort(ranking)][:NBLK]
    chosen = jax.random.permutation(third, chosen)
    return jnp.stack([1 + chosen // SLOTS, chosen % SLOTS], axis=1).astype(jnp.int32)


def with_spikes(array, key, source, target, blocks, factor):
    owner, partner = [(jnp.arange(array.shape[position]) // (array.shape[position] // blocks)).reshape([-1 if axis == position else 1 for axis in range(array.ndim)]) for position in (source, target)]
    chosen = jax.random.permutation(key, blocks)[partner]
    strong = (owner == chosen) | (owner == (partner + blocks // 2) % blocks)
    return jnp.where(strong, factor * array, array)


def shard_levels(key, dims, cuts, low, top_value):
    def one(dim, shards_of):
        heights = jax.random.uniform(jax.random.fold_in(jax.random.fold_in(key, 6), dim), (shards_of,), jnp.float32, low / len(cuts), top_value / len(cuts))
        return jnp.repeat(jnp.exp(heights), dims[dim] // shards_of).reshape((-1,) + (1,) * (len(dims) - dim - 1))

    level = one(*cuts[0])
    for cut in cuts[1:]:
        level = level * one(*cut)
    return level


def noise(rng, extent, deviation, most, cuts=(), held_as=jnp.bfloat16):
    loudness = shard_levels(rng, extent, cuts, -0.22, 0.18) if cuts else 1.0
    values = jax.random.normal(rng, extent, jnp.float32) * deviation * loudness
    return jnp.minimum(jnp.maximum(values, -most), most).astype(held_as)


def noise_with(stream_key, dims, deviation, limit, cuts, heavy, kind=jnp.bfloat16):
    values = deviation * jax.random.normal(stream_key, dims, jnp.float32)
    if cuts:
        values = values * shard_levels(stream_key, dims, cuts, -0.22, 0.18)
    return jnp.clip(with_spikes(values, jax.random.fold_in(stream_key, 3), *heavy), -limit, limit).astype(kind)


def setup_inputs(seed: int = 0) -> dict:
    key_of = jax.random.split(jax.random.key(seed), 9)
    return {
        "layer_input": noise(key_of[0], (GROUPS, TOK, D), 1.0, 6.0, ((0, 8), (2, 16))),
        "query_weight": noise(key_of[1], (D, QH * HD), (D // 9) ** -0.5, 0.1875, ((1, 16),)),
        "kv_weight": noise(key_of[2], (D, 2 * KVW), (D // 9) ** -0.5, 0.1875, ((1, 16),)),
        "out_weight": noise_with(key_of[3], (QH * HD, D), (QH * HD) ** -0.5, 0.125, ((0, 16),), (0, 1, 16, 2.0)),
        "cache_keys": draw_cache_keys(jax.random.fold_in(key_of[8], 71), 0),
        "cache_values": noise(key_of[5], (GROUPS, R, KVH * L, HD), 1.0, 6.0, ((0, 8), (2, 16))),
        "lengths": draw_lengths(jax.random.fold_in(key_of[8], 71), 0),
        "placement": draw_placement(jax.random.fold_in(key_of[8], 71), 0),
    }


def rotate(values, positions):
    midpoint = values.shape[-1] // 2
    frequency = jnp.exp(-jnp.log(500000.0) * jnp.arange(midpoint, dtype=jnp.float32) * 2.0 / values.shape[-1])
    angles = positions.astype(jnp.float32)[:, None] * frequency[None, :]
    cosine = jnp.cos(angles)[:, None, :]
    sine_term = jnp.sin(angles)[:, None, :]
    first = values[..., :midpoint]
    second = values[..., midpoint:]
    return jnp.concatenate([first * cosine - second * sine_term, second * cosine + first * sine_term], axis=-1)


def attend(query_vectors, key_row_block, value_rows, allowed):
    score_scale = key_row_block.shape[-1] ** -0.5
    scores = jnp.dot(query_vectors, key_row_block.T, preferred_element_type=jnp.float32) * score_scale
    scores = jnp.where(allowed, scores, -jnp.inf)
    largest = jnp.max(scores, axis=1, keepdims=True)
    weights = jnp.where(allowed, jnp.exp(scores - largest), 0.0)
    summed = jnp.sum(weights, axis=1, keepdims=True)
    mixed = jnp.dot(weights.astype(jnp.bfloat16), value_rows, preferred_element_type=jnp.float32)
    return mixed / summed


def reference(layer_input, query_weight, kv_weight, out_weight, cache_keys, cache_values, lengths, placement):
    kv_width = KVH * HD
    prompt_rows = jnp.arange(CH * GQ, dtype=jnp.int32) // GQ
    prompt_causal = jnp.arange(CH, dtype=jnp.int32)[None, :] <= prompt_rows[:, None]
    step_rows = jnp.arange(STEPS * GQ, dtype=jnp.int32) // GQ
    step_causal = jnp.arange(STEPS, dtype=jnp.int32)[None, :] <= step_rows[:, None]
    projected = []
    shipped = None
    for group_index in range(GROUPS):
        tokens = layer_input[group_index]
        row_lengths = lengths[group_index]
        if group_index == 0:
            prefix = jnp.sum(row_lengths.reshape(NPR, RP), axis=1)
            positions = (prefix[:, None] + jnp.arange(CH, dtype=jnp.int32)[None, :]).reshape(TOK)
        else:
            positions = (row_lengths[None, :] + jnp.arange(STEPS, dtype=jnp.int32)[:, None]).reshape(TOK)
        query_vectors = jnp.dot(tokens, query_weight, preferred_element_type=jnp.float32).reshape(TOK, QH, HD)
        query_vectors = rotate(query_vectors, positions).astype(jnp.bfloat16)
        new_pairs = jnp.dot(tokens, kv_weight, preferred_element_type=jnp.float32)
        fresh_keys = rotate(new_pairs[:, :kv_width].reshape(TOK, KVH, HD), positions).astype(jnp.bfloat16)
        new_values = new_pairs[:, kv_width:].reshape(TOK, KVH, HD).astype(jnp.bfloat16)
        group_keys = cache_keys[group_index].reshape(R, KVH, L, HD)
        group_values = cache_values[group_index].reshape(R, KVH, L, HD)
        present = jnp.arange(L, dtype=jnp.int32)[None, :] < row_lengths[:, None]
        if group_index == 0:
            pieces = []
            for prompt in range(NPR):
                prompt_queries = query_vectors[prompt * CH:(prompt + 1) * CH].reshape(CH, KVH, GQ, HD)
                prompt_queries = prompt_queries.transpose(1, 0, 2, 3).reshape(KVH, CH * GQ, HD)
                cached_keys = group_keys[prompt * RP:(prompt + 1) * RP].transpose(1, 0, 2, 3).reshape(KVH, RP * L, HD)
                cached_values = group_values[prompt * RP:(prompt + 1) * RP].transpose(1, 0, 2, 3).reshape(KVH, RP * L, HD)
                stretch_keys = fresh_keys[prompt * CH:(prompt + 1) * CH].transpose(1, 0, 2)
                stretch_values = new_values[prompt * CH:(prompt + 1) * CH].transpose(1, 0, 2)
                all_keys = jnp.concatenate([cached_keys, stretch_keys], axis=1)
                all_values = jnp.concatenate([cached_values, stretch_values], axis=1)
                cached_allowed = jnp.broadcast_to(present[prompt * RP:(prompt + 1) * RP].reshape(1, RP * L), (CH * GQ, RP * L))
                allowed = jnp.concatenate([cached_allowed, prompt_causal], axis=1)
                result = lax.map(lambda operands: attend(operands[0], operands[1], operands[2], allowed), (prompt_queries, all_keys, all_values))
                pieces.append(result.reshape(KVH, CH, GQ, HD).transpose(1, 0, 2, 3).reshape(CH, QH * HD))
            attention = jnp.concatenate(pieces, axis=0)
            paired = jnp.concatenate([fresh_keys, new_values], axis=-1)
            shipped = paired.reshape(NBLK, BS, KVH, 2 * HD).transpose(0, 2, 1, 3).reshape(NBLK, KVH * BS, 2 * HD)
        else:
            row_queries = query_vectors.reshape(STEPS, R, KVH, GQ, HD).transpose(1, 2, 0, 3, 4).reshape(R, KVH, STEPS * GQ, HD)
            step_keys = fresh_keys.reshape(STEPS, R, KVH, HD).transpose(1, 2, 0, 3)
            step_values = new_values.reshape(STEPS, R, KVH, HD).transpose(1, 2, 0, 3)
            all_keys = jnp.concatenate([group_keys, step_keys], axis=2)
            all_values = jnp.concatenate([group_values, step_values], axis=2)
            cached_allowed = jnp.broadcast_to(present[:, None, :], (R, STEPS * GQ, L))
            recent_permitted = jnp.broadcast_to(step_causal[None], (R, STEPS * GQ, STEPS))
            allowed = jnp.concatenate([cached_allowed, recent_permitted], axis=2)
            per_head = jax.vmap(attend, in_axes=(0, 0, 0, None))
            result = jax.vmap(per_head, in_axes=(0, 0, 0, 0))(row_queries, all_keys, all_values, allowed)
            attention = result.reshape(R, KVH, STEPS, GQ, HD).transpose(2, 0, 1, 3, 4).reshape(TOK, QH * HD)
        attention = attention.astype(jnp.bfloat16)
        projected.append(jnp.dot(attention, out_weight, preferred_element_type=jnp.float32).astype(jnp.bfloat16))
    cells = placement[:, 0] * SLOTS + placement[:, 1]
    incoming = jnp.zeros((GROUPS * SLOTS, KVH * BS, 2 * HD), jnp.bfloat16).at[cells].set(shipped)
    return jnp.stack(projected, axis=0), incoming.reshape(GROUPS, SLOTS, KVH * BS, 2 * HD)
```

```python
import jax
import jax.numpy as jnp
from jax import lax
from jax.experimental import pallas as pl
from jax.experimental.pallas import tpu as pltpu
from jax.sharding import PartitionSpec as P

HD = 128
KVH = 8
STEPS = 4
NPR = 2
BS = 16
R = 64
GQ = 4
TOK = 256
CH = 128
RP = 32


NEG_FILL = -1e30


def tp_index(x_hi, y, core):
    return x_hi * 8 + (y % 4) * 2 + core


def moved(shard, x_flip, y_step, core_flip):
    pairs = []
    for x_hi in range(2):
        for y in range(4):
            for core in range(2):
                pairs.append(
                    (
                        tp_index(x_hi, y, core),
                        tp_index(x_hi ^ x_flip, y + y_step, core ^ core_flip),
                    )
                )
    return lax.ppermute(shard, "tp", pairs)


def core_swap(shard):
    return moved(shard, 0, 0, 1)


def turns(positions):
    midpoint = HD // 2
    frequency = jnp.exp(
        -jnp.log(500000.0) * jnp.arange(midpoint, dtype=jnp.float32) * 2.0 / HD
    )
    angles = positions.astype(jnp.float32)[:, None] * frequency[None, :]
    cosine = jnp.cos(angles)
    sine = jnp.sin(angles)
    return (
        jnp.concatenate([cosine, cosine], axis=1),
        jnp.concatenate([-sine, sine], axis=1),
    )


SPAN = 256
CHIPS = 8
SHARD = 512
HALF = TOK // 2
PREFILL_CHUNK = 4096
ROWS_AT_ONCE = 4
LOG2_E = 1.4426950408889634
NT = (((1,), (1,)), ((), ()))


def stacked_heads(queries):
    return jnp.concatenate([queries[:, j * HD : (j + 1) * HD] for j in range(GQ)], axis=0)


def weights_of(scores, largest):
    return jnp.exp2((scores - largest) * (HD**-0.5 * LOG2_E)).astype(jnp.bfloat16)


def with_ones(values):
    return jnp.concatenate([values, jnp.ones_like(values)], axis=1)


def write_heads(mixed_ref, level_ref, rows, mixed, largest):
    count = mixed.shape[0] // GQ
    total = mixed[:, HD : HD + 1]
    normal = (mixed[:, :HD] / total).astype(jnp.bfloat16)
    level = largest * HD**-0.5 + jnp.log(total)
    lane = lax.broadcasted_iota(jnp.int32, (count, GQ), 1)
    levels = jnp.zeros((count, GQ), jnp.float32)
    for j in range(GQ):
        part = slice(j * count, (j + 1) * count)
        mixed_ref[rows, j * HD : (j + 1) * HD] = normal[part]
        levels = jnp.where(lane == j, level[part], levels)
    level_ref[rows, :] = levels


def prefill_kernel(
    query_ref, key_ref, value_ref, bias_ref, mixed_ref, level_ref, keys, values, score_ref, sems
):
    rows = PREFILL_CHUNK // SPAN
    chunks = RP // rows

    def fetches(prompt, step):
        part = pl.ds(prompt * RP + step * rows, rows)
        index = prompt * chunks + step
        return (
            pltpu.make_async_copy(key_ref.at[part], keys.at[part], sems.at[0, index]),
            pltpu.make_async_copy(value_ref.at[part], values.at[part], sems.at[1, index]),
        )

    for prompt in range(NPR):
        for kind in range(2):
            for step in range(chunks):
                fetches(prompt, step)[kind].start()

    def one_prompt(prompt, carry):
        tokens = pl.ds(pl.multiple_of(prompt * CH, CH), CH)
        queries = stacked_heads(query_ref[tokens, :])

        def score_step(step, peak):
            fetches(prompt, step)[0].wait()
            part = keys[pl.ds(prompt * RP + step * rows, rows)].reshape(PREFILL_CHUNK, HD)
            scores = lax.dot_general(queries, part, NT, preferred_element_type=jnp.float32)
            scores = scores + bias_ref[prompt, pl.ds(step, 1), :]
            score_ref[step] = scores
            for lanes in range(PREFILL_CHUNK // HD):
                peak = jnp.maximum(peak, scores[:, lanes * HD : (lanes + 1) * HD])
            return peak

        peak = lax.fori_loop(
            0, chunks, score_step, jnp.full((GQ * CH, HD), NEG_FILL, jnp.float32)
        )
        largest = jnp.max(peak, axis=1, keepdims=True)
        level = jnp.broadcast_to(largest, (GQ * CH, HD))

        def mix_step(step, mixed):
            fetches(prompt, step)[1].wait()
            weights = jnp.concatenate(
                [
                    weights_of(score_ref[step, :, lanes * HD : (lanes + 1) * HD], level)
                    for lanes in range(PREFILL_CHUNK // HD)
                ],
                axis=1,
            )
            part = values[pl.ds(prompt * RP + step * rows, rows)].reshape(PREFILL_CHUNK, HD)
            return mixed + jnp.dot(weights, with_ones(part), preferred_element_type=jnp.float32)

        mixed = lax.fori_loop(0, chunks, mix_step, jnp.zeros((GQ * CH, 2 * HD), jnp.float32))
        write_heads(mixed_ref, level_ref, tokens, mixed, largest)
        return carry

    lax.fori_loop(0, NPR, one_prompt, 0)


def decode_kernel(query_ref, key_ref, value_ref, bias_ref, mixed_ref, level_ref):
    width = ROWS_AT_ONCE * SPAN
    tokens = ROWS_AT_ONCE * STEPS
    owner = lax.broadcasted_iota(jnp.int32, (GQ * tokens, width), 0) % tokens // STEPS
    holder = lax.broadcasted_iota(jnp.int32, (GQ * tokens, width), 1) // SPAN
    for part in range(query_ref.shape[0] // tokens):
        rows = slice(part * tokens, (part + 1) * tokens)
        cached = slice(part * ROWS_AT_ONCE, (part + 1) * ROWS_AT_ONCE)
        queries = stacked_heads(query_ref[rows, :])
        keys = key_ref[cached].reshape(width, HD)
        values = value_ref[cached].reshape(width, HD)
        scores = lax.dot_general(queries, keys, NT, preferred_element_type=jnp.float32)
        scores = jnp.where(owner == holder, scores + bias_ref[part : part + 1, :], NEG_FILL)
        largest = jnp.max(scores, axis=1, keepdims=True)
        mixed = jnp.dot(
            weights_of(scores, largest), with_ones(values), preferred_element_type=jnp.float32
        )
        write_heads(mixed_ref, level_ref, rows, mixed, largest)


def recent_kernel(prefill_ref, query_ref, key_ref, value_ref, mixed_ref, level_ref):
    is_prefill = prefill_ref[0] != 0
    row = lax.broadcasted_iota(jnp.int32, (TOK, TOK), 0)
    column = lax.broadcasted_iota(jnp.int32, (TOK, TOK), 1)
    together = jnp.where(is_prefill, row // CH - column // CH, row % R - column % R) == 0
    allowed = together & (column <= row)
    values = with_ones(value_ref[...])
    lane = lax.broadcasted_iota(jnp.int32, (TOK, GQ), 1)
    levels = jnp.zeros((TOK, GQ), jnp.float32)
    for j in range(GQ):
        head = slice(j * HD, (j + 1) * HD)
        scores = lax.dot_general(
            query_ref[:, head], key_ref[...], NT, preferred_element_type=jnp.float32
        )
        scores = jnp.where(allowed, scores, NEG_FILL)
        largest = jnp.max(scores, axis=1, keepdims=True)
        mixed = jnp.dot(weights_of(scores, largest), values, preferred_element_type=jnp.float32)
        total = mixed[:, HD : HD + 1]
        mixed_ref[:, head] = mixed[:, :HD] / total
        levels = jnp.where(lane == j, largest * HD**-0.5 + jnp.log(total), levels)
    level_ref[...] = levels


def merged(parts, levels):
    top = jnp.maximum(jnp.maximum(levels[0], levels[1]), levels[2])
    shares = [jnp.exp(level - top) for level in levels]
    total = shares[0] + shares[1] + shares[2]
    shares = [share / total for share in shares]
    heads = []
    for j in range(GQ):
        head = slice(j * HD, (j + 1) * HD)
        mixed = jnp.zeros((TOK, HD), jnp.float32)
        for part, share in zip(parts, shares):
            mixed = mixed + part[:, head].astype(jnp.float32) * share[:, j : j + 1]
        heads.append(mixed.astype(jnp.bfloat16))
    return jnp.concatenate(heads, axis=1)


def merge_out_kernel(
    place_ref,
    weight_ref,
    swapped_ref,
    own_ref,
    own_level,
    other_ref,
    other_level,
    recent_ref,
    recent_level,
    plus,
    minus,
    up,
    down,
    next_ref,
    last_ref,
    partner_ref,
    here_ref,
    attention_ref,
    held_ref,
    sems,
):
    core = place_ref[0]
    rows = weight_ref.shape[0]
    copies = []
    for index in range(CHIPS):
        chip = place_ref[1 + index]
        own = pl.ds(pl.multiple_of((2 * chip + core) * SHARD, SHARD), SHARD)
        other = pl.ds(pl.multiple_of(chip * SHARD, SHARD), SHARD)
        pair = (
            pltpu.make_async_copy(
                weight_ref.at[:, own], held_ref.at[index, :rows], sems.at[0, index]
            ),
            pltpu.make_async_copy(
                swapped_ref.at[:, other], held_ref.at[index, rows:], sems.at[1, index]
            ),
        )
        for copy in pair:
            copy.start()
        copies.append(pair)
    attention_ref[...] = merged(
        (own_ref, other_ref, recent_ref), (own_level[...], other_level[...], recent_level[...])
    )
    own = attention_ref[:, pl.ds(pl.multiple_of(core * rows, rows), rows)]
    other = attention_ref[:, pl.ds(pl.multiple_of((1 - core) * rows, rows), rows)]
    joined = jnp.concatenate([own, other], axis=1)

    def product(index):
        for copy in copies[index]:
            copy.wait()
        total = jnp.dot(joined, held_ref[index], preferred_element_type=jnp.float32)
        return total.astype(jnp.bfloat16)

    plus[:TOK] = product(0)
    minus[:TOK] = product(1)
    far = product(2)
    plus[TOK:] = far[:HALF]
    minus[TOK:] = far[HALF:]
    far = product(3)
    up[...] = far[:HALF]
    down[...] = far[HALF:]
    for index, ref in ((4, next_ref), (5, last_ref), (6, partner_ref), (7, here_ref)):
        ref[...] = product(index)


def total_of(*parts):
    total = parts[0].astype(jnp.float32)
    for part in parts[1:]:
        total = total + part.astype(jnp.float32)
    return total.astype(jnp.bfloat16)


def second_message_kernel(
    next_ref, last_ref, partner_ref, from_last, from_next, up, down, plus, minus, partner
):
    plus[:HALF] = total_of(next_ref[:HALF], from_last[TOK:], up[...])
    plus[HALF:] = next_ref[HALF:]
    minus[:HALF] = last_ref[:HALF]
    minus[HALF:] = total_of(last_ref[HALF:], from_next[TOK:], down[...])
    partner[...] = total_of(partner_ref[...], from_last[:TOK], from_next[:TOK])


def total_kernel(here_ref, from_last, from_next, from_partner, out_ref):
    out_ref[...] = total_of(here_ref[...], from_last[...], from_next[...], from_partner[...])


def join_kernel(token_ref, partner_ref, last_ref, next_ref, plus, minus, up, down):
    plus[:TOK] = partner_ref[...]
    plus[TOK:] = last_ref[:HALF]
    minus[:TOK] = partner_ref[...]
    minus[TOK:] = next_ref[HALF:]
    up[...] = last_ref[HALF:]
    down[...] = next_ref[:HALF]


def far_join_kernel(from_last, from_next, upper_ref, lower_ref, far):
    far[:HALF] = upper_ref[...]
    far[HALF:] = lower_ref[...]


def projected_parts(row_ref, shards, query_weight, pair_weight):
    joined = jnp.concatenate(shards, axis=1)
    rows = [
        pl.ds(pl.multiple_of(row_ref[index], SHARD), SHARD) for index in range(len(shards))
    ]
    return [
        jnp.dot(
            joined,
            jnp.concatenate([weight[part, :] for part in rows], axis=0),
            preferred_element_type=jnp.float32,
        )
        for weight in (query_weight, pair_weight)
    ]


def near_kernel(row_ref, query_weight, pair_weight, *refs):
    *shards, query, pair = refs
    query[...], pair[...] = projected_parts(
        row_ref, [ref[...] for ref in shards], query_weight, pair_weight
    )


def far_shards(last_ref, next_ref, far_ref):
    far = jnp.concatenate([last_ref[TOK:], next_ref[TOK:]], axis=0)
    return [last_ref[:TOK], next_ref[:TOK], far, far_ref[...]]


def last_kernel(row_ref, query_weight, pair_weight, query_in, pair_in, *refs):
    *sides, cosine_ref, sine_ref, query_out, pair_out = refs
    shards = far_shards(*sides[:3]) + far_shards(*sides[3:])
    sums = projected_parts(row_ref, shards, query_weight, pair_weight)
    query = query_in[...] + sums[0]
    pair = pair_in[...] + sums[1]
    cosine = cosine_ref[...]
    sine = sine_ref[...]

    def rotated(values):
        return values * cosine + pltpu.roll(values, HD // 2, 1) * sine

    for head in range(query.shape[1] // HD):
        part = slice(head * HD, (head + 1) * HD)
        query_out[:, part] = rotated(query[:, part]).astype(jnp.bfloat16)
    is_key = row_ref[len(shards)] != 0
    pair_out[...] = jnp.where(is_key, rotated(pair), pair).astype(jnp.bfloat16)


def blocks_kernel(cell_ref, key_ref, value_ref, out_ref):
    sliver = out_ref.shape[1]
    out_ref[...] = jnp.zeros_like(out_ref)

    @pl.when(cell_ref[0] != 0)
    def _():
        for block in range(TOK // BS):
            start = pl.multiple_of(cell_ref[1] * sliver, sliver) + block * BS
            cell = cell_ref[2 + block]
            out_ref[cell, :, :HD] = key_ref[pl.ds(start, sliver), :]
            out_ref[cell, :, HD:] = value_ref[pl.ds(start, sliver), :]


def called(kernel, shapes, scalars, *arrays, streamed=(), scratch=(), flops=0, grant=12):
    whole = pl.BlockSpec(memory_space=pltpu.VMEM)
    specs = [pl.BlockSpec(memory_space=pl.ANY)] * len(streamed) + [whole] * len(arrays)
    arrays = tuple(streamed) + arrays
    if scalars is not None:
        specs = [pl.BlockSpec(memory_space=pltpu.SMEM)] + specs
        arrays = (scalars,) + arrays
    return pl.pallas_call(
        kernel,
        in_specs=specs,
        out_specs=tuple(whole for _ in shapes),
        out_shape=tuple(jax.ShapeDtypeStruct(shape, kind) for shape, kind in shapes),
        scratch_shapes=scratch,
        compiler_params=pltpu.CompilerParams(vmem_limit_bytes=grant * 2**20),
        cost_estimate=pl.CostEstimate(flops=flops, transcendentals=0, bytes_accessed=2**21),
    )(*arrays)


def outputs_of(kind):
    return (
        jax.ShapeDtypeStruct((TOK, GQ * HD), kind),
        jax.ShapeDtypeStruct((TOK, GQ), jnp.float32),
    )


def prefill_part(queries, keys, values, bias):
    chunks = RP * SPAN // PREFILL_CHUNK
    whole = pl.BlockSpec(memory_space=pltpu.VMEM)
    there = pl.BlockSpec(memory_space=pl.ANY)
    return pl.pallas_call(
        prefill_kernel,
        in_specs=[whole, there, there, whole],
        out_specs=(whole, whole),
        out_shape=outputs_of(jnp.bfloat16),
        scratch_shapes=[
            pltpu.VMEM((R, SPAN, HD), jnp.bfloat16),
            pltpu.VMEM((R, SPAN, HD), jnp.bfloat16),
            pltpu.VMEM((chunks, GQ * CH, PREFILL_CHUNK), jnp.float32),
            pltpu.SemaphoreType.DMA((2, NPR * chunks)),
        ],
        compiler_params=pltpu.CompilerParams(vmem_limit_bytes=44 * 2**20),
    )(queries, keys, values, bias.reshape(NPR, chunks, PREFILL_CHUNK))


def decode_part(queries, keys, values, bias):
    def by_row(array):
        return array.reshape(STEPS, R, -1).transpose(1, 0, 2).reshape(TOK, -1)

    def by_step(array):
        return array.reshape(R, STEPS, -1).transpose(1, 0, 2).reshape(TOK, -1)

    rows = 8 * ROWS_AT_ONCE
    mixed, level = pl.pallas_call(
        decode_kernel,
        grid=(R // rows,),
        in_specs=[
            pl.BlockSpec((rows * STEPS, GQ * HD), lambda i: (i, 0)),
            pl.BlockSpec((rows, SPAN, HD), lambda i: (i, 0, 0)),
            pl.BlockSpec((rows, SPAN, HD), lambda i: (i, 0, 0)),
            pl.BlockSpec((rows // ROWS_AT_ONCE, ROWS_AT_ONCE * SPAN), lambda i: (i, 0)),
        ],
        out_specs=(
            pl.BlockSpec((rows * STEPS, GQ * HD), lambda i: (i, 0)),
            pl.BlockSpec((rows * STEPS, GQ), lambda i: (i, 0)),
        ),
        out_shape=outputs_of(jnp.bfloat16),
        compiler_params=pltpu.CompilerParams(vmem_limit_bytes=40 * 2**20),
    )(by_row(queries), keys, values, bias.reshape(R // ROWS_AT_ONCE, ROWS_AT_ONCE * SPAN))
    return by_step(mixed), by_step(level)


def recent_part(is_prefill, queries, keys, values):
    whole = pl.BlockSpec(memory_space=pltpu.VMEM)
    return pl.pallas_call(
        recent_kernel,
        in_specs=[pl.BlockSpec(memory_space=pltpu.SMEM), whole, whole, whole],
        out_specs=(whole, whole),
        out_shape=outputs_of(jnp.float32),
        compiler_params=pltpu.CompilerParams(vmem_limit_bytes=16 * 2**20),
    )(is_prefill.astype(jnp.int32).reshape(1), queries, keys, values)


def cut_kernel(core_ref, weight_ref, out_ref, held_ref, in_sems, out_sems):
    fetches = []
    stores = []
    for chip in range(CHIPS):
        columns = pl.ds(pl.multiple_of((2 * chip + 1 - core_ref[0]) * SHARD, SHARD), SHARD)
        fetches.append(
            pltpu.make_async_copy(weight_ref.at[:, columns], held_ref.at[chip], in_sems.at[chip])
        )
        stores.append(
            pltpu.make_async_copy(
                held_ref.at[chip],
                out_ref.at[:, chip * SHARD : (chip + 1) * SHARD],
                out_sems.at[chip],
            )
        )
    for fetch in fetches:
        fetch.start()
    for fetch, store in zip(fetches, stores):
        fetch.wait()
        store.start()
    for store in stores:
        store.wait()


def cut_columns(out_weight, core):
    return pl.pallas_call(
        cut_kernel,
        in_specs=[
            pl.BlockSpec(memory_space=pltpu.SMEM),
            pl.BlockSpec(memory_space=pl.ANY),
        ],
        out_specs=pl.BlockSpec(memory_space=pl.ANY),
        out_shape=jax.ShapeDtypeStruct((out_weight.shape[0], CHIPS * SHARD), jnp.bfloat16),
        scratch_shapes=[
            pltpu.VMEM((CHIPS, out_weight.shape[0], SHARD), jnp.bfloat16),
            pltpu.SemaphoreType.DMA((CHIPS,)),
            pltpu.SemaphoreType.DMA((CHIPS,)),
        ],
        compiler_params=pltpu.CompilerParams(vmem_limit_bytes=12 * 2**20),
    )(core.reshape(1), out_weight)


def on_device(
    layer_input, query_weight, kv_weight, out_weight, cache_keys, cache_values, lengths, placement
):
    group_count = lax.axis_size("group")
    splits = 2
    tp_rank = lax.axis_index("tp")
    group_rank = lax.axis_index("group")
    core = tp_rank % 2
    y = (tp_rank // 2) % 4
    x_hi = tp_rank // 8
    block_index = core
    last_block = block_index == splits - 1
    is_prefill = group_rank == 0
    tokens = layer_input[0]
    row_lengths = lengths[0]
    prefix = jnp.sum(row_lengths.reshape(NPR, RP), axis=1)
    prompt_positions = (prefix[:, None] + jnp.arange(CH, dtype=jnp.int32)[None, :]).reshape(TOK)
    decode_step_positions = (
        row_lengths[None, :] + jnp.arange(STEPS, dtype=jnp.int32)[:, None]
    ).reshape(TOK)
    positions = jnp.where(is_prefill, prompt_positions, decode_step_positions)

    cosine, sine = turns(positions)

    cut_out = cut_columns(out_weight, core)

    wide = ((TOK + HALF, SHARD), jnp.bfloat16)
    half = ((HALF, SHARD), jnp.bfloat16)
    shard = ((TOK, SHARD), jnp.bfloat16)
    weights = (query_weight, kv_weight)
    sums = (((TOK, query_weight.shape[1]), jnp.float32), ((TOK, kv_weight.shape[1]), jnp.float32))

    def rows_of(*owners):
        firsts = [tp_index(x_hi ^ flip, y + step, core) for flip, step in owners]
        return jnp.stack(firsts + [first ^ 1 for first in firsts]).astype(jnp.int32) * SHARD

    last_tokens, next_tokens = moved(tokens, 0, 1, 0), moved(tokens, 0, 3, 0)
    partner_tokens = moved(tokens, 1, 0, 0)
    token, *_ = lax.optimization_barrier((tp_rank.reshape(1), cut_out, cosine, sine))
    swapped_out = core_swap(cut_out)
    near = (tokens, last_tokens, next_tokens, partner_tokens)
    plus, minus, up, down = called(
        join_kernel, (wide, wide, half, half), token, partner_tokens, last_tokens, next_tokens
    )
    from_last, from_next = moved(plus, 0, 1, 0), moved(minus, 0, 3, 0)
    (far,) = called(
        far_join_kernel,
        (shard,),
        None,
        moved(down, 1, 3, 0),
        moved(up, 1, 1, 0),
        streamed=(from_last, from_next),
    )
    sides = (from_last, from_next, far)
    part = called(
        near_kernel,
        sums,
        rows_of((0, 0), (0, 3), (0, 1), (1, 0)),
        *weights,
        *near,
        *[core_swap(source) for source in near],
        flops=2 * TOK * 8 * SHARD * 3 * HD,
    )
    query_local, pair_local = called(
        last_kernel,
        tuple((shape, jnp.bfloat16) for shape, _ in sums),
        jnp.concatenate(
            [
                rows_of((1, 3), (1, 1), (0, 2), (1, 2)),
                (tp_rank < KVH).astype(jnp.int32)[None],
            ]
        ),
        *weights,
        *part,
        *sides,
        *[core_swap(source) for source in sides],
        cosine,
        sine,
        flops=2 * TOK * 8 * SHARD * 3 * HD,
    )
    query_other = core_swap(query_local)
    pair_held = lax.ppermute(
        pair_local, "tp", [(t, 2 * t if t < KVH else 2 * (t - KVH) + 1) for t in range(2 * KVH)]
    )
    my_queries = jnp.concatenate(
        [jnp.where(core == 0, query_local, query_other), jnp.where(core == 0, query_other, query_local)],
        axis=1,
    )
    present = (block_index * SPAN + jnp.arange(SPAN, dtype=jnp.int32))[None, :] < row_lengths[
        :, None
    ]
    bias = jnp.where(present, 0.0, NEG_FILL).astype(jnp.float32)
    cached = lax.cond(
        is_prefill, prefill_part, decode_part, my_queries, cache_keys[0], cache_values[0], bias
    )
    _, pair_held = lax.optimization_barrier((cached[1], pair_held))
    pair_other = core_swap(pair_held)
    my_keys = jnp.where(core == 0, pair_held, pair_other)
    my_values = jnp.where(core == 0, pair_other, pair_held)
    other_cached = (core_swap(cached[0]), core_swap(cached[1]))
    recent = recent_part(is_prefill, my_queries, my_keys, my_values)

    places = ((1, 1), (1, 3), (0, 2), (1, 2), (0, 1), (0, 3), (1, 0), (0, 0))
    place = jnp.stack(
        [core] + [(x_hi ^ flip) * 4 + (y + step) % 4 for flip, step in places]
    ).astype(jnp.int32)
    plus, minus, up, down, next_part, last_part, partner_part, here_part = called(
        merge_out_kernel,
        (wide, wide, half, half, shard, shard, shard, shard),
        place,
        *cached,
        *other_cached,
        *recent,
        streamed=(out_weight, swapped_out),
        scratch=(
            pltpu.VMEM((TOK, GQ * HD), jnp.bfloat16),
            pltpu.VMEM((CHIPS, GQ * HD, SHARD), jnp.bfloat16),
            pltpu.SemaphoreType.DMA((2, CHIPS)),
        ),
        flops=2 * TOK * CHIPS * SHARD * GQ * HD,
        grant=24,
    )
    from_last, from_next = moved(plus, 0, 1, 0), moved(minus, 0, 3, 0)
    up, down = moved(up, 1, 1, 0), moved(down, 1, 3, 0)

    block_count = TOK // BS
    slot_count = 2 * block_count // (group_count - 1)
    cells = placement[:, 0] * slot_count + placement[:, 1]
    sender = jnp.stack([is_prefill.astype(jnp.int32), core.astype(jnp.int32)])
    (blocks,) = called(
        blocks_kernel,
        (((group_count * slot_count, BS // splits, 2 * HD), jnp.bfloat16),),
        jnp.concatenate([sender, cells]),
        my_keys,
        my_values,
    )
    _, blocks = lax.optimization_barrier((here_part, blocks))
    blocks = blocks.reshape(2, 4, slot_count, BS // splits, 2 * HD)
    arrived = lax.ppermute(blocks, "group", [(0, 4)])
    plus, minus, partner = called(
        second_message_kernel,
        (shard, shard, shard),
        None,
        next_part,
        last_part,
        partner_part,
        from_last,
        from_next,
        up,
        down,
    )
    from_last, from_next = moved(plus, 0, 1, 0), moved(minus, 0, 3, 0)
    from_partner = moved(partner, 1, 0, 0)
    _, arrived = lax.optimization_barrier((partner, arrived))
    sent = lax.ppermute(arrived[:, 2:], "group", [(4, 6)])
    arrived = jnp.where(group_rank == 6, sent, arrived[:, :2])
    sent = lax.ppermute(arrived[:, 1:], "group", [(4, 5), (6, 7)])
    arrived = jnp.where(group_rank % 2 == 1, sent, arrived[:, :1])
    sent = lax.ppermute(arrived[0], "group", [(5, 1), (6, 2), (7, 3)])
    incoming = jnp.where(group_rank >= 4, arrived[1], sent)
    (projected,) = called(
        total_kernel, (shard,), None, here_part, from_last, from_next, from_partner
    )
    return (projected[None], incoming)


def solution(mesh):
    in_specs = (
        P("group", None, "tp"),
        P(None, "tp"),
        P(None, "tp"),
        P("tp", None),
        P("group", None, "tp", None),
        P("group", None, "tp", None),
        P("group", None),
        P(),
    )
    out_specs = (P("group", None, "tp"), P("group", None, "tp", None))
    return jax.shard_map(
        on_device, mesh=mesh, in_specs=in_specs, out_specs=out_specs, check_vma=False
    )
```

```python
import functools

import jax
import jax.numpy as jnp
from jax import lax
from jax.experimental import pallas as pl
from jax.experimental.pallas import tpu as pltpu
from jax.sharding import PartitionSpec as P

HD = 128
KVH = 8
STEPS = 4
NPR = 2
BS = 16
R = 64
GQ = 4
TOK = 256
CH = 128
RP = 32


NEG_FILL = -1e30


def tp_index(x_hi, y, core):
    return x_hi * 8 + (y % 4) * 2 + core


def moved(shard, x_flip, y_step, core_flip):
    pairs = []
    for x_hi in range(2):
        for y in range(4):
            for core in range(2):
                pairs.append(
                    (
                        tp_index(x_hi, y, core),
                        tp_index(x_hi ^ x_flip, y + y_step, core ^ core_flip),
                    )
                )
    return lax.ppermute(shard, "tp", pairs)


def core_swap(shard):
    return moved(shard, 0, 0, 1)


def turns(positions):
    midpoint = HD // 2
    frequency = jnp.exp(
        -jnp.log(500000.0) * jnp.arange(midpoint, dtype=jnp.float32) * 2.0 / HD
    )
    angles = positions.astype(jnp.float32)[:, None] * frequency[None, :]
    cosine = jnp.cos(angles)
    sine = jnp.sin(angles)
    return (
        jnp.concatenate([cosine, cosine], axis=1),
        jnp.concatenate([-sine, sine], axis=1),
    )


SPAN = 256
CHIPS = 8
SHARD = 512
HALF = TOK // 2
PREFILL_CHUNK = 4096
ROWS_AT_ONCE = 4
LOG2_E = 1.4426950408889634
NT = (((1,), (1,)), ((), ()))

CORE, IS_PREFILL, IS_KEY, NEAR_ROWS, FAR_ROWS, PLACE, CELLS, PICKS = 0, 1, 2, 3, 11, 19, 27, 43


def stacked_heads(*parts):
    return jnp.concatenate(
        [part[:, j * HD : (j + 1) * HD] for part in parts for j in range(part.shape[1] // HD)],
        axis=0,
    )


def length_bias(scalar_ref, length_ref, first, count):
    place = lax.broadcasted_iota(jnp.int32, (1, SPAN), 1) + scalar_ref[CORE] * SPAN
    return jnp.concatenate(
        [jnp.where(place < length_ref[first + row], 0.0, NEG_FILL) for row in range(count)],
        axis=1,
    )


def weights_of(scores, largest):
    return jnp.exp2((scores - largest) * (HD**-0.5 * LOG2_E)).astype(jnp.bfloat16)


def with_ones(values):
    return jnp.concatenate([values, jnp.ones_like(values)], axis=1)


def write_heads(mixed_ref, level_ref, rows, mixed, largest):
    count = mixed.shape[0] // GQ
    total = mixed[:, HD : HD + 1]
    normal = (mixed[:, :HD] / total).astype(jnp.bfloat16)
    level = largest * HD**-0.5 + jnp.log(total)
    lane = lax.broadcasted_iota(jnp.int32, (count, GQ), 1)
    levels = jnp.zeros((count, GQ), jnp.float32)
    for j in range(GQ):
        part = slice(j * count, (j + 1) * count)
        mixed_ref[rows, j * HD : (j + 1) * HD] = normal[part]
        levels = jnp.where(lane == j, level[part], levels)
    level_ref[rows, :] = levels


def prefill_kernel(
    scalar_ref,
    length_ref,
    own_ref,
    other_ref,
    key_ref,
    value_ref,
    mixed_ref,
    level_ref,
    keys,
    values,
    score_ref,
    sems,
):
    rows = PREFILL_CHUNK // SPAN
    chunks = RP // rows

    def fetches(prompt, step):
        part = pl.ds(prompt * RP + step * rows, rows)
        index = prompt * chunks + step
        return (
            pltpu.make_async_copy(key_ref.at[part], keys.at[part], sems.at[0, index]),
            pltpu.make_async_copy(value_ref.at[part], values.at[part], sems.at[1, index]),
        )

    for prompt in range(NPR):
        for kind in range(2):
            for step in range(chunks):
                fetches(prompt, step)[kind].start()

    def one_prompt(prompt, carry):
        tokens = pl.ds(pl.multiple_of(prompt * CH, CH), CH)
        queries = stacked_heads(own_ref[tokens, :], other_ref[tokens, :])

        def score_step(step, peak):
            fetches(prompt, step)[0].wait()
            part = keys[pl.ds(prompt * RP + step * rows, rows)].reshape(PREFILL_CHUNK, HD)
            scores = lax.dot_general(queries, part, NT, preferred_element_type=jnp.float32)
            scores = scores + length_bias(scalar_ref, length_ref, prompt * RP + step * rows, rows)
            score_ref[step] = scores
            for lanes in range(PREFILL_CHUNK // HD):
                peak = jnp.maximum(peak, scores[:, lanes * HD : (lanes + 1) * HD])
            return peak

        peak = lax.fori_loop(
            0, chunks, score_step, jnp.full((GQ * CH, HD), NEG_FILL, jnp.float32)
        )
        largest = jnp.max(peak, axis=1, keepdims=True)
        level = jnp.broadcast_to(largest, (GQ * CH, HD))

        def mix_step(step, mixed):
            fetches(prompt, step)[1].wait()
            weights = jnp.concatenate(
                [
                    weights_of(score_ref[step, :, lanes * HD : (lanes + 1) * HD], level)
                    for lanes in range(PREFILL_CHUNK // HD)
                ],
                axis=1,
            )
            part = values[pl.ds(prompt * RP + step * rows, rows)].reshape(PREFILL_CHUNK, HD)
            return mixed + jnp.dot(weights, with_ones(part), preferred_element_type=jnp.float32)

        mixed = lax.fori_loop(0, chunks, mix_step, jnp.zeros((GQ * CH, 2 * HD), jnp.float32))
        write_heads(mixed_ref, level_ref, tokens, mixed, largest)
        return carry

    lax.fori_loop(0, NPR, one_prompt, 0)


def decode_kernel(
    scalar_ref, length_ref, query_ref, key_ref, value_ref, mixed_ref, level_ref
):
    width = ROWS_AT_ONCE * SPAN
    tokens = ROWS_AT_ONCE * STEPS
    owner = lax.broadcasted_iota(jnp.int32, (GQ * tokens, width), 0) % tokens // STEPS
    holder = lax.broadcasted_iota(jnp.int32, (GQ * tokens, width), 1) // SPAN
    for part in range(query_ref.shape[0] // tokens):
        rows = slice(part * tokens, (part + 1) * tokens)
        cached = slice(part * ROWS_AT_ONCE, (part + 1) * ROWS_AT_ONCE)
        queries = stacked_heads(query_ref[rows, :])
        keys = key_ref[cached].reshape(width, HD)
        values = value_ref[cached].reshape(width, HD)
        scores = lax.dot_general(queries, keys, NT, preferred_element_type=jnp.float32)
        first = (pl.program_id(0) * (query_ref.shape[0] // tokens) + part) * ROWS_AT_ONCE
        bias = length_bias(scalar_ref, length_ref, first, ROWS_AT_ONCE)
        scores = jnp.where(owner == holder, scores + bias, NEG_FILL)
        largest = jnp.max(scores, axis=1, keepdims=True)
        mixed = jnp.dot(
            weights_of(scores, largest), with_ones(values), preferred_element_type=jnp.float32
        )
        write_heads(mixed_ref, level_ref, rows, mixed, largest)


def pair_of(scalar_ref, held_ref, other_ref):
    first = scalar_ref[CORE] == 0
    held, other = held_ref[...], other_ref[...]
    return jnp.where(first, held, other), jnp.where(first, other, held)


def recent_kernel(scalar_ref, own_ref, other_ref, held_ref, swapped_ref, mixed_ref, level_ref):
    is_prefill = scalar_ref[IS_PREFILL] != 0
    keys, values = pair_of(scalar_ref, held_ref, swapped_ref)
    row = lax.broadcasted_iota(jnp.int32, (TOK, TOK), 0)
    column = lax.broadcasted_iota(jnp.int32, (TOK, TOK), 1)
    together = jnp.where(is_prefill, row // CH - column // CH, row % R - column % R) == 0
    allowed = together & (column <= row)
    values = with_ones(values)
    queries = [ref[:, j * HD : (j + 1) * HD] for ref in (own_ref, other_ref) for j in range(2)]
    lane = lax.broadcasted_iota(jnp.int32, (TOK, GQ), 1)
    levels = jnp.zeros((TOK, GQ), jnp.float32)
    for j in range(GQ):
        head = slice(j * HD, (j + 1) * HD)
        scores = lax.dot_general(queries[j], keys, NT, preferred_element_type=jnp.float32)
        scores = jnp.where(allowed, scores, NEG_FILL)
        largest = jnp.max(scores, axis=1, keepdims=True)
        mixed = jnp.dot(weights_of(scores, largest), values, preferred_element_type=jnp.float32)
        total = mixed[:, HD : HD + 1]
        mixed_ref[:, head] = mixed[:, :HD] / total
        levels = jnp.where(lane == j, largest * HD**-0.5 + jnp.log(total), levels)
    level_ref[...] = levels


def merged(parts, levels):
    heads = []
    for j in range(GQ):
        places = (j, (j + GQ // 2) % GQ, j)
        columns = [level[:, place : place + 1] for level, place in zip(levels, places)]
        top = jnp.maximum(jnp.maximum(columns[0], columns[1]), columns[2])
        shares = [jnp.exp(column - top) for column in columns]
        total = shares[0] + shares[1] + shares[2]
        mixed = jnp.zeros((TOK, HD), jnp.float32)
        for part, share, place in zip(parts, shares, places):
            values = part[:, place * HD : (place + 1) * HD].astype(jnp.float32)
            mixed = mixed + values * (share / total)
        heads.append(mixed.astype(jnp.bfloat16))
    return jnp.concatenate(heads, axis=1)


def merge_out_kernel(
    scalar_ref,
    weight_ref,
    swapped_ref,
    own_ref,
    own_level,
    other_ref,
    other_level,
    recent_ref,
    recent_level,
    plus,
    minus,
    up,
    down,
    next_ref,
    last_ref,
    partner_ref,
    here_ref,
    held_ref,
    sems,
):
    core = scalar_ref[CORE]
    rows = weight_ref.shape[0]
    copies = []
    for index in range(CHIPS):
        chip = scalar_ref[PLACE + index]
        own = pl.ds(pl.multiple_of((2 * chip + core) * SHARD, SHARD), SHARD)
        other = pl.ds(pl.multiple_of(chip * SHARD, SHARD), SHARD)
        pair = (
            pltpu.make_async_copy(
                weight_ref.at[:, own], held_ref.at[index, :rows], sems.at[0, index]
            ),
            pltpu.make_async_copy(
                swapped_ref.at[:, other], held_ref.at[index, rows:], sems.at[1, index]
            ),
        )
        for copy in pair:
            copy.start()
        copies.append(pair)
    joined = merged(
        (own_ref, other_ref, recent_ref), (own_level[...], other_level[...], recent_level[...])
    )

    def product(index):
        for copy in copies[index]:
            copy.wait()
        total = jnp.dot(joined, held_ref[index], preferred_element_type=jnp.float32)
        return total.astype(jnp.bfloat16)

    plus[:TOK] = product(0)
    minus[:TOK] = product(1)
    far = product(2)
    plus[TOK:] = far[:HALF]
    minus[TOK:] = far[HALF:]
    far = product(3)
    up[...] = far[:HALF]
    down[...] = far[HALF:]
    for index, ref in ((4, next_ref), (5, last_ref), (6, partner_ref), (7, here_ref)):
        ref[...] = product(index)


def total_of(*parts):
    total = parts[0].astype(jnp.float32)
    for part in parts[1:]:
        total = total + part.astype(jnp.float32)
    return total.astype(jnp.bfloat16)


def second_message_kernel(
    next_ref, last_ref, partner_ref, from_last, from_next, up, down, plus, minus, partner
):
    plus[:HALF] = total_of(next_ref[:HALF], from_last[TOK:], up[...])
    plus[HALF:] = next_ref[HALF:]
    minus[:HALF] = last_ref[:HALF]
    minus[HALF:] = total_of(last_ref[HALF:], from_next[TOK:], down[...])
    partner[...] = total_of(partner_ref[...], from_last[:TOK], from_next[:TOK])


def total_kernel(here_ref, from_last, from_next, from_partner, out_ref):
    out_ref[...] = total_of(here_ref[...], from_last[...], from_next[...], from_partner[...])


def join_kernel(scalar_ref, partner_ref, last_ref, next_ref, plus, minus, near):
    plus[:TOK] = partner_ref[...]
    plus[TOK:] = last_ref[:HALF]
    minus[:TOK] = partner_ref[...]
    minus[TOK:] = next_ref[HALF:]
    near[:TOK] = last_ref[...]
    near[TOK : 2 * TOK] = next_ref[...]
    near[2 * TOK :] = partner_ref[...]


def projected_parts(scalar_ref, first, shards, query_weight, pair_weight):
    joined = jnp.concatenate(shards, axis=1)
    rows = [
        pl.ds(pl.multiple_of(scalar_ref[first + index], SHARD), SHARD)
        for index in range(len(shards))
    ]
    return [
        jnp.dot(
            joined,
            jnp.concatenate([weight[part, :] for part in rows], axis=0),
            preferred_element_type=jnp.float32,
        )
        for weight in (query_weight, pair_weight)
    ]


def near_kernel(scalar_ref, query_weight, pair_weight, *refs):
    *sources, query, pair, mark = refs
    mark[...] = jnp.zeros_like(mark)
    shards = []
    for own_ref, near_ref in (sources[:2], sources[2:]):
        shards.append(own_ref[...])
        shards.extend(near_ref[index * TOK : (index + 1) * TOK] for index in range(3))
    query[...], pair[...] = projected_parts(
        scalar_ref, NEAR_ROWS, shards, query_weight, pair_weight
    )


def far_shards(last_ref, next_ref, upper_ref, lower_ref):
    middle = jnp.concatenate([last_ref[TOK:], next_ref[TOK:]], axis=0)
    far = jnp.concatenate([upper_ref[...], lower_ref[...]], axis=0)
    return [last_ref[:TOK], next_ref[:TOK], middle, far]


def last_kernel(scalar_ref, query_weight, pair_weight, query_in, pair_in, *refs):
    *sides, cosine_ref, sine_ref, query_out, pair_out = refs
    shards = far_shards(*sides[:4]) + far_shards(*sides[4:])
    sums = projected_parts(scalar_ref, FAR_ROWS, shards, query_weight, pair_weight)
    query = query_in[...] + sums[0]
    pair = pair_in[...] + sums[1]
    cosine = cosine_ref[...]
    sine = sine_ref[...]

    def rotated(values):
        return values * cosine + pltpu.roll(values, HD // 2, 1) * sine

    for head in range(query.shape[1] // HD):
        part = slice(head * HD, (head + 1) * HD)
        query_out[:, part] = rotated(query[:, part]).astype(jnp.bfloat16)
    is_key = scalar_ref[IS_KEY] != 0
    pair_out[...] = jnp.where(is_key, rotated(pair), pair).astype(jnp.bfloat16)


def blocks_kernel(scalar_ref, held_ref, swapped_ref, out_ref, pair_ref):
    sliver = out_ref.shape[1]
    out_ref[...] = jnp.zeros_like(out_ref)

    @pl.when(scalar_ref[IS_PREFILL] != 0)
    def _():
        keys, values = pair_of(scalar_ref, held_ref, swapped_ref)
        pair_ref[:, :HD] = keys.astype(jnp.float32)
        pair_ref[:, HD:] = values.astype(jnp.float32)
        for block in range(TOK // BS):
            start = pl.multiple_of(scalar_ref[CORE] * sliver, sliver) + block * BS
            out_ref[scalar_ref[CELLS + block]] = pair_ref[pl.ds(start, sliver), :].astype(
                jnp.bfloat16
            )


def pick_kernel(pick, scalar_ref, sent_ref, kept_ref, out_ref):
    chosen = scalar_ref[PICKS + pick] != 0
    out_ref[...] = jnp.where(chosen, sent_ref[...], kept_ref[...])


def called(kernel, shapes, scalars, *arrays, streamed=(), scratch=(), flops=0, grant=12):
    whole = pl.BlockSpec(memory_space=pltpu.VMEM)
    specs = [pl.BlockSpec(memory_space=pl.ANY)] * len(streamed) + [whole] * len(arrays)
    arrays = tuple(streamed) + arrays
    if scalars is not None:
        specs = [pl.BlockSpec(memory_space=pltpu.SMEM)] + specs
        arrays = (scalars,) + arrays
    return pl.pallas_call(
        kernel,
        in_specs=specs,
        out_specs=tuple(whole for _ in shapes),
        out_shape=tuple(jax.ShapeDtypeStruct(shape, kind) for shape, kind in shapes),
        scratch_shapes=scratch,
        compiler_params=pltpu.CompilerParams(vmem_limit_bytes=grant * 2**20),
        cost_estimate=pl.CostEstimate(flops=flops, transcendentals=0, bytes_accessed=2**21),
    )(*arrays)


def outputs_of(kind):
    return (
        jax.ShapeDtypeStruct((TOK, GQ * HD), kind),
        jax.ShapeDtypeStruct((TOK, GQ), jnp.float32),
    )


def prefill_part(scalars, lengths, own, other, keys, values):
    chunks = RP * SPAN // PREFILL_CHUNK
    whole = pl.BlockSpec(memory_space=pltpu.VMEM)
    there = pl.BlockSpec(memory_space=pl.ANY)
    small = pl.BlockSpec(memory_space=pltpu.SMEM)
    return pl.pallas_call(
        prefill_kernel,
        in_specs=[small, small, whole, whole, there, there],
        out_specs=(whole, whole),
        out_shape=outputs_of(jnp.bfloat16),
        scratch_shapes=[
            pltpu.VMEM((R, SPAN, HD), jnp.bfloat16),
            pltpu.VMEM((R, SPAN, HD), jnp.bfloat16),
            pltpu.VMEM((chunks, GQ * CH, PREFILL_CHUNK), jnp.float32),
            pltpu.SemaphoreType.DMA((2, NPR * chunks)),
        ],
        compiler_params=pltpu.CompilerParams(vmem_limit_bytes=44 * 2**20),
    )(scalars, lengths, own, other, keys, values)


def decode_part(scalars, lengths, own, other, keys, values):
    def by_row(array):
        return array.reshape(STEPS, R, -1).transpose(1, 0, 2).reshape(TOK, -1)

    def by_step(array):
        return array.reshape(R, STEPS, -1).transpose(1, 0, 2).reshape(TOK, -1)

    rows = 8 * ROWS_AT_ONCE
    mixed, level = pl.pallas_call(
        decode_kernel,
        grid=(R // rows,),
        in_specs=[
            pl.BlockSpec(memory_space=pltpu.SMEM),
            pl.BlockSpec(memory_space=pltpu.SMEM),
            pl.BlockSpec((rows * STEPS, GQ * HD), lambda i: (i, 0)),
            pl.BlockSpec((rows, SPAN, HD), lambda i: (i, 0, 0)),
            pl.BlockSpec((rows, SPAN, HD), lambda i: (i, 0, 0)),
        ],
        out_specs=(
            pl.BlockSpec((rows * STEPS, GQ * HD), lambda i: (i, 0)),
            pl.BlockSpec((rows * STEPS, GQ), lambda i: (i, 0)),
        ),
        out_shape=outputs_of(jnp.bfloat16),
        compiler_params=pltpu.CompilerParams(vmem_limit_bytes=40 * 2**20),
    )(scalars, lengths, by_row(jnp.concatenate([own, other], axis=1)), keys, values)
    return by_step(mixed), by_step(level)


def cut_kernel(scalar_ref, weight_ref, out_ref, held_ref, in_sems, out_sems):
    fetches = []
    stores = []
    for chip in range(CHIPS):
        columns = pl.ds(pl.multiple_of((2 * chip + 1 - scalar_ref[CORE]) * SHARD, SHARD), SHARD)
        fetches.append(
            pltpu.make_async_copy(weight_ref.at[:, columns], held_ref.at[chip], in_sems.at[chip])
        )
        stores.append(
            pltpu.make_async_copy(
                held_ref.at[chip],
                out_ref.at[:, chip * SHARD : (chip + 1) * SHARD],
                out_sems.at[chip],
            )
        )
    for fetch in fetches:
        fetch.start()
    for fetch, store in zip(fetches, stores):
        fetch.wait()
        store.start()
    for store in stores:
        store.wait()


def cut_columns(scalars, out_weight):
    return pl.pallas_call(
        cut_kernel,
        in_specs=[
            pl.BlockSpec(memory_space=pltpu.SMEM),
            pl.BlockSpec(memory_space=pl.ANY),
        ],
        out_specs=pl.BlockSpec(memory_space=pl.ANY),
        out_shape=jax.ShapeDtypeStruct((out_weight.shape[0], CHIPS * SHARD), jnp.bfloat16),
        scratch_shapes=[
            pltpu.VMEM((CHIPS, out_weight.shape[0], SHARD), jnp.bfloat16),
            pltpu.SemaphoreType.DMA((CHIPS,)),
            pltpu.SemaphoreType.DMA((CHIPS,)),
        ],
        compiler_params=pltpu.CompilerParams(vmem_limit_bytes=12 * 2**20),
    )(scalars, out_weight)


def on_device(
    layer_input, query_weight, kv_weight, out_weight, cache_keys, cache_values, lengths, placement
):
    group_count = lax.axis_size("group")
    tp_rank = lax.axis_index("tp")
    group_rank = lax.axis_index("group")
    core = tp_rank % 2
    y = (tp_rank // 2) % 4
    x_hi = tp_rank // 8
    is_prefill = group_rank == 0
    tokens = layer_input[0]
    row_lengths = lengths[0]
    slot_count = 2 * (TOK // BS) // (group_count - 1)

    def rows_of(*owners):
        firsts = [tp_index(x_hi ^ flip, y + step, core) for flip, step in owners]
        return [first * SHARD for first in firsts] + [(first ^ 1) * SHARD for first in firsts]

    places = ((1, 1), (1, 3), (0, 2), (1, 2), (0, 1), (0, 3), (1, 0), (0, 0))
    single = (
        [core, is_prefill, tp_rank < KVH]
        + rows_of((0, 0), (0, 3), (0, 1), (1, 0))
        + rows_of((1, 3), (1, 1), (0, 2), (1, 2))
        + [(x_hi ^ flip) * 4 + (y + step) % 4 for flip, step in places]
    )
    picks = [group_rank == 6, group_rank % 2 == 1, group_rank < 4]
    scalars = jnp.concatenate(
        [
            jnp.stack([jnp.asarray(one, jnp.int32) for one in single]),
            placement[:, 0] * slot_count + placement[:, 1],
            jnp.stack([jnp.asarray(one, jnp.int32) for one in picks]),
        ]
    )
    prefix = jnp.sum(row_lengths.reshape(NPR, RP), axis=1)
    prompt_positions = (prefix[:, None] + jnp.arange(CH, dtype=jnp.int32)[None, :]).reshape(TOK)
    decode_step_positions = (
        row_lengths[None, :] + jnp.arange(STEPS, dtype=jnp.int32)[:, None]
    ).reshape(TOK)
    positions = jnp.where(is_prefill, prompt_positions, decode_step_positions)
    cosine, sine = turns(positions)

    cut_out = cut_columns(scalars, out_weight)

    wide = ((TOK + HALF, SHARD), jnp.bfloat16)
    half = ((HALF, SHARD), jnp.bfloat16)
    shard = ((TOK, SHARD), jnp.bfloat16)
    triple = ((3 * TOK, SHARD), jnp.bfloat16)
    weights = (query_weight, kv_weight)
    sums = (((TOK, query_weight.shape[1]), jnp.float32), ((TOK, kv_weight.shape[1]), jnp.float32))
    partner_tokens = moved(tokens, 1, 0, 0)
    last_tokens, next_tokens = moved(tokens, 0, 1, 0), moved(tokens, 0, 3, 0)
    other_tokens = core_swap(tokens)
    scalars, *_ = lax.optimization_barrier((scalars, cut_out, cosine, sine))
    plus, minus, near = called(
        join_kernel,
        (wide, wide, triple),
        scalars,
        partner_tokens,
        last_tokens,
        next_tokens,
    )
    from_last, from_next = moved(plus, 0, 1, 0), moved(minus, 0, 3, 0)
    far_upper, far_lower = moved(from_last[:HALF], 0, 1, 0), moved(from_next[HALF:TOK], 0, 3, 0)
    *part, mark = called(
        near_kernel,
        sums + (((8, HD), jnp.float32),),
        scalars,
        *weights,
        tokens,
        near,
        other_tokens,
        core_swap(near),
        flops=2 * TOK * 8 * SHARD * 3 * HD,
    )
    sides = (from_last, from_next, far_upper, far_lower)
    _, *ready = lax.optimization_barrier((mark, far_upper, far_lower))
    query_local, pair_local = called(
        last_kernel,
        tuple((shape, jnp.bfloat16) for shape, _ in sums),
        scalars,
        *weights,
        *part,
        *sides,
        *[core_swap(source) for source in (from_last, from_next, *ready)],
        cosine,
        sine,
        flops=2 * TOK * 8 * SHARD * 3 * HD,
    )
    query_other = core_swap(query_local)
    pair_held = lax.ppermute(
        pair_local, "tp", [(t, 2 * t if t < KVH else 2 * (t - KVH) + 1) for t in range(2 * KVH)]
    )
    _, cut_out = lax.optimization_barrier((query_local, cut_out))
    _, row_lengths = lax.optimization_barrier((pair_held, row_lengths))
    swapped_out = core_swap(cut_out)
    cached = lax.cond(
        is_prefill,
        prefill_part,
        decode_part,
        scalars,
        row_lengths,
        query_local,
        query_other,
        cache_keys[0],
        cache_values[0],
    )
    pair_other = core_swap(pair_held)
    other_cached = (core_swap(cached[0]), core_swap(cached[1]))
    recent = called(
        recent_kernel,
        (((TOK, GQ * HD), jnp.float32), ((TOK, GQ), jnp.float32)),
        scalars,
        query_local,
        query_other,
        pair_held,
        pair_other,
        flops=4 * GQ * TOK * TOK * HD,
    )

    plus, minus, up, down, next_part, last_part, partner_part, here_part = called(
        merge_out_kernel,
        (wide, wide, half, half, shard, shard, shard, shard),
        scalars,
        *cached,
        *other_cached,
        *recent,
        streamed=(out_weight, swapped_out),
        scratch=(
            pltpu.VMEM((CHIPS, GQ * HD, SHARD), jnp.bfloat16),
            pltpu.SemaphoreType.DMA((2, CHIPS)),
        ),
        flops=2 * TOK * CHIPS * SHARD * GQ * HD,
        grant=16,
    )
    from_last, from_next = moved(plus, 0, 1, 0), moved(minus, 0, 3, 0)
    up, down = moved(up, 1, 1, 0), moved(down, 1, 3, 0)

    (blocks,) = called(
        blocks_kernel,
        (((group_count * slot_count, BS // 2, 2 * HD), jnp.bfloat16),),
        scalars,
        pair_held,
        pair_other,
        scratch=(pltpu.VMEM((TOK, 2 * HD), jnp.float32),),
    )
    _, blocks = lax.optimization_barrier((here_part, blocks))
    blocks = blocks.reshape(2, 4, slot_count, BS // 2, 2 * HD)
    arrived = lax.ppermute(blocks, "group", [(0, 4)])

    plus, minus, partner = called(
        second_message_kernel,
        (shard, shard, shard),
        None,
        next_part,
        last_part,
        partner_part,
        from_last,
        from_next,
        up,
        down,
    )
    from_last, from_next = moved(plus, 0, 1, 0), moved(minus, 0, 3, 0)
    from_partner = moved(partner, 1, 0, 0)

    def picked(pick, sent, kept):
        kernel = functools.partial(pick_kernel, pick)
        return called(kernel, ((sent.shape, sent.dtype),), scalars, sent, kept)[0]

    _, arrived = lax.optimization_barrier((partner, arrived))
    sent = lax.ppermute(arrived[:, 2:], "group", [(4, 6)])
    arrived = picked(0, sent, arrived[:, :2])
    sent = lax.ppermute(arrived[:, 1:], "group", [(4, 5), (6, 7)])
    arrived = picked(1, sent, arrived[:, :1])
    sent = lax.ppermute(arrived[0], "group", [(5, 1), (6, 2), (7, 3)])
    incoming = picked(2, sent, arrived[1])
    (projected,) = called(
        total_kernel, (shard,), None, here_part, from_last, from_next, from_partner
    )
    return (projected[None], incoming)


def solution(mesh):
    in_specs = (
        P("group", None, "tp"),
        P(None, "tp"),
        P(None, "tp"),
        P("tp", None),
        P("group", None, "tp", None),
        P("group", None, "tp", None),
        P("group", None),
        P(),
    )
    out_specs = (P("group", None, "tp"), P("group", None, "tp", None))
    return jax.shard_map(
        on_device, mesh=mesh, in_specs=in_specs, out_specs=out_specs, check_vma=False
    )
```

```python
import jax
import jax.numpy as jnp
from jax import lax
from jax.experimental import pallas as pl
from jax.experimental.pallas import tpu as pltpu
from jax.sharding import PartitionSpec as P

HD = 128
KVH = 8
STEPS = 4
NPR = 2
BS = 16
R = 64
GQ = 4
TOK = 256
CH = 128
RP = 32


NEG_FILL = -1e30


def tp_index(x_hi, y, core):
    return x_hi * 8 + (y % 4) * 2 + core


def moved(shard, x_flip, y_step, core_flip):
    pairs = []
    for x_hi in range(2):
        for y in range(4):
            for core in range(2):
                pairs.append(
                    (
                        tp_index(x_hi, y, core),
                        tp_index(x_hi ^ x_flip, y + y_step, core ^ core_flip),
                    )
                )
    return lax.ppermute(shard, "tp", pairs)


def core_swap(shard):
    return moved(shard, 0, 0, 1)


def turns(positions):
    midpoint = HD // 2
    frequency = jnp.exp(
        -jnp.log(500000.0) * jnp.arange(midpoint, dtype=jnp.float32) * 2.0 / HD
    )
    angles = positions.astype(jnp.float32)[:, None] * frequency[None, :]
    cosine = jnp.cos(angles)
    sine = jnp.sin(angles)
    return (
        jnp.concatenate([cosine, cosine], axis=1),
        jnp.concatenate([-sine, sine], axis=1),
    )


SPAN = 256
CHIPS = 8
SHARD = 512
HALF = TOK // 2
PREFILL_CHUNK = 4096
ROWS_AT_ONCE = 4
LOG2_E = 1.4426950408889634
NT = (((1,), (1,)), ((), ()))
LONG = 6 * 10**9

CORE, IS_PREFILL, IS_KEY, NEAR_ROWS, FAR_ROWS, PLACE, CELLS = 0, 1, 2, 3, 11, 19, 27


def stacked_heads(*parts):
    return jnp.concatenate(
        [part[:, j * HD : (j + 1) * HD] for part in parts for j in range(part.shape[1] // HD)],
        axis=0,
    )


def length_bias(scalar_ref, length_ref, first, count):
    place = lax.broadcasted_iota(jnp.int32, (1, SPAN), 1) + scalar_ref[CORE] * SPAN
    return jnp.concatenate(
        [jnp.where(place < length_ref[first + row], 0.0, NEG_FILL) for row in range(count)],
        axis=1,
    )


def weights_of(scores, largest):
    return jnp.exp2((scores - largest) * (HD**-0.5 * LOG2_E)).astype(jnp.bfloat16)


def with_ones(values):
    return jnp.concatenate([values, jnp.ones_like(values)], axis=1)


def write_heads(mixed_ref, level_ref, rows, mixed, largest):
    count = mixed.shape[0] // GQ
    total = mixed[:, HD : HD + 1]
    normal = (mixed[:, :HD] / total).astype(jnp.bfloat16)
    level = largest * HD**-0.5 + jnp.log(total)
    lane = lax.broadcasted_iota(jnp.int32, (count, GQ), 1)
    levels = jnp.zeros((count, GQ), jnp.float32)
    for j in range(GQ):
        part = slice(j * count, (j + 1) * count)
        mixed_ref[rows, j * HD : (j + 1) * HD] = normal[part]
        levels = jnp.where(lane == j, level[part], levels)
    level_ref[rows, :] = levels


def prefill_kernel(
    scalar_ref,
    length_ref,
    own_ref,
    other_ref,
    key_ref,
    value_ref,
    mixed_ref,
    level_ref,
    keys,
    values,
    score_ref,
    sems,
):
    rows = PREFILL_CHUNK // SPAN
    chunks = RP // rows

    def fetches(prompt, step):
        part = pl.ds(prompt * RP + step * rows, rows)
        index = prompt * chunks + step
        return (
            pltpu.make_async_copy(key_ref.at[part], keys.at[part], sems.at[0, index]),
            pltpu.make_async_copy(value_ref.at[part], values.at[part], sems.at[1, index]),
        )

    for prompt in range(NPR):
        for kind in range(2):
            for step in range(chunks):
                fetches(prompt, step)[kind].start()

    def one_prompt(prompt, carry):
        tokens = pl.ds(pl.multiple_of(prompt * CH, CH), CH)
        queries = stacked_heads(own_ref[tokens, :], other_ref[tokens, :])

        def score_step(step, peak):
            fetches(prompt, step)[0].wait()
            part = keys[pl.ds(prompt * RP + step * rows, rows)].reshape(PREFILL_CHUNK, HD)
            scores = lax.dot_general(queries, part, NT, preferred_element_type=jnp.float32)
            scores = scores + length_bias(scalar_ref, length_ref, prompt * RP + step * rows, rows)
            score_ref[step] = scores
            for lanes in range(PREFILL_CHUNK // HD):
                peak = jnp.maximum(peak, scores[:, lanes * HD : (lanes + 1) * HD])
            return peak

        peak = lax.fori_loop(
            0, chunks, score_step, jnp.full((GQ * CH, HD), NEG_FILL, jnp.float32)
        )
        largest = jnp.max(peak, axis=1, keepdims=True)
        level = jnp.broadcast_to(largest, (GQ * CH, HD))

        def mix_step(step, mixed):
            fetches(prompt, step)[1].wait()
            weights = jnp.concatenate(
                [
                    weights_of(score_ref[step, :, lanes * HD : (lanes + 1) * HD], level)
                    for lanes in range(PREFILL_CHUNK // HD)
                ],
                axis=1,
            )
            part = values[pl.ds(prompt * RP + step * rows, rows)].reshape(PREFILL_CHUNK, HD)
            return mixed + jnp.dot(weights, with_ones(part), preferred_element_type=jnp.float32)

        mixed = lax.fori_loop(0, chunks, mix_step, jnp.zeros((GQ * CH, 2 * HD), jnp.float32))
        write_heads(mixed_ref, level_ref, tokens, mixed, largest)
        return carry

    lax.fori_loop(0, NPR, one_prompt, 0)


def decode_kernel(
    scalar_ref, length_ref, query_ref, key_ref, value_ref, mixed_ref, level_ref
):
    width = ROWS_AT_ONCE * SPAN
    tokens = ROWS_AT_ONCE * STEPS
    owner = lax.broadcasted_iota(jnp.int32, (GQ * tokens, width), 0) % tokens // STEPS
    holder = lax.broadcasted_iota(jnp.int32, (GQ * tokens, width), 1) // SPAN
    for part in range(query_ref.shape[0] // tokens):
        rows = slice(part * tokens, (part + 1) * tokens)
        cached = slice(part * ROWS_AT_ONCE, (part + 1) * ROWS_AT_ONCE)
        queries = stacked_heads(query_ref[rows, :])
        keys = key_ref[cached].reshape(width, HD)
        values = value_ref[cached].reshape(width, HD)
        scores = lax.dot_general(queries, keys, NT, preferred_element_type=jnp.float32)
        first = (pl.program_id(0) * (query_ref.shape[0] // tokens) + part) * ROWS_AT_ONCE
        bias = length_bias(scalar_ref, length_ref, first, ROWS_AT_ONCE)
        scores = jnp.where(owner == holder, scores + bias, NEG_FILL)
        largest = jnp.max(scores, axis=1, keepdims=True)
        mixed = jnp.dot(
            weights_of(scores, largest), with_ones(values), preferred_element_type=jnp.float32
        )
        write_heads(mixed_ref, level_ref, rows, mixed, largest)


def sort_pair(scalar_ref, held_ref, swapped_ref, keys, values):
    @pl.when(scalar_ref[CORE] == 0)
    def _():
        keys[...] = held_ref[...].astype(keys.dtype)
        values[...] = swapped_ref[...].astype(values.dtype)

    @pl.when(scalar_ref[CORE] != 0)
    def _():
        keys[...] = swapped_ref[...].astype(keys.dtype)
        values[...] = held_ref[...].astype(values.dtype)


def recent_kernel(scalar_ref, own_ref, other_ref, held_ref, swapped_ref, mixed_ref, level_ref):
    row = lax.broadcasted_iota(jnp.int32, (TOK, TOK), 0)
    column = lax.broadcasted_iota(jnp.int32, (TOK, TOK), 1)
    is_prefill = scalar_ref[IS_PREFILL] != 0
    together = jnp.where(is_prefill, row // CH - column // CH, row % R - column % R) == 0
    allowed = together & (column <= row)
    lane = lax.broadcasted_iota(jnp.int32, (TOK, GQ), 1)

    def attend(key_ref, value_ref):
        values = with_ones(value_ref[...])
        levels = jnp.zeros((TOK, GQ), jnp.float32)
        for j in range(GQ):
            source = own_ref if j < GQ // 2 else other_ref
            part = slice(j % (GQ // 2) * HD, (j % (GQ // 2) + 1) * HD)
            scores = lax.dot_general(
                source[:, part], key_ref[...], NT, preferred_element_type=jnp.float32
            )
            scores = jnp.where(allowed, scores, NEG_FILL)
            largest = jnp.max(scores, axis=1, keepdims=True)
            mixed = jnp.dot(
                weights_of(scores, largest), values, preferred_element_type=jnp.float32
            )
            total = mixed[:, HD : HD + 1]
            mixed_ref[:, j * HD : (j + 1) * HD] = (mixed[:, :HD] / total).astype(mixed_ref.dtype)
            levels = jnp.where(lane == j, largest * HD**-0.5 + jnp.log(total), levels)
        level_ref[...] = levels

    @pl.when(scalar_ref[CORE] == 0)
    def _():
        attend(held_ref, swapped_ref)

    @pl.when(scalar_ref[CORE] != 0)
    def _():
        attend(swapped_ref, held_ref)


def merged(parts, levels):
    half = GQ // 2
    turned = jnp.concatenate([levels[1][:, half:], levels[1][:, :half]], axis=1)
    levels = [levels[0], turned, levels[2]]
    top = jnp.maximum(jnp.maximum(levels[0], levels[1]), levels[2])
    shares = [jnp.exp(level - top) for level in levels]
    total = shares[0] + shares[1] + shares[2]
    shares = [share / total for share in shares]
    heads = []
    for j in range(GQ):
        mixed = jnp.zeros((TOK, HD), jnp.float32)
        for part, share, place in zip(parts, shares, (j, (j + half) % GQ, j)):
            values = part[:, place * HD : (place + 1) * HD].astype(jnp.float32)
            mixed = mixed + values * share[:, j : j + 1]
        heads.append(mixed.astype(jnp.bfloat16))
    return jnp.concatenate(heads, axis=1)


def swapped_copies(scalar_ref, first, swapped_ref, held_ref, sems):
    copies = []
    for index in range(4):
        columns = pl.ds(pl.multiple_of(scalar_ref[PLACE + first + index] * SHARD, SHARD), SHARD)
        copies.append(
            pltpu.make_async_copy(
                swapped_ref.at[:, columns], held_ref.at[index], sems.at[index]
            )
        )
        copies[-1].start()
    return copies


def product(scalar_ref, chip, joined, copy, weight_ref, held_ref, index):
    column = 2 * scalar_ref[PLACE + chip] + scalar_ref[CORE]
    own = weight_ref[:, pl.ds(pl.multiple_of(column * SHARD, SHARD), SHARD)]
    copy.wait()
    weights = jnp.concatenate([own, held_ref[index]], axis=0)
    return jnp.dot(joined, weights, preferred_element_type=jnp.float32).astype(jnp.bfloat16)


def merge_out_kernel(
    scalar_ref,
    swapped_ref,
    weight_ref,
    own_ref,
    own_level,
    other_ref,
    other_level,
    recent_ref,
    recent_level,
    plus,
    minus,
    up,
    down,
    attention,
    held_ref,
    sems,
):
    copies = swapped_copies(scalar_ref, 0, swapped_ref, held_ref, sems)
    joined = merged(
        (own_ref, other_ref, recent_ref), (own_level[...], other_level[...], recent_level[...])
    )
    attention[...] = joined
    parts = [
        product(scalar_ref, index, joined, copies[index], weight_ref, held_ref, index)
        for index in range(4)
    ]
    plus[:TOK] = parts[0]
    minus[:TOK] = parts[1]
    plus[TOK:] = parts[2][:HALF]
    minus[TOK:] = parts[2][HALF:]
    up[...] = parts[3][:HALF]
    down[...] = parts[3][HALF:]


def out_kernel(scalar_ref, swapped_ref, weight_ref, attention, *refs):
    *out_refs, held_ref, sems = refs
    copies = swapped_copies(scalar_ref, 4, swapped_ref, held_ref, sems)
    joined = attention[...]
    for index, ref in enumerate(out_refs):
        ref[...] = product(
            scalar_ref, 4 + index, joined, copies[index], weight_ref, held_ref, index
        )


def total_of(*parts):
    total = parts[0].astype(jnp.float32)
    for part in parts[1:]:
        total = total + part.astype(jnp.float32)
    return total.astype(jnp.bfloat16)


def second_message_kernel(
    arrived_ref,
    next_ref,
    last_ref,
    partner_ref,
    from_last,
    from_next,
    up,
    down,
    plus,
    minus,
    partner,
):
    plus[:HALF] = total_of(next_ref[:HALF], from_last[TOK:], up[...])
    plus[HALF:] = next_ref[HALF:]
    minus[:HALF] = last_ref[:HALF]
    minus[HALF:] = total_of(last_ref[HALF:], from_next[TOK:], down[...])
    partner[...] = total_of(partner_ref[...], from_last[:TOK], from_next[:TOK])


def total_kernel(here_ref, from_last, from_next, from_partner, out_ref):
    out_ref[...] = total_of(here_ref[...], from_last[...], from_next[...], from_partner[...])


def join_kernel(
    scalar_ref, own_ref, partner_ref, last_ref, next_ref, plus, minus, up, down, near, sem
):
    own = pltpu.make_async_copy(own_ref, near.at[:TOK], sem)
    own.start()
    plus[:TOK] = partner_ref[...]
    plus[TOK:] = last_ref[:HALF]
    minus[:TOK] = partner_ref[...]
    minus[TOK:] = next_ref[HALF:]
    up[...] = last_ref[HALF:]
    down[...] = next_ref[:HALF]
    for index, ref in enumerate((last_ref, next_ref, partner_ref)):
        near[(index + 1) * TOK : (index + 2) * TOK] = ref[...]
    own.wait()


def sides_kernel(mark_ref, last_ref, next_ref, upper_ref, lower_ref, sides):
    sides[:TOK] = last_ref[:TOK]
    sides[TOK : 2 * TOK] = next_ref[:TOK]
    sides[2 * TOK : 2 * TOK + HALF] = last_ref[TOK:]
    sides[2 * TOK + HALF : 3 * TOK] = next_ref[TOK:]
    sides[3 * TOK : 3 * TOK + HALF] = upper_ref[...]
    sides[3 * TOK + HALF :] = lower_ref[...]


def projected_parts(scalar_ref, first, shards, query_weight, pair_weight):
    joined = jnp.concatenate(shards, axis=1)
    rows = [
        pl.ds(pl.multiple_of(scalar_ref[first + index], SHARD), SHARD)
        for index in range(len(shards))
    ]
    return [
        jnp.dot(
            joined,
            jnp.concatenate([weight[part, :] for part in rows], axis=0),
            preferred_element_type=jnp.float32,
        )
        for weight in (query_weight, pair_weight)
    ]


def four_shards(ref):
    return [ref[index * TOK : (index + 1) * TOK] for index in range(4)]


def near_kernel(scalar_ref, query_weight, pair_weight, near_ref, other_ref, query, pair, mark):
    mark[...] = jnp.zeros_like(mark)
    query[...], pair[...] = projected_parts(
        scalar_ref,
        NEAR_ROWS,
        four_shards(near_ref) + four_shards(other_ref),
        query_weight,
        pair_weight,
    )


def far_kernel(scalar_ref, query_weight, pair_weight, query_in, pair_in, far_ref, query, pair):
    sums = projected_parts(scalar_ref, FAR_ROWS, four_shards(far_ref), query_weight, pair_weight)
    query[...] = query_in[...] + sums[0]
    pair[...] = pair_in[...] + sums[1]


def last_kernel(
    scalar_ref,
    query_weight,
    pair_weight,
    query_in,
    pair_in,
    far_ref,
    cosine_ref,
    sine_ref,
    query_out,
    pair_out,
):
    sums = projected_parts(
        scalar_ref, FAR_ROWS + 4, four_shards(far_ref), query_weight, pair_weight
    )
    query = query_in[...] + sums[0]
    pair = pair_in[...] + sums[1]
    cosine = cosine_ref[...]
    sine = sine_ref[...]

    def rotated(values):
        return values * cosine + pltpu.roll(values, HD // 2, 1) * sine

    for head in range(query.shape[1] // HD):
        part = slice(head * HD, (head + 1) * HD)
        query_out[:, part] = rotated(query[:, part]).astype(jnp.bfloat16)
    is_key = scalar_ref[IS_KEY] != 0
    pair_out[...] = jnp.where(is_key, rotated(pair), pair).astype(jnp.bfloat16)


def blocks_kernel(scalar_ref, held_ref, swapped_ref, out_ref, keys, values):
    sliver = out_ref.shape[1]
    out_ref[...] = jnp.zeros_like(out_ref)

    @pl.when(scalar_ref[IS_PREFILL] != 0)
    def _():
        sort_pair(scalar_ref, held_ref, swapped_ref, keys, values)
        for block in range(TOK // BS):
            start = pl.multiple_of(scalar_ref[CORE] * sliver, sliver) + block * BS
            cell = scalar_ref[CELLS + block]
            out_ref[cell, :, :HD] = keys[pl.ds(start, sliver), :].astype(jnp.bfloat16)
            out_ref[cell, :, HD:] = values[pl.ds(start, sliver), :].astype(jnp.bfloat16)


def called(kernel, shapes, scalars, *arrays, streamed=(), scratch=(), flops=0, grant=12):
    whole = pl.BlockSpec(memory_space=pltpu.VMEM)
    specs = [pl.BlockSpec(memory_space=pl.ANY)] * len(streamed) + [whole] * len(arrays)
    arrays = tuple(streamed) + arrays
    if scalars is not None:
        specs = [pl.BlockSpec(memory_space=pltpu.SMEM)] + specs
        arrays = (scalars,) + arrays
    return pl.pallas_call(
        kernel,
        in_specs=specs,
        out_specs=tuple(whole for _ in shapes),
        out_shape=tuple(jax.ShapeDtypeStruct(shape, kind) for shape, kind in shapes),
        scratch_shapes=scratch,
        compiler_params=pltpu.CompilerParams(vmem_limit_bytes=grant * 2**20),
        cost_estimate=pl.CostEstimate(flops=flops, transcendentals=0, bytes_accessed=2**21),
    )(*arrays)


def outputs_of(kind):
    return (
        jax.ShapeDtypeStruct((TOK, GQ * HD), kind),
        jax.ShapeDtypeStruct((TOK, GQ), jnp.float32),
    )


def prefill_part(scalars, lengths, own, other, keys, values):
    chunks = RP * SPAN // PREFILL_CHUNK
    whole = pl.BlockSpec(memory_space=pltpu.VMEM)
    there = pl.BlockSpec(memory_space=pl.ANY)
    small = pl.BlockSpec(memory_space=pltpu.SMEM)
    return pl.pallas_call(
        prefill_kernel,
        in_specs=[small, small, whole, whole, there, there],
        out_specs=(whole, whole),
        out_shape=outputs_of(jnp.bfloat16),
        scratch_shapes=[
            pltpu.VMEM((R, SPAN, HD), jnp.bfloat16),
            pltpu.VMEM((R, SPAN, HD), jnp.bfloat16),
            pltpu.VMEM((chunks, GQ * CH, PREFILL_CHUNK), jnp.float32),
            pltpu.SemaphoreType.DMA((2, NPR * chunks)),
        ],
        compiler_params=pltpu.CompilerParams(vmem_limit_bytes=44 * 2**20),
    )(scalars, lengths, own, other, keys, values)


def decode_part(scalars, lengths, own, other, keys, values):
    def by_row(array):
        return array.reshape(STEPS, R, -1).transpose(1, 0, 2).reshape(TOK, -1)

    def by_step(array):
        return array.reshape(R, STEPS, -1).transpose(1, 0, 2).reshape(TOK, -1)

    rows = 8 * ROWS_AT_ONCE
    mixed, level = pl.pallas_call(
        decode_kernel,
        grid=(R // rows,),
        in_specs=[
            pl.BlockSpec(memory_space=pltpu.SMEM),
            pl.BlockSpec(memory_space=pltpu.SMEM),
            pl.BlockSpec((rows * STEPS, GQ * HD), lambda i: (i, 0)),
            pl.BlockSpec((rows, SPAN, HD), lambda i: (i, 0, 0)),
            pl.BlockSpec((rows, SPAN, HD), lambda i: (i, 0, 0)),
        ],
        out_specs=(
            pl.BlockSpec((rows * STEPS, GQ * HD), lambda i: (i, 0)),
            pl.BlockSpec((rows * STEPS, GQ), lambda i: (i, 0)),
        ),
        out_shape=outputs_of(jnp.bfloat16),
        compiler_params=pltpu.CompilerParams(vmem_limit_bytes=40 * 2**20),
    )(scalars, lengths, by_row(jnp.concatenate([own, other], axis=1)), keys, values)
    return by_step(mixed), by_step(level)


def cut_kernel(scalar_ref, weight_ref, out_ref, held_ref, in_sems, out_sems):
    fetches = []
    stores = []
    for chip in range(CHIPS):
        columns = pl.ds(pl.multiple_of((2 * chip + 1 - scalar_ref[CORE]) * SHARD, SHARD), SHARD)
        fetches.append(
            pltpu.make_async_copy(weight_ref.at[:, columns], held_ref.at[chip], in_sems.at[chip])
        )
        stores.append(
            pltpu.make_async_copy(
                held_ref.at[chip],
                out_ref.at[:, chip * SHARD : (chip + 1) * SHARD],
                out_sems.at[chip],
            )
        )
    for fetch in fetches:
        fetch.start()
    for fetch, store in zip(fetches, stores):
        fetch.wait()
        store.start()
    for store in stores:
        store.wait()


def cut_columns(scalars, out_weight):
    return pl.pallas_call(
        cut_kernel,
        in_specs=[
            pl.BlockSpec(memory_space=pltpu.SMEM),
            pl.BlockSpec(memory_space=pl.ANY),
        ],
        out_specs=pl.BlockSpec(memory_space=pl.ANY),
        out_shape=jax.ShapeDtypeStruct((out_weight.shape[0], CHIPS * SHARD), jnp.bfloat16),
        scratch_shapes=[
            pltpu.VMEM((CHIPS, out_weight.shape[0], SHARD), jnp.bfloat16),
            pltpu.SemaphoreType.DMA((CHIPS,)),
            pltpu.SemaphoreType.DMA((CHIPS,)),
        ],
        compiler_params=pltpu.CompilerParams(vmem_limit_bytes=12 * 2**20),
    )(scalars, out_weight)


def on_device(
    layer_input, query_weight, kv_weight, out_weight, cache_keys, cache_values, lengths, placement
):
    group_count = lax.axis_size("group")
    tp_rank = lax.axis_index("tp")
    group_rank = lax.axis_index("group")
    core = tp_rank % 2
    y = (tp_rank // 2) % 4
    x_hi = tp_rank // 8
    is_prefill = group_rank == 0
    tokens = layer_input[0]
    row_lengths = lengths[0]
    slot_count = 2 * (TOK // BS) // (group_count - 1)

    def rows_of(*owners):
        firsts = [tp_index(x_hi ^ flip, y + step, core) for flip, step in owners]
        return [first * SHARD for first in firsts] + [(first ^ 1) * SHARD for first in firsts]

    places = ((1, 1), (1, 3), (0, 2), (1, 2), (0, 1), (0, 3), (1, 0), (0, 0))
    single = (
        [core, is_prefill, tp_rank < KVH]
        + rows_of((0, 0), (0, 3), (0, 1), (1, 0))
        + rows_of((1, 3), (1, 1), (0, 2), (1, 2))
        + [(x_hi ^ flip) * 4 + (y + step) % 4 for flip, step in places]
    )
    picks = [group_rank >= 4, group_rank // 2 % 2 == 1, group_rank % 2 == 1]
    scalars = jnp.concatenate(
        [
            jnp.stack([jnp.asarray(one, jnp.int32) for one in single]),
            placement[:, 0] * slot_count + placement[:, 1],
        ]
    )
    prefix = jnp.sum(row_lengths.reshape(NPR, RP), axis=1)
    prompt_positions = (prefix[:, None] + jnp.arange(CH, dtype=jnp.int32)[None, :]).reshape(TOK)
    decode_step_positions = (
        row_lengths[None, :] + jnp.arange(STEPS, dtype=jnp.int32)[:, None]
    ).reshape(TOK)
    positions = jnp.where(is_prefill, prompt_positions, decode_step_positions)

    cut_out = cut_columns(scalars, out_weight)

    wide = ((TOK + HALF, SHARD), jnp.bfloat16)
    half = ((HALF, SHARD), jnp.bfloat16)
    shard = ((TOK, SHARD), jnp.bfloat16)
    four = ((4 * TOK, SHARD), jnp.bfloat16)
    weights = (query_weight, kv_weight)
    sums = (((TOK, query_weight.shape[1]), jnp.float32), ((TOK, kv_weight.shape[1]), jnp.float32))
    partner_tokens = moved(tokens, 1, 0, 0)
    last_tokens, next_tokens = moved(tokens, 0, 1, 0), moved(tokens, 0, 3, 0)
    scalars, picks, positions = lax.optimization_barrier((scalars, picks, positions))
    cosine, sine = turns(positions)
    plus, minus, up, down, near = called(
        join_kernel,
        (wide, wide, half, half, four),
        scalars,
        partner_tokens,
        last_tokens,
        next_tokens,
        streamed=(tokens,),
        scratch=(pltpu.SemaphoreType.DMA(()),),
        flops=LONG,
    )
    from_last, from_next = moved(plus, 0, 1, 0), moved(minus, 0, 3, 0)
    far_upper, far_lower = moved(down, 1, 3, 0), moved(up, 1, 1, 0)
    scalars, cut_out = lax.optimization_barrier((scalars, cut_out))
    *part, mark = called(
        near_kernel,
        sums + (((8, HD), jnp.float32),),
        scalars,
        *weights,
        near,
        core_swap(near),
        flops=2 * TOK * 8 * SHARD * 3 * HD,
    )
    (sides,) = called(
        sides_kernel,
        (four,),
        None,
        from_last,
        from_next,
        far_upper,
        far_lower,
        streamed=(mark,),
    )
    other_sides = core_swap(sides)
    part = called(
        far_kernel,
        sums,
        scalars,
        *weights,
        *part,
        sides,
        flops=2 * TOK * 4 * SHARD * 3 * HD,
    )
    query_local, pair_local = called(
        last_kernel,
        tuple((shape, jnp.bfloat16) for shape, _ in sums),
        scalars,
        *weights,
        *part,
        other_sides,
        cosine,
        sine,
        flops=2 * TOK * 4 * SHARD * 3 * HD,
    )
    pair_local, cut_out = lax.optimization_barrier((pair_local, cut_out))
    query_other = core_swap(query_local)
    pair_held = lax.ppermute(
        pair_local, "tp", [(t, 2 * t if t < KVH else 2 * (t - KVH) + 1) for t in range(2 * KVH)]
    )
    swapped_out = core_swap(cut_out)
    cached = lax.cond(
        is_prefill,
        prefill_part,
        decode_part,
        scalars,
        row_lengths,
        query_local,
        query_other,
        cache_keys[0],
        cache_values[0],
    )
    cached, pair_held = lax.optimization_barrier((cached, pair_held))
    pair_other = core_swap(pair_held)
    other_cached = (core_swap(cached[0]), core_swap(cached[1]))
    recent = called(
        recent_kernel,
        (((TOK, GQ * HD), jnp.bfloat16), ((TOK, GQ), jnp.float32)),
        scalars,
        query_local,
        query_other,
        pair_held,
        pair_other,
        flops=LONG,
    )

    product_scratch = (
        pltpu.VMEM((4, out_weight.shape[0], SHARD), jnp.bfloat16),
        pltpu.SemaphoreType.DMA((4,)),
    )
    plus, minus, up, down, attention = called(
        merge_out_kernel,
        (wide, wide, half, half, ((TOK, GQ * HD), jnp.bfloat16)),
        scalars,
        out_weight,
        *cached,
        *other_cached,
        *recent,
        streamed=(swapped_out,),
        scratch=product_scratch,
        flops=2 * TOK * 4 * SHARD * GQ * HD,
    )
    next_part, last_part, partner_part, here_part = called(
        out_kernel,
        (shard,) * 4,
        scalars,
        out_weight,
        attention,
        streamed=(swapped_out,),
        scratch=product_scratch,
        flops=2 * TOK * 4 * SHARD * GQ * HD,
    )
    from_last, from_next = moved(plus, 0, 1, 0), moved(minus, 0, 3, 0)
    up, down = moved(up, 1, 1, 0), moved(down, 1, 3, 0)

    _, late_scalars = lax.optimization_barrier((attention, scalars))
    (blocks,) = called(
        blocks_kernel,
        (((group_count * slot_count, BS // 2, 2 * HD), jnp.bfloat16),),
        late_scalars,
        pair_held,
        pair_other,
        scratch=(pltpu.VMEM((TOK, HD), jnp.float32),) * 2,
    )
    blocks = blocks.reshape(group_count, slot_count, BS // 2, 2 * HD)
    arrived = lax.ppermute(blocks[4:], "group", [(0, 4)])

    plus, minus, partner = called(
        second_message_kernel,
        (shard, shard, shard),
        None,
        next_part,
        last_part,
        partner_part,
        from_last,
        from_next,
        up,
        down,
        streamed=(arrived,),
    )
    from_last, from_next = moved(plus, 0, 1, 0), moved(minus, 0, 3, 0)
    from_partner = moved(partner, 1, 0, 0)

    blocks = jnp.where(picks[0], arrived, blocks[:4])
    sent = lax.ppermute(blocks[2:], "group", [(0, 2), (4, 6)])
    blocks = jnp.where(picks[1], sent, blocks[:2])
    sent = lax.ppermute(blocks[1:], "group", [(0, 1), (2, 3), (4, 5), (6, 7)])
    incoming = jnp.where(picks[2], sent, blocks[:1])
    (projected,) = called(
        total_kernel, (shard,), None, here_part, from_last, from_next, from_partner
    )
    return (projected[None], incoming)


def solution(mesh):
    in_specs = (
        P("group", None, "tp"),
        P(None, "tp"),
        P(None, "tp"),
        P("tp", None),
        P("group", None, "tp", None),
        P("group", None, "tp", None),
        P("group", None),
        P(),
    )
    out_specs = (P("group", None, "tp"), P("group", None, "tp", None))
    return jax.shard_map(
        on_device, mesh=mesh, in_specs=in_specs, out_specs=out_specs, check_vma=False
    )
```

```python
import jax
import jax.numpy as jnp
from jax import lax
from jax.experimental import pallas as pl
from jax.experimental.pallas import tpu as pltpu
from jax.sharding import PartitionSpec as P

HD = 128
KVH = 8
STEPS = 4
NPR = 2
BS = 16
R = 64
GQ = 4
TOK = 256
CH = 128
RP = 32


NEG_FILL = -1e30


def tp_index(x_hi, y, core):
    return x_hi * 8 + (y % 4) * 2 + core


def moved(shard, x_flip, y_step, core_flip):
    pairs = []
    for x_hi in range(2):
        for y in range(4):
            for core in range(2):
                pairs.append(
                    (
                        tp_index(x_hi, y, core),
                        tp_index(x_hi ^ x_flip, y + y_step, core ^ core_flip),
                    )
                )
    return lax.ppermute(shard, "tp", pairs)


def core_swap(shard):
    return moved(shard, 0, 0, 1)


def turns(positions):
    midpoint = HD // 2
    frequency = jnp.exp(
        -jnp.log(500000.0) * jnp.arange(midpoint, dtype=jnp.float32) * 2.0 / HD
    )
    angles = positions.astype(jnp.float32)[:, None] * frequency[None, :]
    cosine = jnp.cos(angles)
    sine = jnp.sin(angles)
    return (
        jnp.concatenate([cosine, cosine], axis=1),
        jnp.concatenate([-sine, sine], axis=1),
    )


SPAN = 256
CHIPS = 8
SHARD = 512
HALF = TOK // 2
PREFILL_CHUNK = 4096
ROWS_AT_ONCE = 4
LOG2_E = 1.4426950408889634
NT = (((1,), (1,)), ((), ()))
LONG = 6 * 10**9

CORE, IS_PREFILL, IS_KEY, NEAR_ROWS, FAR_ROWS, PLACE, CELLS = 0, 1, 2, 3, 11, 19, 27


def stacked_heads(*parts):
    return jnp.concatenate(
        [part[:, j * HD : (j + 1) * HD] for part in parts for j in range(part.shape[1] // HD)],
        axis=0,
    )


def length_bias(scalar_ref, length_ref, first, count):
    place = lax.broadcasted_iota(jnp.int32, (1, SPAN), 1) + scalar_ref[CORE] * SPAN
    return jnp.concatenate(
        [jnp.where(place < length_ref[first + row], 0.0, NEG_FILL) for row in range(count)],
        axis=1,
    )


def weights_of(scores, largest):
    return jnp.exp2((scores - largest) * (HD**-0.5 * LOG2_E)).astype(jnp.bfloat16)


def with_ones(values):
    return jnp.concatenate([values, jnp.ones_like(values)], axis=1)


def write_heads(mixed_ref, level_ref, rows, mixed, largest):
    count = mixed.shape[0] // GQ
    total = mixed[:, HD : HD + 1]
    normal = (mixed[:, :HD] / total).astype(jnp.bfloat16)
    level = largest * HD**-0.5 + jnp.log(total)
    lane = lax.broadcasted_iota(jnp.int32, (count, GQ), 1)
    levels = jnp.zeros((count, GQ), jnp.float32)
    for j in range(GQ):
        part = slice(j * count, (j + 1) * count)
        mixed_ref[rows, j * HD : (j + 1) * HD] = normal[part]
        levels = jnp.where(lane == j, level[part], levels)
    level_ref[rows, :] = levels


def prefill_kernel(
    scalar_ref,
    length_ref,
    own_ref,
    other_ref,
    key_ref,
    value_ref,
    mixed_ref,
    level_ref,
    keys,
    values,
    score_ref,
    sems,
):
    rows = PREFILL_CHUNK // SPAN
    chunks = RP // rows

    def fetches(prompt, step):
        part = pl.ds(prompt * RP + step * rows, rows)
        index = prompt * chunks + step
        return (
            pltpu.make_async_copy(key_ref.at[part], keys.at[part], sems.at[0, index]),
            pltpu.make_async_copy(value_ref.at[part], values.at[part], sems.at[1, index]),
        )

    for prompt in range(NPR):
        for kind in range(2):
            for step in range(chunks):
                fetches(prompt, step)[kind].start()

    def one_prompt(prompt, carry):
        tokens = pl.ds(pl.multiple_of(prompt * CH, CH), CH)
        queries = stacked_heads(own_ref[tokens, :], other_ref[tokens, :])

        def score_step(step, peak):
            fetches(prompt, step)[0].wait()
            part = keys[pl.ds(prompt * RP + step * rows, rows)].reshape(PREFILL_CHUNK, HD)
            scores = lax.dot_general(queries, part, NT, preferred_element_type=jnp.float32)
            scores = scores + length_bias(scalar_ref, length_ref, prompt * RP + step * rows, rows)
            score_ref[step] = scores
            for lanes in range(PREFILL_CHUNK // HD):
                peak = jnp.maximum(peak, scores[:, lanes * HD : (lanes + 1) * HD])
            return peak

        peak = lax.fori_loop(
            0, chunks, score_step, jnp.full((GQ * CH, HD), NEG_FILL, jnp.float32)
        )
        largest = jnp.max(peak, axis=1, keepdims=True)
        level = jnp.broadcast_to(largest, (GQ * CH, HD))

        def mix_step(step, mixed):
            fetches(prompt, step)[1].wait()
            weights = jnp.concatenate(
                [
                    weights_of(score_ref[step, :, lanes * HD : (lanes + 1) * HD], level)
                    for lanes in range(PREFILL_CHUNK // HD)
                ],
                axis=1,
            )
            part = values[pl.ds(prompt * RP + step * rows, rows)].reshape(PREFILL_CHUNK, HD)
            return mixed + jnp.dot(weights, with_ones(part), preferred_element_type=jnp.float32)

        mixed = lax.fori_loop(0, chunks, mix_step, jnp.zeros((GQ * CH, 2 * HD), jnp.float32))
        write_heads(mixed_ref, level_ref, tokens, mixed, largest)
        return carry

    lax.fori_loop(0, NPR, one_prompt, 0)


def decode_kernel(
    scalar_ref, length_ref, query_ref, key_ref, value_ref, mixed_ref, level_ref
):
    width = ROWS_AT_ONCE * SPAN
    tokens = ROWS_AT_ONCE * STEPS
    owner = lax.broadcasted_iota(jnp.int32, (GQ * tokens, width), 0) % tokens // STEPS
    holder = lax.broadcasted_iota(jnp.int32, (GQ * tokens, width), 1) // SPAN
    for part in range(query_ref.shape[0] // tokens):
        rows = slice(part * tokens, (part + 1) * tokens)
        cached = slice(part * ROWS_AT_ONCE, (part + 1) * ROWS_AT_ONCE)
        queries = stacked_heads(query_ref[rows, :])
        keys = key_ref[cached].reshape(width, HD)
        values = value_ref[cached].reshape(width, HD)
        scores = lax.dot_general(queries, keys, NT, preferred_element_type=jnp.float32)
        first = (pl.program_id(0) * (query_ref.shape[0] // tokens) + part) * ROWS_AT_ONCE
        bias = length_bias(scalar_ref, length_ref, first, ROWS_AT_ONCE)
        scores = jnp.where(owner == holder, scores + bias, NEG_FILL)
        largest = jnp.max(scores, axis=1, keepdims=True)
        mixed = jnp.dot(
            weights_of(scores, largest), with_ones(values), preferred_element_type=jnp.float32
        )
        write_heads(mixed_ref, level_ref, rows, mixed, largest)


def sort_pair(scalar_ref, held_ref, swapped_ref, keys, values):
    @pl.when(scalar_ref[CORE] == 0)
    def _():
        keys[...] = held_ref[...].astype(keys.dtype)
        values[...] = swapped_ref[...].astype(values.dtype)

    @pl.when(scalar_ref[CORE] != 0)
    def _():
        keys[...] = swapped_ref[...].astype(keys.dtype)
        values[...] = held_ref[...].astype(values.dtype)


def recent_kernel(scalar_ref, own_ref, other_ref, held_ref, swapped_ref, mixed_ref, level_ref):
    row = lax.broadcasted_iota(jnp.int32, (TOK, TOK), 0)
    column = lax.broadcasted_iota(jnp.int32, (TOK, TOK), 1)
    is_prefill = scalar_ref[IS_PREFILL] != 0
    together = jnp.where(is_prefill, row // CH - column // CH, row % R - column % R) == 0
    allowed = together & (column <= row)
    lane = lax.broadcasted_iota(jnp.int32, (TOK, GQ), 1)

    held = held_ref[...].astype(jnp.float32)
    swapped = swapped_ref[...].astype(jnp.float32)
    first = scalar_ref[CORE] == 0
    keys = jnp.where(first, held, swapped).astype(jnp.bfloat16)
    values = with_ones(jnp.where(first, swapped, held).astype(jnp.bfloat16))
    levels = jnp.zeros((TOK, GQ), jnp.float32)
    for j in range(GQ):
        source = own_ref if j < GQ // 2 else other_ref
        part = slice(j % (GQ // 2) * HD, (j % (GQ // 2) + 1) * HD)
        scores = lax.dot_general(
            source[:, part], keys, NT, preferred_element_type=jnp.float32
        )
        scores = jnp.where(allowed, scores, NEG_FILL)
        largest = jnp.max(scores, axis=1, keepdims=True)
        mixed = jnp.dot(
            weights_of(scores, largest), values, preferred_element_type=jnp.float32
        )
        total = mixed[:, HD : HD + 1]
        mixed_ref[:, j * HD : (j + 1) * HD] = (mixed[:, :HD] / total).astype(mixed_ref.dtype)
        levels = jnp.where(lane == j, largest * HD**-0.5 + jnp.log(total), levels)
    level_ref[...] = levels


def merged(parts, levels):
    half = GQ // 2
    turned = jnp.concatenate([levels[1][:, half:], levels[1][:, :half]], axis=1)
    levels = [levels[0], turned, levels[2]]
    top = jnp.maximum(jnp.maximum(levels[0], levels[1]), levels[2])
    shares = [jnp.exp(level - top) for level in levels]
    total = shares[0] + shares[1] + shares[2]
    shares = [share / total for share in shares]
    heads = []
    for j in range(GQ):
        mixed = jnp.zeros((TOK, HD), jnp.float32)
        for part, share, place in zip(parts, shares, (j, (j + half) % GQ, j)):
            values = part[:, place * HD : (place + 1) * HD].astype(jnp.float32)
            mixed = mixed + values * share[:, j : j + 1]
        heads.append(mixed.astype(jnp.bfloat16))
    return jnp.concatenate(heads, axis=1)


def swapped_copies(scalar_ref, first, swapped_ref, held_ref, sems):
    copies = []
    for index in range(4):
        columns = pl.ds(pl.multiple_of(scalar_ref[PLACE + first + index] * SHARD, SHARD), SHARD)
        copies.append(
            pltpu.make_async_copy(
                swapped_ref.at[:, columns], held_ref.at[index], sems.at[index]
            )
        )
        copies[-1].start()
    return copies


def product(scalar_ref, chip, joined, copy, weight_ref, held_ref, index):
    column = 2 * scalar_ref[PLACE + chip] + scalar_ref[CORE]
    own = weight_ref[:, pl.ds(pl.multiple_of(column * SHARD, SHARD), SHARD)]
    copy.wait()
    weights = jnp.concatenate([own, held_ref[index]], axis=0)
    return jnp.dot(joined, weights, preferred_element_type=jnp.float32).astype(jnp.bfloat16)


def merge_out_kernel(
    scalar_ref,
    swapped_ref,
    weight_ref,
    own_ref,
    own_level,
    other_ref,
    other_level,
    recent_ref,
    recent_level,
    plus,
    minus,
    up,
    down,
    attention,
    held_ref,
    sems,
):
    copies = swapped_copies(scalar_ref, 0, swapped_ref, held_ref, sems)
    joined = merged(
        (own_ref, other_ref, recent_ref), (own_level[...], other_level[...], recent_level[...])
    )
    attention[...] = joined
    parts = [
        product(scalar_ref, index, joined, copies[index], weight_ref, held_ref, index)
        for index in range(4)
    ]
    plus[:TOK] = parts[0]
    minus[:TOK] = parts[1]
    plus[TOK:] = parts[2][:HALF]
    minus[TOK:] = parts[2][HALF:]
    up[...] = parts[3][:HALF]
    down[...] = parts[3][HALF:]


def out_kernel(scalar_ref, swapped_ref, weight_ref, attention, *refs):
    *out_refs, held_ref, sems = refs
    copies = swapped_copies(scalar_ref, 4, swapped_ref, held_ref, sems)
    joined = attention[...]
    for index, ref in enumerate(out_refs):
        ref[...] = product(
            scalar_ref, 4 + index, joined, copies[index], weight_ref, held_ref, index
        )


def total_of(*parts):
    total = parts[0].astype(jnp.float32)
    for part in parts[1:]:
        total = total + part.astype(jnp.float32)
    return total.astype(jnp.bfloat16)


def second_message_kernel(
    arrived_ref,
    next_ref,
    last_ref,
    partner_ref,
    from_last,
    from_next,
    up,
    down,
    plus,
    minus,
    partner,
):
    plus[:HALF] = total_of(next_ref[:HALF], from_last[TOK:], up[...])
    plus[HALF:] = next_ref[HALF:]
    minus[:HALF] = last_ref[:HALF]
    minus[HALF:] = total_of(last_ref[HALF:], from_next[TOK:], down[...])
    partner[...] = total_of(partner_ref[...], from_last[:TOK], from_next[:TOK])


def total_kernel(here_ref, from_last, from_next, from_partner, out_ref):
    out_ref[...] = total_of(here_ref[...], from_last[...], from_next[...], from_partner[...])


def join_kernel(
    scalar_ref, swapped_ref, partner_ref, last_ref, next_ref, plus, minus, up, down, near
):
    plus[:TOK] = partner_ref[...]
    plus[TOK:] = last_ref[:HALF]
    minus[:TOK] = partner_ref[...]
    minus[TOK:] = next_ref[HALF:]
    up[...] = last_ref[HALF:]
    down[...] = next_ref[:HALF]
    for index, ref in enumerate((last_ref, next_ref, partner_ref)):
        near[index * TOK : (index + 1) * TOK] = ref[...]


def sides_kernel(mark_ref, last_ref, next_ref, upper_ref, lower_ref, sides):
    sides[:TOK] = last_ref[:TOK]
    sides[TOK : 2 * TOK] = next_ref[:TOK]
    sides[2 * TOK : 2 * TOK + HALF] = last_ref[TOK:]
    sides[2 * TOK + HALF : 3 * TOK] = next_ref[TOK:]
    sides[3 * TOK : 3 * TOK + HALF] = upper_ref[...]
    sides[3 * TOK + HALF :] = lower_ref[...]


def projected_parts(scalar_ref, first, shards, query_weight, pair_weight):
    joined = jnp.concatenate(shards, axis=1)
    rows = [
        pl.ds(pl.multiple_of(scalar_ref[first + index], SHARD), SHARD)
        for index in range(len(shards))
    ]
    return [
        jnp.dot(
            joined,
            jnp.concatenate([weight[part, :] for part in rows], axis=0),
            preferred_element_type=jnp.float32,
        )
        for weight in (query_weight, pair_weight)
    ]


def shards_of(ref):
    return [ref[index * TOK : (index + 1) * TOK] for index in range(ref.shape[0] // TOK)]


def near_kernel(
    scalar_ref,
    query_weight,
    pair_weight,
    own_ref,
    near_ref,
    other_ref,
    other_near_ref,
    query,
    pair,
    mark,
):
    mark[...] = jnp.zeros_like(mark)
    sources = (own_ref, near_ref, other_ref, other_near_ref)
    shards = [shard for ref in sources for shard in shards_of(ref)]
    query[...], pair[...] = projected_parts(
        scalar_ref, NEAR_ROWS, shards, query_weight, pair_weight
    )


def far_kernel(scalar_ref, query_weight, pair_weight, query_in, pair_in, far_ref, query, pair):
    sums = projected_parts(scalar_ref, FAR_ROWS, shards_of(far_ref), query_weight, pair_weight)
    query[...] = query_in[...] + sums[0]
    pair[...] = pair_in[...] + sums[1]


def last_kernel(
    scalar_ref,
    query_weight,
    pair_weight,
    query_in,
    pair_in,
    far_ref,
    cosine_ref,
    sine_ref,
    query_out,
    pair_out,
):
    sums = projected_parts(
        scalar_ref, FAR_ROWS + 4, shards_of(far_ref), query_weight, pair_weight
    )
    query = query_in[...] + sums[0]
    pair = pair_in[...] + sums[1]
    cosine = cosine_ref[...]
    sine = sine_ref[...]

    def rotated(values):
        return values * cosine + pltpu.roll(values, HD // 2, 1) * sine

    for head in range(query.shape[1] // HD):
        part = slice(head * HD, (head + 1) * HD)
        query_out[:, part] = rotated(query[:, part]).astype(jnp.bfloat16)
    is_key = scalar_ref[IS_KEY] != 0
    pair_out[...] = jnp.where(is_key, rotated(pair), pair).astype(jnp.bfloat16)


def blocks_kernel(scalar_ref, held_ref, swapped_ref, out_ref, keys, values):
    sliver = out_ref.shape[1]
    out_ref[...] = jnp.zeros_like(out_ref)

    @pl.when(scalar_ref[IS_PREFILL] != 0)
    def _():
        sort_pair(scalar_ref, held_ref, swapped_ref, keys, values)
        for block in range(TOK // BS):
            start = pl.multiple_of(scalar_ref[CORE] * sliver, sliver) + block * BS
            cell = scalar_ref[CELLS + block]
            out_ref[cell, :, :HD] = keys[pl.ds(start, sliver), :].astype(jnp.bfloat16)
            out_ref[cell, :, HD:] = values[pl.ds(start, sliver), :].astype(jnp.bfloat16)


def called(kernel, shapes, scalars, *arrays, streamed=(), scratch=(), flops=0, grant=12):
    whole = pl.BlockSpec(memory_space=pltpu.VMEM)
    specs = [pl.BlockSpec(memory_space=pl.ANY)] * len(streamed) + [whole] * len(arrays)
    arrays = tuple(streamed) + arrays
    if scalars is not None:
        specs = [pl.BlockSpec(memory_space=pltpu.SMEM)] + specs
        arrays = (scalars,) + arrays
    return pl.pallas_call(
        kernel,
        in_specs=specs,
        out_specs=tuple(whole for _ in shapes),
        out_shape=tuple(jax.ShapeDtypeStruct(shape, kind) for shape, kind in shapes),
        scratch_shapes=scratch,
        compiler_params=pltpu.CompilerParams(vmem_limit_bytes=grant * 2**20),
        cost_estimate=pl.CostEstimate(flops=flops, transcendentals=0, bytes_accessed=2**21),
    )(*arrays)


def outputs_of(kind):
    return (
        jax.ShapeDtypeStruct((TOK, GQ * HD), kind),
        jax.ShapeDtypeStruct((TOK, GQ), jnp.float32),
    )


def prefill_part(scalars, lengths, own, other, keys, values):
    chunks = RP * SPAN // PREFILL_CHUNK
    whole = pl.BlockSpec(memory_space=pltpu.VMEM)
    there = pl.BlockSpec(memory_space=pl.ANY)
    small = pl.BlockSpec(memory_space=pltpu.SMEM)
    return pl.pallas_call(
        prefill_kernel,
        in_specs=[small, small, whole, whole, there, there],
        out_specs=(whole, whole),
        out_shape=outputs_of(jnp.bfloat16),
        scratch_shapes=[
            pltpu.VMEM((R, SPAN, HD), jnp.bfloat16),
            pltpu.VMEM((R, SPAN, HD), jnp.bfloat16),
            pltpu.VMEM((chunks, GQ * CH, PREFILL_CHUNK), jnp.float32),
            pltpu.SemaphoreType.DMA((2, NPR * chunks)),
        ],
        compiler_params=pltpu.CompilerParams(vmem_limit_bytes=44 * 2**20),
    )(scalars, lengths, own, other, keys, values)


def decode_part(scalars, lengths, own, other, keys, values):
    def by_row(array):
        return array.reshape(STEPS, R, -1).transpose(1, 0, 2).reshape(TOK, -1)

    def by_step(array):
        return array.reshape(R, STEPS, -1).transpose(1, 0, 2).reshape(TOK, -1)

    rows = 8 * ROWS_AT_ONCE
    mixed, level = pl.pallas_call(
        decode_kernel,
        grid=(R // rows,),
        in_specs=[
            pl.BlockSpec(memory_space=pltpu.SMEM),
            pl.BlockSpec(memory_space=pltpu.SMEM),
            pl.BlockSpec((rows * STEPS, GQ * HD), lambda i: (i, 0)),
            pl.BlockSpec((rows, SPAN, HD), lambda i: (i, 0, 0)),
            pl.BlockSpec((rows, SPAN, HD), lambda i: (i, 0, 0)),
        ],
        out_specs=(
            pl.BlockSpec((rows * STEPS, GQ * HD), lambda i: (i, 0)),
            pl.BlockSpec((rows * STEPS, GQ), lambda i: (i, 0)),
        ),
        out_shape=outputs_of(jnp.bfloat16),
        compiler_params=pltpu.CompilerParams(vmem_limit_bytes=40 * 2**20),
    )(scalars, lengths, by_row(jnp.concatenate([own, other], axis=1)), keys, values)
    return by_step(mixed), by_step(level)


def cut_kernel(scalar_ref, weight_ref, out_ref, held_ref, in_sems, out_sems):
    fetches = []
    stores = []
    for chip in range(CHIPS):
        columns = pl.ds(pl.multiple_of((2 * chip + 1 - scalar_ref[CORE]) * SHARD, SHARD), SHARD)
        fetches.append(
            pltpu.make_async_copy(weight_ref.at[:, columns], held_ref.at[chip], in_sems.at[chip])
        )
        stores.append(
            pltpu.make_async_copy(
                held_ref.at[chip],
                out_ref.at[:, chip * SHARD : (chip + 1) * SHARD],
                out_sems.at[chip],
            )
        )
    for fetch in fetches:
        fetch.start()
    for fetch, store in zip(fetches, stores):
        fetch.wait()
        store.start()
    for store in stores:
        store.wait()


def cut_columns(scalars, out_weight):
    return pl.pallas_call(
        cut_kernel,
        in_specs=[
            pl.BlockSpec(memory_space=pltpu.SMEM),
            pl.BlockSpec(memory_space=pl.ANY),
        ],
        out_specs=pl.BlockSpec(memory_space=pl.ANY),
        out_shape=jax.ShapeDtypeStruct((out_weight.shape[0], CHIPS * SHARD), jnp.bfloat16),
        scratch_shapes=[
            pltpu.VMEM((CHIPS, out_weight.shape[0], SHARD), jnp.bfloat16),
            pltpu.SemaphoreType.DMA((CHIPS,)),
            pltpu.SemaphoreType.DMA((CHIPS,)),
        ],
        compiler_params=pltpu.CompilerParams(vmem_limit_bytes=12 * 2**20),
    )(scalars, out_weight)


def on_device(
    layer_input, query_weight, kv_weight, out_weight, cache_keys, cache_values, lengths, placement
):
    group_count = lax.axis_size("group")
    tp_rank = lax.axis_index("tp")
    group_rank = lax.axis_index("group")
    core = tp_rank % 2
    y = (tp_rank // 2) % 4
    x_hi = tp_rank // 8
    is_prefill = group_rank == 0
    tokens = layer_input[0]
    row_lengths = lengths[0]
    slot_count = 2 * (TOK // BS) // (group_count - 1)

    def rows_of(*owners):
        firsts = [tp_index(x_hi ^ flip, y + step, core) for flip, step in owners]
        return [first * SHARD for first in firsts] + [(first ^ 1) * SHARD for first in firsts]

    places = ((1, 1), (1, 3), (0, 2), (1, 2), (0, 1), (0, 3), (1, 0), (0, 0))
    single = (
        [core, is_prefill, tp_rank < KVH]
        + rows_of((0, 0), (0, 3), (0, 1), (1, 0))
        + rows_of((1, 3), (1, 1), (0, 2), (1, 2))
        + [(x_hi ^ flip) * 4 + (y + step) % 4 for flip, step in places]
    )
    picks = [group_rank >= 4, group_rank // 2 % 2 == 1, group_rank % 2 == 1]
    scalars = jnp.concatenate(
        [
            jnp.stack([jnp.asarray(one, jnp.int32) for one in single]),
            placement[:, 0] * slot_count + placement[:, 1],
        ]
    )
    prefix = jnp.sum(row_lengths.reshape(NPR, RP), axis=1)
    prompt_positions = (prefix[:, None] + jnp.arange(CH, dtype=jnp.int32)[None, :]).reshape(TOK)
    decode_step_positions = (
        row_lengths[None, :] + jnp.arange(STEPS, dtype=jnp.int32)[:, None]
    ).reshape(TOK)
    positions = jnp.where(is_prefill, prompt_positions, decode_step_positions)

    cut_out = cut_columns(scalars, out_weight)

    wide = ((TOK + HALF, SHARD), jnp.bfloat16)
    half = ((HALF, SHARD), jnp.bfloat16)
    shard = ((TOK, SHARD), jnp.bfloat16)
    triple = ((3 * TOK, SHARD), jnp.bfloat16)
    four = ((4 * TOK, SHARD), jnp.bfloat16)
    weights = (query_weight, kv_weight)
    sums = (((TOK, query_weight.shape[1]), jnp.float32), ((TOK, kv_weight.shape[1]), jnp.float32))
    partner_tokens = moved(tokens, 1, 0, 0)
    last_tokens, next_tokens = moved(tokens, 0, 1, 0), moved(tokens, 0, 3, 0)
    other_tokens = core_swap(tokens)
    scalars, picks, positions = lax.optimization_barrier((scalars, picks, positions))
    cosine, sine = turns(positions)
    plus, minus, up, down, near = called(
        join_kernel,
        (wide, wide, half, half, triple),
        scalars,
        partner_tokens,
        last_tokens,
        next_tokens,
        streamed=(other_tokens,),
        flops=LONG,
    )
    from_last, from_next = moved(plus, 0, 1, 0), moved(minus, 0, 3, 0)
    far_upper, far_lower = moved(down, 1, 3, 0), moved(up, 1, 1, 0)
    scalars, cut_out = lax.optimization_barrier((scalars, cut_out))
    swapped_out = core_swap(cut_out)
    *part, mark = called(
        near_kernel,
        sums + (((8, HD), jnp.float32),),
        scalars,
        *weights,
        tokens,
        near,
        other_tokens,
        core_swap(near),
        flops=2 * TOK * 8 * SHARD * 3 * HD,
    )
    (sides,) = called(
        sides_kernel,
        (four,),
        None,
        from_last,
        from_next,
        far_upper,
        far_lower,
        streamed=(mark,),
    )
    other_sides = core_swap(sides)
    part = called(
        far_kernel,
        sums,
        scalars,
        *weights,
        *part,
        sides,
        flops=2 * TOK * 4 * SHARD * 3 * HD,
    )
    query_local, pair_local = called(
        last_kernel,
        tuple((shape, jnp.bfloat16) for shape, _ in sums),
        scalars,
        *weights,
        *part,
        other_sides,
        cosine,
        sine,
        flops=2 * TOK * 4 * SHARD * 3 * HD,
    )
    query_other = core_swap(query_local)
    pair_held = lax.ppermute(
        pair_local, "tp", [(t, 2 * t if t < KVH else 2 * (t - KVH) + 1) for t in range(2 * KVH)]
    )
    cached = lax.cond(
        is_prefill,
        prefill_part,
        decode_part,
        scalars,
        row_lengths,
        query_local,
        query_other,
        cache_keys[0],
        cache_values[0],
    )
    cached, pair_held = lax.optimization_barrier((cached, pair_held))
    pair_other = core_swap(pair_held)
    other_cached = (core_swap(cached[0]), core_swap(cached[1]))
    recent = called(
        recent_kernel,
        (((TOK, GQ * HD), jnp.bfloat16), ((TOK, GQ), jnp.float32)),
        scalars,
        query_local,
        query_other,
        pair_held,
        pair_other,
        flops=LONG,
    )

    product_scratch = (
        pltpu.VMEM((4, out_weight.shape[0], SHARD), jnp.bfloat16),
        pltpu.SemaphoreType.DMA((4,)),
    )
    plus, minus, up, down, attention = called(
        merge_out_kernel,
        (wide, wide, half, half, ((TOK, GQ * HD), jnp.bfloat16)),
        scalars,
        out_weight,
        *cached,
        *other_cached,
        *recent,
        streamed=(swapped_out,),
        scratch=product_scratch,
        flops=2 * TOK * 4 * SHARD * GQ * HD,
    )
    next_part, last_part, partner_part, here_part = called(
        out_kernel,
        (shard,) * 4,
        scalars,
        out_weight,
        attention,
        streamed=(swapped_out,),
        scratch=product_scratch,
        flops=2 * TOK * 4 * SHARD * GQ * HD,
    )
    from_last, from_next = moved(plus, 0, 1, 0), moved(minus, 0, 3, 0)
    up, down = moved(up, 1, 1, 0), moved(down, 1, 3, 0)

    _, late_scalars = lax.optimization_barrier((attention, scalars))
    (blocks,) = called(
        blocks_kernel,
        (((group_count * slot_count, BS // 2, 2 * HD), jnp.bfloat16),),
        late_scalars,
        pair_held,
        pair_other,
        scratch=(pltpu.VMEM((TOK, HD), jnp.float32),) * 2,
    )
    blocks = blocks.reshape(group_count, slot_count, BS // 2, 2 * HD)
    arrived = lax.ppermute(blocks[4:], "group", [(0, 4)])

    plus, minus, partner = called(
        second_message_kernel,
        (shard, shard, shard),
        None,
        next_part,
        last_part,
        partner_part,
        from_last,
        from_next,
        up,
        down,
        streamed=(arrived,),
    )
    from_last, from_next = moved(plus, 0, 1, 0), moved(minus, 0, 3, 0)
    from_partner = moved(partner, 1, 0, 0)

    blocks = jnp.where(picks[0], arrived, blocks[:4])
    sent = lax.ppermute(blocks[2:], "group", [(0, 2), (4, 6)])
    blocks = jnp.where(picks[1], sent, blocks[:2])
    sent = lax.ppermute(blocks[1:], "group", [(0, 1), (2, 3), (4, 5), (6, 7)])
    incoming = jnp.where(picks[2], sent, blocks[:1])
    (projected,) = called(
        total_kernel, (shard,), None, here_part, from_last, from_next, from_partner
    )
    return (projected[None], incoming)


def solution(mesh):
    in_specs = (
        P("group", None, "tp"),
        P(None, "tp"),
        P(None, "tp"),
        P("tp", None),
        P("group", None, "tp", None),
        P("group", None, "tp", None),
        P("group", None),
        P(),
    )
    out_specs = (P("group", None, "tp"), P("group", None, "tp", None))
    return jax.shard_map(
        on_device, mesh=mesh, in_specs=in_specs, out_specs=out_specs, check_vma=False
    )
```

```python
import jax
import jax.numpy as jnp
from jax import lax
from jax.experimental import pallas as pl
from jax.experimental.pallas import tpu as pltpu
from jax.sharding import PartitionSpec as P

HD = 128
KVH = 8
STEPS = 4
NPR = 2
BS = 16
R = 64
GQ = 4
TOK = 256
CH = 128
RP = 32


NEG_FILL = -1e30


def tp_index(x_hi, y, core):
    return x_hi * 8 + (y % 4) * 2 + core


def moved(shard, x_flip, y_step, core_flip):
    pairs = []
    for x_hi in range(2):
        for y in range(4):
            for core in range(2):
                pairs.append(
                    (
                        tp_index(x_hi, y, core),
                        tp_index(x_hi ^ x_flip, y + y_step, core ^ core_flip),
                    )
                )
    return lax.ppermute(shard, "tp", pairs)


def core_swap(shard):
    return moved(shard, 0, 0, 1)


def turns(positions):
    midpoint = HD // 2
    frequency = jnp.exp(
        -jnp.log(500000.0) * jnp.arange(midpoint, dtype=jnp.float32) * 2.0 / HD
    )
    angles = positions.astype(jnp.float32)[:, None] * frequency[None, :]
    cosine = jnp.cos(angles)
    sine = jnp.sin(angles)
    return (
        jnp.concatenate([cosine, cosine], axis=1),
        jnp.concatenate([-sine, sine], axis=1),
    )


SPAN = 256
CHIPS = 8
SHARD = 512
HALF = TOK // 2
PREFILL_CHUNK = 4096
ROWS_AT_ONCE = 4
LOG2_E = 1.4426950408889634
NT = (((1,), (1,)), ((), ()))
TN = (((0,), (0,)), ((), ()))
LONG = 6 * 10**9

CORE, IS_PREFILL, IS_KEY, NEAR_ROWS, FAR_ROWS, PLACE, CELLS = 0, 1, 2, 3, 11, 19, 27


def stacked_heads(*parts):
    return jnp.concatenate(
        [part[:, j * HD : (j + 1) * HD] for part in parts for j in range(part.shape[1] // HD)],
        axis=0,
    )


def length_bias(scalar_ref, length_ref, first, count):
    place = lax.broadcasted_iota(jnp.int32, (1, SPAN), 1) + scalar_ref[CORE] * SPAN
    return jnp.concatenate(
        [jnp.where(place < length_ref[first + row], 0.0, NEG_FILL) for row in range(count)],
        axis=1,
    )


def weights_of(scores, largest):
    return jnp.exp2((scores - largest) * (HD**-0.5 * LOG2_E)).astype(jnp.bfloat16)


def with_ones(values):
    return jnp.concatenate([values, jnp.ones_like(values)], axis=1)


def write_heads(mixed_ref, level_ref, rows, mixed, largest):
    count = mixed.shape[0] // GQ
    total = mixed[:, HD : HD + 1]
    normal = (mixed[:, :HD] / total).astype(jnp.bfloat16)
    level = largest * HD**-0.5 + jnp.log(total)
    lane = lax.broadcasted_iota(jnp.int32, (count, GQ), 1)
    levels = jnp.zeros((count, GQ), jnp.float32)
    for j in range(GQ):
        part = slice(j * count, (j + 1) * count)
        mixed_ref[rows, j * HD : (j + 1) * HD] = normal[part]
        levels = jnp.where(lane == j, level[part], levels)
    level_ref[rows, :] = levels


def prefill_kernel(
    scalar_ref,
    length_ref,
    own_ref,
    other_ref,
    key_ref,
    value_ref,
    mixed_ref,
    level_ref,
    keys,
    values,
    score_ref,
    sems,
):
    rows = PREFILL_CHUNK // SPAN
    chunks = RP // rows

    def fetches(prompt, step):
        part = pl.ds(prompt * RP + step * rows, rows)
        index = prompt * chunks + step
        return (
            pltpu.make_async_copy(key_ref.at[part], keys.at[part], sems.at[0, index]),
            pltpu.make_async_copy(value_ref.at[part], values.at[part], sems.at[1, index]),
        )

    for prompt in range(NPR):
        for kind in range(2):
            for step in range(chunks):
                fetches(prompt, step)[kind].start()

    position = lax.broadcasted_iota(jnp.int32, (SPAN, GQ * CH), 0) + scalar_ref[CORE] * SPAN
    folded = (PREFILL_CHUNK // 8, 8, GQ * CH)

    def one_prompt(prompt, carry):
        tokens = pl.ds(pl.multiple_of(prompt * CH, CH), CH)
        queries = stacked_heads(own_ref[tokens, :], other_ref[tokens, :])

        def score_step(step, peak):
            fetches(prompt, step)[0].wait()
            first = prompt * RP + step * rows
            part = keys[pl.ds(first, rows)].reshape(PREFILL_CHUNK, HD)
            scores = lax.dot_general(part, queries, NT, preferred_element_type=jnp.float32)
            scores = jnp.concatenate(
                [
                    jnp.where(
                        position < length_ref[first + row],
                        scores[row * SPAN : (row + 1) * SPAN],
                        NEG_FILL,
                    )
                    for row in range(rows)
                ],
                axis=0,
            )
            score_ref[step] = scores
            return jnp.maximum(peak, jnp.max(scores.reshape(folded), axis=0))

        peak = lax.fori_loop(0, chunks, score_step, jnp.full((8, GQ * CH), NEG_FILL, jnp.float32))
        largest = jnp.max(peak, axis=0, keepdims=True)

        def mix_step(step, sums):
            mixed, total = sums
            fetches(prompt, step)[1].wait()
            weights = jnp.exp2((score_ref[step] - largest) * (HD**-0.5 * LOG2_E))
            total = total + jnp.sum(weights.reshape(folded), axis=0)
            part = values[pl.ds(prompt * RP + step * rows, rows)].reshape(PREFILL_CHUNK, HD)
            mixed = mixed + lax.dot_general(
                part, weights.astype(jnp.bfloat16), TN, preferred_element_type=jnp.float32
            )
            return mixed, total

        mixed, total = lax.fori_loop(
            0,
            chunks,
            mix_step,
            (jnp.zeros((HD, GQ * CH), jnp.float32), jnp.zeros((8, GQ * CH), jnp.float32)),
        )
        total = jnp.sum(total, axis=0, keepdims=True)
        normal = mixed / total
        level = jnp.broadcast_to(largest * HD**-0.5 + jnp.log(total), (8, GQ * CH))
        lane = lax.broadcasted_iota(jnp.int32, (CH, GQ), 1)
        levels = jnp.zeros((CH, GQ), jnp.float32)
        for j in range(GQ):
            head = slice(j * HD, (j + 1) * HD)
            mixed_ref[tokens, head] = normal[:, j * CH : (j + 1) * CH].T.astype(jnp.bfloat16)
            column = level[:, j * CH : (j + 1) * CH].T
            levels = jnp.where(lane == j, column[:, :1], levels)
        level_ref[tokens, :] = levels
        return carry

    lax.fori_loop(0, NPR, one_prompt, 0)


def decode_kernel(
    scalar_ref, length_ref, query_ref, key_ref, value_ref, mixed_ref, level_ref
):
    width = ROWS_AT_ONCE * SPAN
    tokens = ROWS_AT_ONCE * STEPS
    owner = lax.broadcasted_iota(jnp.int32, (GQ * tokens, width), 0) % tokens // STEPS
    holder = lax.broadcasted_iota(jnp.int32, (GQ * tokens, width), 1) // SPAN
    for part in range(query_ref.shape[0] // tokens):
        rows = slice(part * tokens, (part + 1) * tokens)
        cached = slice(part * ROWS_AT_ONCE, (part + 1) * ROWS_AT_ONCE)
        queries = stacked_heads(query_ref[rows, :])
        keys = key_ref[cached].reshape(width, HD)
        values = value_ref[cached].reshape(width, HD)
        scores = lax.dot_general(queries, keys, NT, preferred_element_type=jnp.float32)
        first = (pl.program_id(0) * (query_ref.shape[0] // tokens) + part) * ROWS_AT_ONCE
        bias = length_bias(scalar_ref, length_ref, first, ROWS_AT_ONCE)
        scores = jnp.where(owner == holder, scores + bias, NEG_FILL)
        largest = jnp.max(scores, axis=1, keepdims=True)
        mixed = jnp.dot(
            weights_of(scores, largest), with_ones(values), preferred_element_type=jnp.float32
        )
        write_heads(mixed_ref, level_ref, rows, mixed, largest)


def sort_pair(scalar_ref, held_ref, swapped_ref, keys, values):
    @pl.when(scalar_ref[CORE] == 0)
    def _():
        keys[...] = held_ref[...].astype(keys.dtype)
        values[...] = swapped_ref[...].astype(values.dtype)

    @pl.when(scalar_ref[CORE] != 0)
    def _():
        keys[...] = swapped_ref[...].astype(keys.dtype)
        values[...] = held_ref[...].astype(values.dtype)


def recent_kernel(scalar_ref, own_ref, other_ref, held_ref, swapped_ref, mixed_ref, level_ref):
    row = lax.broadcasted_iota(jnp.int32, (TOK, TOK), 0)
    column = lax.broadcasted_iota(jnp.int32, (TOK, TOK), 1)
    is_prefill = scalar_ref[IS_PREFILL] != 0
    together = jnp.where(is_prefill, row // CH - column // CH, row % R - column % R) == 0
    allowed = together & (column <= row)
    lane = lax.broadcasted_iota(jnp.int32, (TOK, GQ), 1)

    held = held_ref[...].astype(jnp.float32)
    swapped = swapped_ref[...].astype(jnp.float32)
    first = scalar_ref[CORE] == 0
    keys = jnp.where(first, held, swapped).astype(jnp.bfloat16)
    values = with_ones(jnp.where(first, swapped, held).astype(jnp.bfloat16))
    levels = jnp.zeros((TOK, GQ), jnp.float32)
    for j in range(GQ):
        source = own_ref if j < GQ // 2 else other_ref
        part = slice(j % (GQ // 2) * HD, (j % (GQ // 2) + 1) * HD)
        scores = lax.dot_general(
            source[:, part], keys, NT, preferred_element_type=jnp.float32
        )
        scores = jnp.where(allowed, scores, NEG_FILL)
        largest = jnp.max(scores, axis=1, keepdims=True)
        mixed = jnp.dot(
            weights_of(scores, largest), values, preferred_element_type=jnp.float32
        )
        total = mixed[:, HD : HD + 1]
        mixed_ref[:, j * HD : (j + 1) * HD] = (mixed[:, :HD] / total).astype(mixed_ref.dtype)
        levels = jnp.where(lane == j, largest * HD**-0.5 + jnp.log(total), levels)
    level_ref[...] = levels


def merged(parts, levels):
    half = GQ // 2
    turned = jnp.concatenate([levels[1][:, half:], levels[1][:, :half]], axis=1)
    levels = [levels[0], turned, levels[2]]
    top = jnp.maximum(jnp.maximum(levels[0], levels[1]), levels[2])
    shares = [jnp.exp(level - top) for level in levels]
    total = shares[0] + shares[1] + shares[2]
    shares = [share / total for share in shares]
    heads = []
    for j in range(GQ):
        mixed = jnp.zeros((TOK, HD), jnp.float32)
        for part, share, place in zip(parts, shares, (j, (j + half) % GQ, j)):
            values = part[:, place * HD : (place + 1) * HD].astype(jnp.float32)
            mixed = mixed + values * share[:, j : j + 1]
        heads.append(mixed.astype(jnp.bfloat16))
    return jnp.concatenate(heads, axis=1)


def swapped_copies(scalar_ref, first, swapped_ref, held_ref, sems):
    copies = []
    for index in range(4):
        columns = pl.ds(pl.multiple_of(scalar_ref[PLACE + first + index] * SHARD, SHARD), SHARD)
        copies.append(
            pltpu.make_async_copy(
                swapped_ref.at[:, columns], held_ref.at[index], sems.at[index]
            )
        )
        copies[-1].start()
    return copies


def product(scalar_ref, chip, joined, copy, weight_ref, held_ref, index):
    column = 2 * scalar_ref[PLACE + chip] + scalar_ref[CORE]
    own = weight_ref[:, pl.ds(pl.multiple_of(column * SHARD, SHARD), SHARD)]
    copy.wait()
    weights = jnp.concatenate([own, held_ref[index]], axis=0)
    return jnp.dot(joined, weights, preferred_element_type=jnp.float32).astype(jnp.bfloat16)


def merge_out_kernel(
    scalar_ref,
    swapped_ref,
    weight_ref,
    own_ref,
    own_level,
    other_ref,
    other_level,
    recent_ref,
    recent_level,
    plus,
    minus,
    up,
    down,
    attention,
    held_ref,
    sems,
):
    copies = swapped_copies(scalar_ref, 0, swapped_ref, held_ref, sems)
    joined = merged(
        (own_ref, other_ref, recent_ref), (own_level[...], other_level[...], recent_level[...])
    )
    attention[...] = joined
    parts = [
        product(scalar_ref, index, joined, copies[index], weight_ref, held_ref, index)
        for index in range(4)
    ]
    plus[:TOK] = parts[0]
    minus[:TOK] = parts[1]
    plus[TOK:] = parts[2][:HALF]
    minus[TOK:] = parts[2][HALF:]
    up[...] = parts[3][:HALF]
    down[...] = parts[3][HALF:]


def out_kernel(scalar_ref, swapped_ref, weight_ref, attention, *refs):
    *out_refs, held_ref, sems = refs
    copies = swapped_copies(scalar_ref, 4, swapped_ref, held_ref, sems)
    joined = attention[...]
    for index, ref in enumerate(out_refs):
        ref[...] = product(
            scalar_ref, 4 + index, joined, copies[index], weight_ref, held_ref, index
        )


def total_of(*parts):
    total = parts[0].astype(jnp.float32)
    for part in parts[1:]:
        total = total + part.astype(jnp.float32)
    return total.astype(jnp.bfloat16)


def second_message_kernel(
    arrived_ref,
    next_ref,
    last_ref,
    partner_ref,
    from_last,
    from_next,
    up,
    down,
    plus,
    minus,
    partner,
):
    plus[:HALF] = total_of(next_ref[:HALF], from_last[TOK:], up[...])
    plus[HALF:] = next_ref[HALF:]
    minus[:HALF] = last_ref[:HALF]
    minus[HALF:] = total_of(last_ref[HALF:], from_next[TOK:], down[...])
    partner[...] = total_of(partner_ref[...], from_last[:TOK], from_next[:TOK])


def total_kernel(here_ref, from_last, from_next, from_partner, out_ref):
    out_ref[...] = total_of(here_ref[...], from_last[...], from_next[...], from_partner[...])


def join_kernel(
    scalar_ref, own_ref, partner_ref, last_ref, next_ref, plus, minus, up, down, near, sem
):
    own = pltpu.make_async_copy(own_ref, near.at[:TOK], sem)
    own.start()
    plus[:TOK] = partner_ref[...]
    plus[TOK:] = last_ref[:HALF]
    minus[:TOK] = partner_ref[...]
    minus[TOK:] = next_ref[HALF:]
    up[...] = last_ref[HALF:]
    down[...] = next_ref[:HALF]
    for index, ref in enumerate((last_ref, next_ref, partner_ref)):
        near[(index + 1) * TOK : (index + 2) * TOK] = ref[...]
    own.wait()


def sides_kernel(mark_ref, last_ref, next_ref, upper_ref, lower_ref, sides):
    sides[:TOK] = last_ref[:TOK]
    sides[TOK : 2 * TOK] = next_ref[:TOK]
    sides[2 * TOK : 2 * TOK + HALF] = last_ref[TOK:]
    sides[2 * TOK + HALF : 3 * TOK] = next_ref[TOK:]
    sides[3 * TOK : 3 * TOK + HALF] = upper_ref[...]
    sides[3 * TOK + HALF :] = lower_ref[...]


def projected_parts(scalar_ref, first, shards, query_weight, pair_weight):
    joined = jnp.concatenate(shards, axis=1)
    rows = [
        pl.ds(pl.multiple_of(scalar_ref[first + index], SHARD), SHARD)
        for index in range(len(shards))
    ]
    return [
        jnp.dot(
            joined,
            jnp.concatenate([weight[part, :] for part in rows], axis=0),
            preferred_element_type=jnp.float32,
        )
        for weight in (query_weight, pair_weight)
    ]


def four_shards(ref):
    return [ref[index * TOK : (index + 1) * TOK] for index in range(4)]


def near_kernel(scalar_ref, query_weight, pair_weight, near_ref, other_ref, query, pair, mark):
    mark[...] = jnp.zeros_like(mark)
    query[...], pair[...] = projected_parts(
        scalar_ref,
        NEAR_ROWS,
        four_shards(near_ref) + four_shards(other_ref),
        query_weight,
        pair_weight,
    )


def far_kernel(scalar_ref, query_weight, pair_weight, query_in, pair_in, far_ref, query, pair):
    sums = projected_parts(scalar_ref, FAR_ROWS, four_shards(far_ref), query_weight, pair_weight)
    query[...] = query_in[...] + sums[0]
    pair[...] = pair_in[...] + sums[1]


def last_kernel(
    scalar_ref,
    query_weight,
    pair_weight,
    query_in,
    pair_in,
    far_ref,
    cosine_ref,
    sine_ref,
    query_out,
    pair_out,
):
    sums = projected_parts(
        scalar_ref, FAR_ROWS + 4, four_shards(far_ref), query_weight, pair_weight
    )
    query = query_in[...] + sums[0]
    pair = pair_in[...] + sums[1]
    cosine = cosine_ref[...]
    sine = sine_ref[...]

    def rotated(values):
        return values * cosine + pltpu.roll(values, HD // 2, 1) * sine

    for head in range(query.shape[1] // HD):
        part = slice(head * HD, (head + 1) * HD)
        query_out[:, part] = rotated(query[:, part]).astype(jnp.bfloat16)
    is_key = scalar_ref[IS_KEY] != 0
    pair_out[...] = jnp.where(is_key, rotated(pair), pair).astype(jnp.bfloat16)


def blocks_kernel(scalar_ref, held_ref, swapped_ref, out_ref, keys, values):
    sliver = out_ref.shape[1]
    out_ref[...] = jnp.zeros_like(out_ref)

    @pl.when(scalar_ref[IS_PREFILL] != 0)
    def _():
        sort_pair(scalar_ref, held_ref, swapped_ref, keys, values)
        for block in range(TOK // BS):
            start = pl.multiple_of(scalar_ref[CORE] * sliver, sliver) + block * BS
            cell = scalar_ref[CELLS + block]
            out_ref[cell, :, :HD] = keys[pl.ds(start, sliver), :].astype(jnp.bfloat16)
            out_ref[cell, :, HD:] = values[pl.ds(start, sliver), :].astype(jnp.bfloat16)


def called(kernel, shapes, scalars, *arrays, streamed=(), scratch=(), flops=0, grant=12):
    whole = pl.BlockSpec(memory_space=pltpu.VMEM)
    specs = [pl.BlockSpec(memory_space=pl.ANY)] * len(streamed) + [whole] * len(arrays)
    arrays = tuple(streamed) + arrays
    if scalars is not None:
        specs = [pl.BlockSpec(memory_space=pltpu.SMEM)] + specs
        arrays = (scalars,) + arrays
    return pl.pallas_call(
        kernel,
        in_specs=specs,
        out_specs=tuple(whole for _ in shapes),
        out_shape=tuple(jax.ShapeDtypeStruct(shape, kind) for shape, kind in shapes),
        scratch_shapes=scratch,
        compiler_params=pltpu.CompilerParams(vmem_limit_bytes=grant * 2**20),
        cost_estimate=pl.CostEstimate(flops=flops, transcendentals=0, bytes_accessed=2**21),
    )(*arrays)


def outputs_of(kind):
    return (
        jax.ShapeDtypeStruct((TOK, GQ * HD), kind),
        jax.ShapeDtypeStruct((TOK, GQ), jnp.float32),
    )


def prefill_part(scalars, lengths, own, other, keys, values):
    chunks = RP * SPAN // PREFILL_CHUNK
    whole = pl.BlockSpec(memory_space=pltpu.VMEM)
    there = pl.BlockSpec(memory_space=pl.ANY)
    small = pl.BlockSpec(memory_space=pltpu.SMEM)
    return pl.pallas_call(
        prefill_kernel,
        in_specs=[small, small, whole, whole, there, there],
        out_specs=(whole, whole),
        out_shape=outputs_of(jnp.bfloat16),
        scratch_shapes=[
            pltpu.VMEM((R, SPAN, HD), jnp.bfloat16),
            pltpu.VMEM((R, SPAN, HD), jnp.bfloat16),
            pltpu.VMEM((chunks, PREFILL_CHUNK, GQ * CH), jnp.float32),
            pltpu.SemaphoreType.DMA((2, NPR * chunks)),
        ],
        compiler_params=pltpu.CompilerParams(vmem_limit_bytes=44 * 2**20),
    )(scalars, lengths, own, other, keys, values)


def decode_part(scalars, lengths, own, other, keys, values):
    def by_row(array):
        return array.reshape(STEPS, R, -1).transpose(1, 0, 2).reshape(TOK, -1)

    def by_step(array):
        return array.reshape(R, STEPS, -1).transpose(1, 0, 2).reshape(TOK, -1)

    rows = 8 * ROWS_AT_ONCE
    mixed, level = pl.pallas_call(
        decode_kernel,
        grid=(R // rows,),
        in_specs=[
            pl.BlockSpec(memory_space=pltpu.SMEM),
            pl.BlockSpec(memory_space=pltpu.SMEM),
            pl.BlockSpec((rows * STEPS, GQ * HD), lambda i: (i, 0)),
            pl.BlockSpec((rows, SPAN, HD), lambda i: (i, 0, 0)),
            pl.BlockSpec((rows, SPAN, HD), lambda i: (i, 0, 0)),
        ],
        out_specs=(
            pl.BlockSpec((rows * STEPS, GQ * HD), lambda i: (i, 0)),
            pl.BlockSpec((rows * STEPS, GQ), lambda i: (i, 0)),
        ),
        out_shape=outputs_of(jnp.bfloat16),
        compiler_params=pltpu.CompilerParams(vmem_limit_bytes=40 * 2**20),
    )(scalars, lengths, by_row(jnp.concatenate([own, other], axis=1)), keys, values)
    return by_step(mixed), by_step(level)


def cut_kernel(scalar_ref, weight_ref, out_ref, held_ref, in_sems, out_sems):
    fetches = []
    stores = []
    for chip in range(CHIPS):
        columns = pl.ds(pl.multiple_of((2 * chip + 1 - scalar_ref[CORE]) * SHARD, SHARD), SHARD)
        fetches.append(
            pltpu.make_async_copy(weight_ref.at[:, columns], held_ref.at[chip], in_sems.at[chip])
        )
        stores.append(
            pltpu.make_async_copy(
                held_ref.at[chip],
                out_ref.at[:, chip * SHARD : (chip + 1) * SHARD],
                out_sems.at[chip],
            )
        )
    for fetch in fetches:
        fetch.start()
    for fetch, store in zip(fetches, stores):
        fetch.wait()
        store.start()
    for store in stores:
        store.wait()


def cut_columns(scalars, out_weight):
    return pl.pallas_call(
        cut_kernel,
        in_specs=[
            pl.BlockSpec(memory_space=pltpu.SMEM),
            pl.BlockSpec(memory_space=pl.ANY),
        ],
        out_specs=pl.BlockSpec(memory_space=pl.ANY),
        out_shape=jax.ShapeDtypeStruct((out_weight.shape[0], CHIPS * SHARD), jnp.bfloat16),
        scratch_shapes=[
            pltpu.VMEM((CHIPS, out_weight.shape[0], SHARD), jnp.bfloat16),
            pltpu.SemaphoreType.DMA((CHIPS,)),
            pltpu.SemaphoreType.DMA((CHIPS,)),
        ],
        compiler_params=pltpu.CompilerParams(vmem_limit_bytes=12 * 2**20),
    )(scalars, out_weight)


def on_device(
    layer_input, query_weight, kv_weight, out_weight, cache_keys, cache_values, lengths, placement
):
    group_count = lax.axis_size("group")
    tp_rank = lax.axis_index("tp")
    group_rank = lax.axis_index("group")
    core = tp_rank % 2
    y = (tp_rank // 2) % 4
    x_hi = tp_rank // 8
    is_prefill = group_rank == 0
    tokens = layer_input[0]
    row_lengths = lengths[0]
    slot_count = 2 * (TOK // BS) // (group_count - 1)

    def rows_of(*owners):
        firsts = [tp_index(x_hi ^ flip, y + step, core) for flip, step in owners]
        return [first * SHARD for first in firsts] + [(first ^ 1) * SHARD for first in firsts]

    places = ((1, 1), (1, 3), (0, 2), (1, 2), (0, 1), (0, 3), (1, 0), (0, 0))
    single = (
        [core, is_prefill, tp_rank < KVH]
        + rows_of((0, 0), (0, 3), (0, 1), (1, 0))
        + rows_of((1, 3), (1, 1), (0, 2), (1, 2))
        + [(x_hi ^ flip) * 4 + (y + step) % 4 for flip, step in places]
    )
    picks = [group_rank >= 4, group_rank // 2 % 2 == 1, group_rank % 2 == 1]
    scalars = jnp.concatenate(
        [
            jnp.stack([jnp.asarray(one, jnp.int32) for one in single]),
            placement[:, 0] * slot_count + placement[:, 1],
        ]
    )
    prefix = jnp.sum(row_lengths.reshape(NPR, RP), axis=1)
    prompt_positions = (prefix[:, None] + jnp.arange(CH, dtype=jnp.int32)[None, :]).reshape(TOK)
    decode_step_positions = (
        row_lengths[None, :] + jnp.arange(STEPS, dtype=jnp.int32)[:, None]
    ).reshape(TOK)
    positions = jnp.where(is_prefill, prompt_positions, decode_step_positions)

    cut_out = cut_columns(scalars, out_weight)

    wide = ((TOK + HALF, SHARD), jnp.bfloat16)
    half = ((HALF, SHARD), jnp.bfloat16)
    shard = ((TOK, SHARD), jnp.bfloat16)
    four = ((4 * TOK, SHARD), jnp.bfloat16)
    weights = (query_weight, kv_weight)
    sums = (((TOK, query_weight.shape[1]), jnp.float32), ((TOK, kv_weight.shape[1]), jnp.float32))
    partner_tokens = moved(tokens, 1, 0, 0)
    last_tokens, next_tokens = moved(tokens, 0, 1, 0), moved(tokens, 0, 3, 0)
    scalars, picks, positions = lax.optimization_barrier((scalars, picks, positions))
    cosine, sine = turns(positions)
    plus, minus, up, down, near = called(
        join_kernel,
        (wide, wide, half, half, four),
        scalars,
        partner_tokens,
        last_tokens,
        next_tokens,
        streamed=(tokens,),
        scratch=(pltpu.SemaphoreType.DMA(()),),
        flops=LONG,
    )
    from_last, from_next = moved(plus, 0, 1, 0), moved(minus, 0, 3, 0)
    far_upper, far_lower = moved(down, 1, 3, 0), moved(up, 1, 1, 0)
    scalars, cut_out = lax.optimization_barrier((scalars, cut_out))
    *part, mark = called(
        near_kernel,
        sums + (((8, HD), jnp.float32),),
        scalars,
        *weights,
        near,
        core_swap(near),
        flops=2 * TOK * 8 * SHARD * 3 * HD,
    )
    (sides,) = called(
        sides_kernel,
        (four,),
        None,
        from_last,
        from_next,
        far_upper,
        far_lower,
        streamed=(mark,),
    )
    other_sides = core_swap(sides)
    part = called(
        far_kernel,
        sums,
        scalars,
        *weights,
        *part,
        sides,
        flops=2 * TOK * 4 * SHARD * 3 * HD,
    )
    query_local, pair_local = called(
        last_kernel,
        tuple((shape, jnp.bfloat16) for shape, _ in sums),
        scalars,
        *weights,
        *part,
        other_sides,
        cosine,
        sine,
        flops=2 * TOK * 4 * SHARD * 3 * HD,
    )
    pair_local, cut_out = lax.optimization_barrier((pair_local, cut_out))
    query_other = core_swap(query_local)
    pair_held = lax.ppermute(
        pair_local, "tp", [(t, 2 * t if t < KVH else 2 * (t - KVH) + 1) for t in range(2 * KVH)]
    )
    swapped_out = core_swap(cut_out)
    cached = lax.cond(
        is_prefill,
        prefill_part,
        decode_part,
        scalars,
        row_lengths,
        query_local,
        query_other,
        cache_keys[0],
        cache_values[0],
    )
    cached, pair_held = lax.optimization_barrier((cached, pair_held))
    pair_other = core_swap(pair_held)
    other_cached = (core_swap(cached[0]), core_swap(cached[1]))
    recent = called(
        recent_kernel,
        (((TOK, GQ * HD), jnp.bfloat16), ((TOK, GQ), jnp.float32)),
        scalars,
        query_local,
        query_other,
        pair_held,
        pair_other,
        flops=LONG,
    )

    product_scratch = (
        pltpu.VMEM((4, out_weight.shape[0], SHARD), jnp.bfloat16),
        pltpu.SemaphoreType.DMA((4,)),
    )
    plus, minus, up, down, attention = called(
        merge_out_kernel,
        (wide, wide, half, half, ((TOK, GQ * HD), jnp.bfloat16)),
        scalars,
        out_weight,
        *cached,
        *other_cached,
        *recent,
        streamed=(swapped_out,),
        scratch=product_scratch,
        flops=2 * TOK * 4 * SHARD * GQ * HD,
    )
    next_part, last_part, partner_part, here_part = called(
        out_kernel,
        (shard,) * 4,
        scalars,
        out_weight,
        attention,
        streamed=(swapped_out,),
        scratch=product_scratch,
        flops=2 * TOK * 4 * SHARD * GQ * HD,
    )
    from_last, from_next = moved(plus, 0, 1, 0), moved(minus, 0, 3, 0)
    up, down = moved(up, 1, 1, 0), moved(down, 1, 3, 0)

    _, late_scalars = lax.optimization_barrier((attention, scalars))
    (blocks,) = called(
        blocks_kernel,
        (((group_count * slot_count, BS // 2, 2 * HD), jnp.bfloat16),),
        late_scalars,
        pair_held,
        pair_other,
        scratch=(pltpu.VMEM((TOK, HD), jnp.float32),) * 2,
    )
    blocks = blocks.reshape(group_count, slot_count, BS // 2, 2 * HD)
    arrived = lax.ppermute(blocks[4:], "group", [(0, 4)])

    plus, minus, partner = called(
        second_message_kernel,
        (shard, shard, shard),
        None,
        next_part,
        last_part,
        partner_part,
        from_last,
        from_next,
        up,
        down,
        streamed=(arrived,),
    )
    from_last, from_next = moved(plus, 0, 1, 0), moved(minus, 0, 3, 0)
    from_partner = moved(partner, 1, 0, 0)

    blocks = jnp.where(picks[0], arrived, blocks[:4])
    sent = lax.ppermute(blocks[2:], "group", [(0, 2), (4, 6)])
    blocks = jnp.where(picks[1], sent, blocks[:2])
    sent = lax.ppermute(blocks[1:], "group", [(0, 1), (2, 3), (4, 5), (6, 7)])
    incoming = jnp.where(picks[2], sent, blocks[:1])
    (projected,) = called(
        total_kernel, (shard,), None, here_part, from_last, from_next, from_partner
    )
    return (projected[None], incoming)


def solution(mesh):
    in_specs = (
        P("group", None, "tp"),
        P(None, "tp"),
        P(None, "tp"),
        P("tp", None),
        P("group", None, "tp", None),
        P("group", None, "tp", None),
        P("group", None),
        P(),
    )
    out_specs = (P("group", None, "tp"), P("group", None, "tp", None))
    return jax.shard_map(
        on_device, mesh=mesh, in_specs=in_specs, out_specs=out_specs, check_vma=False
    )
```

```python
import jax
import jax.numpy as jnp
from jax import lax
from jax.experimental import pallas as pl
from jax.experimental.pallas import tpu as pltpu
from jax.sharding import PartitionSpec as P

HD = 128
KVH = 8
STEPS = 4
NPR = 2
BS = 16
R = 64
GQ = 4
TOK = 256
CH = 128
RP = 32


NEG_FILL = -1e30


def tp_index(x_hi, y, core):
    return x_hi * 8 + (y % 4) * 2 + core


def moved(shard, x_flip, y_step, core_flip):
    pairs = []
    for x_hi in range(2):
        for y in range(4):
            for core in range(2):
                pairs.append(
                    (
                        tp_index(x_hi, y, core),
                        tp_index(x_hi ^ x_flip, y + y_step, core ^ core_flip),
                    )
                )
    return lax.ppermute(shard, "tp", pairs)


def core_swap(shard):
    return moved(shard, 0, 0, 1)


def turns(positions):
    midpoint = HD // 2
    frequency = jnp.exp(
        -jnp.log(500000.0) * jnp.arange(midpoint, dtype=jnp.float32) * 2.0 / HD
    )
    angles = positions.astype(jnp.float32)[:, None] * frequency[None, :]
    cosine = jnp.cos(angles)
    sine = jnp.sin(angles)
    return (
        jnp.concatenate([cosine, cosine], axis=1),
        jnp.concatenate([-sine, sine], axis=1),
    )


SPAN = 256
CHIPS = 8
SHARD = 512
HALF = TOK // 2
PREFILL_CHUNK = 8192
ROWS_AT_ONCE = 4
LOG2_E = 1.4426950408889634
NT = (((1,), (1,)), ((), ()))
LONG = 6 * 10**9

CORE, IS_PREFILL, IS_KEY, NEAR_ROWS, FAR_ROWS, PLACE, CELLS = 0, 1, 2, 3, 11, 19, 27


def stacked_heads(*parts):
    return jnp.concatenate(
        [part[:, j * HD : (j + 1) * HD] for part in parts for j in range(part.shape[1] // HD)],
        axis=0,
    )


def length_bias(scalar_ref, length_ref, first, count):
    place = lax.broadcasted_iota(jnp.int32, (1, SPAN), 1) + scalar_ref[CORE] * SPAN
    return jnp.concatenate(
        [jnp.where(place < length_ref[first + row], 0.0, NEG_FILL) for row in range(count)],
        axis=1,
    )


def weights_of(scores, largest):
    return jnp.exp2((scores - largest) * (HD**-0.5 * LOG2_E)).astype(jnp.bfloat16)


def with_ones(values):
    return jnp.concatenate([values, jnp.ones_like(values)], axis=1)


def write_heads(mixed_ref, level_ref, rows, mixed, largest):
    count = mixed.shape[0] // GQ
    total = mixed[:, HD : HD + 1]
    normal = (mixed[:, :HD] / total).astype(jnp.bfloat16)
    level = largest * HD**-0.5 + jnp.log(total)
    lane = lax.broadcasted_iota(jnp.int32, (count, GQ), 1)
    levels = jnp.zeros((count, GQ), jnp.float32)
    for j in range(GQ):
        part = slice(j * count, (j + 1) * count)
        mixed_ref[rows, j * HD : (j + 1) * HD] = normal[part]
        levels = jnp.where(lane == j, level[part], levels)
    level_ref[rows, :] = levels


def prefill_kernel(
    scalar_ref,
    length_ref,
    own_ref,
    other_ref,
    key_ref,
    value_ref,
    mixed_ref,
    level_ref,
    keys,
    values,
    score_ref,
    sems,
):
    rows = PREFILL_CHUNK // SPAN
    chunks = RP // rows

    def fetches(prompt, step):
        part = pl.ds(prompt * RP + step * rows, rows)
        index = prompt * chunks + step
        return (
            pltpu.make_async_copy(key_ref.at[part], keys.at[part], sems.at[0, index]),
            pltpu.make_async_copy(value_ref.at[part], values.at[part], sems.at[1, index]),
        )

    for prompt in range(NPR):
        for kind in range(2):
            for step in range(chunks):
                fetches(prompt, step)[kind].start()

    def one_prompt(prompt, carry):
        tokens = pl.ds(pl.multiple_of(prompt * CH, CH), CH)
        queries = stacked_heads(own_ref[tokens, :], other_ref[tokens, :])

        def score_step(step, peak):
            fetches(prompt, step)[0].wait()
            part = keys[pl.ds(prompt * RP + step * rows, rows)].reshape(PREFILL_CHUNK, HD)
            scores = lax.dot_general(queries, part, NT, preferred_element_type=jnp.float32)
            scores = scores + length_bias(scalar_ref, length_ref, prompt * RP + step * rows, rows)
            score_ref[step] = scores
            for lanes in range(PREFILL_CHUNK // HD):
                peak = jnp.maximum(peak, scores[:, lanes * HD : (lanes + 1) * HD])
            return peak

        peak = lax.fori_loop(
            0, chunks, score_step, jnp.full((GQ * CH, HD), NEG_FILL, jnp.float32)
        )
        largest = jnp.max(peak, axis=1, keepdims=True)
        level = jnp.broadcast_to(largest, (GQ * CH, HD))

        def mix_step(step, mixed):
            fetches(prompt, step)[1].wait()
            weights = jnp.concatenate(
                [
                    weights_of(score_ref[step, :, lanes * HD : (lanes + 1) * HD], level)
                    for lanes in range(PREFILL_CHUNK // HD)
                ],
                axis=1,
            )
            part = values[pl.ds(prompt * RP + step * rows, rows)].reshape(PREFILL_CHUNK, HD)
            return mixed + jnp.dot(weights, with_ones(part), preferred_element_type=jnp.float32)

        mixed = lax.fori_loop(0, chunks, mix_step, jnp.zeros((GQ * CH, 2 * HD), jnp.float32))
        write_heads(mixed_ref, level_ref, tokens, mixed, largest)
        return carry

    lax.fori_loop(0, NPR, one_prompt, 0)


def decode_kernel(
    scalar_ref, length_ref, query_ref, key_ref, value_ref, mixed_ref, level_ref
):
    width = ROWS_AT_ONCE * SPAN
    tokens = ROWS_AT_ONCE * STEPS
    owner = lax.broadcasted_iota(jnp.int32, (GQ * tokens, width), 0) % tokens // STEPS
    holder = lax.broadcasted_iota(jnp.int32, (GQ * tokens, width), 1) // SPAN
    for part in range(query_ref.shape[0] // tokens):
        rows = slice(part * tokens, (part + 1) * tokens)
        cached = slice(part * ROWS_AT_ONCE, (part + 1) * ROWS_AT_ONCE)
        queries = stacked_heads(query_ref[rows, :])
        keys = key_ref[cached].reshape(width, HD)
        values = value_ref[cached].reshape(width, HD)
        scores = lax.dot_general(queries, keys, NT, preferred_element_type=jnp.float32)
        first = (pl.program_id(0) * (query_ref.shape[0] // tokens) + part) * ROWS_AT_ONCE
        bias = length_bias(scalar_ref, length_ref, first, ROWS_AT_ONCE)
        scores = jnp.where(owner == holder, scores + bias, NEG_FILL)
        largest = jnp.max(scores, axis=1, keepdims=True)
        mixed = jnp.dot(
            weights_of(scores, largest), with_ones(values), preferred_element_type=jnp.float32
        )
        write_heads(mixed_ref, level_ref, rows, mixed, largest)


def sort_pair(scalar_ref, held_ref, swapped_ref, keys, values):
    @pl.when(scalar_ref[CORE] == 0)
    def _():
        keys[...] = held_ref[...].astype(keys.dtype)
        values[...] = swapped_ref[...].astype(values.dtype)

    @pl.when(scalar_ref[CORE] != 0)
    def _():
        keys[...] = swapped_ref[...].astype(keys.dtype)
        values[...] = held_ref[...].astype(values.dtype)


def recent_kernel(scalar_ref, own_ref, other_ref, held_ref, swapped_ref, mixed_ref, level_ref):
    row = lax.broadcasted_iota(jnp.int32, (TOK, TOK), 0)
    column = lax.broadcasted_iota(jnp.int32, (TOK, TOK), 1)
    is_prefill = scalar_ref[IS_PREFILL] != 0
    together = jnp.where(is_prefill, row // CH - column // CH, row % R - column % R) == 0
    allowed = together & (column <= row)
    lane = lax.broadcasted_iota(jnp.int32, (TOK, GQ), 1)

    held = held_ref[...].astype(jnp.float32)
    swapped = swapped_ref[...].astype(jnp.float32)
    first = scalar_ref[CORE] == 0
    keys = jnp.where(first, held, swapped).astype(jnp.bfloat16)
    values = with_ones(jnp.where(first, swapped, held).astype(jnp.bfloat16))
    levels = jnp.zeros((TOK, GQ), jnp.float32)
    for j in range(GQ):
        source = own_ref if j < GQ // 2 else other_ref
        part = slice(j % (GQ // 2) * HD, (j % (GQ // 2) + 1) * HD)
        scores = lax.dot_general(
            source[:, part], keys, NT, preferred_element_type=jnp.float32
        )
        scores = jnp.where(allowed, scores, NEG_FILL)
        largest = jnp.max(scores, axis=1, keepdims=True)
        mixed = jnp.dot(
            weights_of(scores, largest), values, preferred_element_type=jnp.float32
        )
        total = mixed[:, HD : HD + 1]
        mixed_ref[:, j * HD : (j + 1) * HD] = (mixed[:, :HD] / total).astype(mixed_ref.dtype)
        levels = jnp.where(lane == j, largest * HD**-0.5 + jnp.log(total), levels)
    level_ref[...] = levels


def merged(parts, levels):
    half = GQ // 2
    turned = jnp.concatenate([levels[1][:, half:], levels[1][:, :half]], axis=1)
    levels = [levels[0], turned, levels[2]]
    top = jnp.maximum(jnp.maximum(levels[0], levels[1]), levels[2])
    shares = [jnp.exp(level - top) for level in levels]
    total = shares[0] + shares[1] + shares[2]
    shares = [share / total for share in shares]
    heads = []
    for j in range(GQ):
        mixed = jnp.zeros((TOK, HD), jnp.float32)
        for part, share, place in zip(parts, shares, (j, (j + half) % GQ, j)):
            values = part[:, place * HD : (place + 1) * HD].astype(jnp.float32)
            mixed = mixed + values * share[:, j : j + 1]
        heads.append(mixed.astype(jnp.bfloat16))
    return jnp.concatenate(heads, axis=1)


def swapped_copies(scalar_ref, first, swapped_ref, held_ref, sems):
    copies = []
    for index in range(4):
        columns = pl.ds(pl.multiple_of(scalar_ref[PLACE + first + index] * SHARD, SHARD), SHARD)
        copies.append(
            pltpu.make_async_copy(
                swapped_ref.at[:, columns], held_ref.at[index], sems.at[index]
            )
        )
        copies[-1].start()
    return copies


def product(scalar_ref, chip, joined, copy, weight_ref, held_ref, index):
    column = 2 * scalar_ref[PLACE + chip] + scalar_ref[CORE]
    own = weight_ref[:, pl.ds(pl.multiple_of(column * SHARD, SHARD), SHARD)]
    copy.wait()
    weights = jnp.concatenate([own, held_ref[index]], axis=0)
    return jnp.dot(joined, weights, preferred_element_type=jnp.float32).astype(jnp.bfloat16)


def merge_out_kernel(
    scalar_ref,
    swapped_ref,
    weight_ref,
    own_ref,
    own_level,
    other_ref,
    other_level,
    recent_ref,
    recent_level,
    plus,
    minus,
    up,
    down,
    attention,
    held_ref,
    sems,
):
    copies = swapped_copies(scalar_ref, 0, swapped_ref, held_ref, sems)
    joined = merged(
        (own_ref, other_ref, recent_ref), (own_level[...], other_level[...], recent_level[...])
    )
    attention[...] = joined
    parts = [
        product(scalar_ref, index, joined, copies[index], weight_ref, held_ref, index)
        for index in range(4)
    ]
    plus[:TOK] = parts[0]
    minus[:TOK] = parts[1]
    plus[TOK:] = parts[2][:HALF]
    minus[TOK:] = parts[2][HALF:]
    up[...] = parts[3][:HALF]
    down[...] = parts[3][HALF:]


def out_kernel(scalar_ref, swapped_ref, weight_ref, attention, *refs):
    *out_refs, held_ref, sems = refs
    copies = swapped_copies(scalar_ref, 4, swapped_ref, held_ref, sems)
    joined = attention[...]
    for index, ref in enumerate(out_refs):
        ref[...] = product(
            scalar_ref, 4 + index, joined, copies[index], weight_ref, held_ref, index
        )


def total_of(*parts):
    total = parts[0].astype(jnp.float32)
    for part in parts[1:]:
        total = total + part.astype(jnp.float32)
    return total.astype(jnp.bfloat16)


def second_message_kernel(
    arrived_ref,
    next_ref,
    last_ref,
    partner_ref,
    from_last,
    from_next,
    up,
    down,
    plus,
    minus,
    partner,
):
    plus[:HALF] = total_of(next_ref[:HALF], from_last[TOK:], up[...])
    plus[HALF:] = next_ref[HALF:]
    minus[:HALF] = last_ref[:HALF]
    minus[HALF:] = total_of(last_ref[HALF:], from_next[TOK:], down[...])
    partner[...] = total_of(partner_ref[...], from_last[:TOK], from_next[:TOK])


def total_kernel(here_ref, from_last, from_next, from_partner, out_ref):
    out_ref[...] = total_of(here_ref[...], from_last[...], from_next[...], from_partner[...])


def join_kernel(
    scalar_ref, own_ref, partner_ref, last_ref, next_ref, plus, minus, up, down, near, sem
):
    own = pltpu.make_async_copy(own_ref, near.at[:TOK], sem)
    own.start()
    plus[:TOK] = partner_ref[...]
    plus[TOK:] = last_ref[:HALF]
    minus[:TOK] = partner_ref[...]
    minus[TOK:] = next_ref[HALF:]
    up[...] = last_ref[HALF:]
    down[...] = next_ref[:HALF]
    for index, ref in enumerate((last_ref, next_ref, partner_ref)):
        near[(index + 1) * TOK : (index + 2) * TOK] = ref[...]
    own.wait()


def sides_kernel(mark_ref, last_ref, next_ref, upper_ref, lower_ref, sides):
    sides[:TOK] = last_ref[:TOK]
    sides[TOK : 2 * TOK] = next_ref[:TOK]
    sides[2 * TOK : 2 * TOK + HALF] = last_ref[TOK:]
    sides[2 * TOK + HALF : 3 * TOK] = next_ref[TOK:]
    sides[3 * TOK : 3 * TOK + HALF] = upper_ref[...]
    sides[3 * TOK + HALF :] = lower_ref[...]


def projected_parts(scalar_ref, first, shards, query_weight, pair_weight):
    joined = jnp.concatenate(shards, axis=1)
    rows = [
        pl.ds(pl.multiple_of(scalar_ref[first + index], SHARD), SHARD)
        for index in range(len(shards))
    ]
    return [
        jnp.dot(
            joined,
            jnp.concatenate([weight[part, :] for part in rows], axis=0),
            preferred_element_type=jnp.float32,
        )
        for weight in (query_weight, pair_weight)
    ]


def four_shards(ref):
    return [ref[index * TOK : (index + 1) * TOK] for index in range(4)]


def near_kernel(scalar_ref, query_weight, pair_weight, near_ref, other_ref, query, pair, mark):
    mark[...] = jnp.zeros_like(mark)
    query[...], pair[...] = projected_parts(
        scalar_ref,
        NEAR_ROWS,
        four_shards(near_ref) + four_shards(other_ref),
        query_weight,
        pair_weight,
    )


def far_kernel(scalar_ref, query_weight, pair_weight, query_in, pair_in, far_ref, query, pair):
    sums = projected_parts(scalar_ref, FAR_ROWS, four_shards(far_ref), query_weight, pair_weight)
    query[...] = query_in[...] + sums[0]
    pair[...] = pair_in[...] + sums[1]


def last_kernel(
    scalar_ref,
    query_weight,
    pair_weight,
    query_in,
    pair_in,
    far_ref,
    cosine_ref,
    sine_ref,
    query_out,
    pair_out,
):
    sums = projected_parts(
        scalar_ref, FAR_ROWS + 4, four_shards(far_ref), query_weight, pair_weight
    )
    query = query_in[...] + sums[0]
    pair = pair_in[...] + sums[1]
    cosine = cosine_ref[...]
    sine = sine_ref[...]

    def rotated(values):
        return values * cosine + pltpu.roll(values, HD // 2, 1) * sine

    for head in range(query.shape[1] // HD):
        part = slice(head * HD, (head + 1) * HD)
        query_out[:, part] = rotated(query[:, part]).astype(jnp.bfloat16)
    is_key = scalar_ref[IS_KEY] != 0
    pair_out[...] = jnp.where(is_key, rotated(pair), pair).astype(jnp.bfloat16)


def blocks_kernel(scalar_ref, held_ref, swapped_ref, out_ref, keys, values):
    sliver = out_ref.shape[1]
    out_ref[...] = jnp.zeros_like(out_ref)

    @pl.when(scalar_ref[IS_PREFILL] != 0)
    def _():
        sort_pair(scalar_ref, held_ref, swapped_ref, keys, values)
        for block in range(TOK // BS):
            start = pl.multiple_of(scalar_ref[CORE] * sliver, sliver) + block * BS
            cell = scalar_ref[CELLS + block]
            out_ref[cell, :, :HD] = keys[pl.ds(start, sliver), :].astype(jnp.bfloat16)
            out_ref[cell, :, HD:] = values[pl.ds(start, sliver), :].astype(jnp.bfloat16)


def called(kernel, shapes, scalars, *arrays, streamed=(), scratch=(), flops=0, grant=12):
    whole = pl.BlockSpec(memory_space=pltpu.VMEM)
    specs = [pl.BlockSpec(memory_space=pl.ANY)] * len(streamed) + [whole] * len(arrays)
    arrays = tuple(streamed) + arrays
    if scalars is not None:
        specs = [pl.BlockSpec(memory_space=pltpu.SMEM)] + specs
        arrays = (scalars,) + arrays
    return pl.pallas_call(
        kernel,
        in_specs=specs,
        out_specs=tuple(whole for _ in shapes),
        out_shape=tuple(jax.ShapeDtypeStruct(shape, kind) for shape, kind in shapes),
        scratch_shapes=scratch,
        compiler_params=pltpu.CompilerParams(vmem_limit_bytes=grant * 2**20),
        cost_estimate=pl.CostEstimate(flops=flops, transcendentals=0, bytes_accessed=2**21),
    )(*arrays)


def outputs_of(kind):
    return (
        jax.ShapeDtypeStruct((TOK, GQ * HD), kind),
        jax.ShapeDtypeStruct((TOK, GQ), jnp.float32),
    )


def prefill_part(scalars, lengths, own, other, keys, values):
    chunks = RP * SPAN // PREFILL_CHUNK
    whole = pl.BlockSpec(memory_space=pltpu.VMEM)
    there = pl.BlockSpec(memory_space=pl.ANY)
    small = pl.BlockSpec(memory_space=pltpu.SMEM)
    return pl.pallas_call(
        prefill_kernel,
        in_specs=[small, small, whole, whole, there, there],
        out_specs=(whole, whole),
        out_shape=outputs_of(jnp.bfloat16),
        scratch_shapes=[
            pltpu.VMEM((R, SPAN, HD), jnp.bfloat16),
            pltpu.VMEM((R, SPAN, HD), jnp.bfloat16),
            pltpu.VMEM((chunks, GQ * CH, PREFILL_CHUNK), jnp.float32),
            pltpu.SemaphoreType.DMA((2, NPR * chunks)),
        ],
        compiler_params=pltpu.CompilerParams(vmem_limit_bytes=58 * 2**20),
    )(scalars, lengths, own, other, keys, values)


def decode_part(scalars, lengths, own, other, keys, values):
    def by_row(array):
        return array.reshape(STEPS, R, -1).transpose(1, 0, 2).reshape(TOK, -1)

    def by_step(array):
        return array.reshape(R, STEPS, -1).transpose(1, 0, 2).reshape(TOK, -1)

    rows = 8 * ROWS_AT_ONCE
    mixed, level = pl.pallas_call(
        decode_kernel,
        grid=(R // rows,),
        in_specs=[
            pl.BlockSpec(memory_space=pltpu.SMEM),
            pl.BlockSpec(memory_space=pltpu.SMEM),
            pl.BlockSpec((rows * STEPS, GQ * HD), lambda i: (i, 0)),
            pl.BlockSpec((rows, SPAN, HD), lambda i: (i, 0, 0)),
            pl.BlockSpec((rows, SPAN, HD), lambda i: (i, 0, 0)),
        ],
        out_specs=(
            pl.BlockSpec((rows * STEPS, GQ * HD), lambda i: (i, 0)),
            pl.BlockSpec((rows * STEPS, GQ), lambda i: (i, 0)),
        ),
        out_shape=outputs_of(jnp.bfloat16),
        compiler_params=pltpu.CompilerParams(vmem_limit_bytes=40 * 2**20),
    )(scalars, lengths, by_row(jnp.concatenate([own, other], axis=1)), keys, values)
    return by_step(mixed), by_step(level)


def cut_kernel(scalar_ref, weight_ref, out_ref, held_ref, in_sems, out_sems):
    fetches = []
    stores = []
    for chip in range(CHIPS):
        columns = pl.ds(pl.multiple_of((2 * chip + 1 - scalar_ref[CORE]) * SHARD, SHARD), SHARD)
        fetches.append(
            pltpu.make_async_copy(weight_ref.at[:, columns], held_ref.at[chip], in_sems.at[chip])
        )
        stores.append(
            pltpu.make_async_copy(
                held_ref.at[chip],
                out_ref.at[:, chip * SHARD : (chip + 1) * SHARD],
                out_sems.at[chip],
            )
        )
    for fetch in fetches:
        fetch.start()
    for fetch, store in zip(fetches, stores):
        fetch.wait()
        store.start()
    for store in stores:
        store.wait()


def cut_columns(scalars, out_weight):
    return pl.pallas_call(
        cut_kernel,
        in_specs=[
            pl.BlockSpec(memory_space=pltpu.SMEM),
            pl.BlockSpec(memory_space=pl.ANY),
        ],
        out_specs=pl.BlockSpec(memory_space=pl.ANY),
        out_shape=jax.ShapeDtypeStruct((out_weight.shape[0], CHIPS * SHARD), jnp.bfloat16),
        scratch_shapes=[
            pltpu.VMEM((CHIPS, out_weight.shape[0], SHARD), jnp.bfloat16),
            pltpu.SemaphoreType.DMA((CHIPS,)),
            pltpu.SemaphoreType.DMA((CHIPS,)),
        ],
        compiler_params=pltpu.CompilerParams(vmem_limit_bytes=12 * 2**20),
    )(scalars, out_weight)


def on_device(
    layer_input, query_weight, kv_weight, out_weight, cache_keys, cache_values, lengths, placement
):
    group_count = lax.axis_size("group")
    tp_rank = lax.axis_index("tp")
    group_rank = lax.axis_index("group")
    core = tp_rank % 2
    y = (tp_rank // 2) % 4
    x_hi = tp_rank // 8
    is_prefill = group_rank == 0
    tokens = layer_input[0]
    row_lengths = lengths[0]
    slot_count = 2 * (TOK // BS) // (group_count - 1)

    def rows_of(*owners):
        firsts = [tp_index(x_hi ^ flip, y + step, core) for flip, step in owners]
        return [first * SHARD for first in firsts] + [(first ^ 1) * SHARD for first in firsts]

    places = ((1, 1), (1, 3), (0, 2), (1, 2), (0, 1), (0, 3), (1, 0), (0, 0))
    single = (
        [core, is_prefill, tp_rank < KVH]
        + rows_of((0, 0), (0, 3), (0, 1), (1, 0))
        + rows_of((1, 3), (1, 1), (0, 2), (1, 2))
        + [(x_hi ^ flip) * 4 + (y + step) % 4 for flip, step in places]
    )
    picks = [group_rank >= 4, group_rank // 2 % 2 == 1, group_rank % 2 == 1]
    scalars = jnp.concatenate(
        [
            jnp.stack([jnp.asarray(one, jnp.int32) for one in single]),
            placement[:, 0] * slot_count + placement[:, 1],
        ]
    )
    prefix = jnp.sum(row_lengths.reshape(NPR, RP), axis=1)
    prompt_positions = (prefix[:, None] + jnp.arange(CH, dtype=jnp.int32)[None, :]).reshape(TOK)
    decode_step_positions = (
        row_lengths[None, :] + jnp.arange(STEPS, dtype=jnp.int32)[:, None]
    ).reshape(TOK)
    positions = jnp.where(is_prefill, prompt_positions, decode_step_positions)

    cut_out = cut_columns(scalars, out_weight)

    wide = ((TOK + HALF, SHARD), jnp.bfloat16)
    half = ((HALF, SHARD), jnp.bfloat16)
    shard = ((TOK, SHARD), jnp.bfloat16)
    four = ((4 * TOK, SHARD), jnp.bfloat16)
    weights = (query_weight, kv_weight)
    sums = (((TOK, query_weight.shape[1]), jnp.float32), ((TOK, kv_weight.shape[1]), jnp.float32))
    partner_tokens = moved(tokens, 1, 0, 0)
    last_tokens, next_tokens = moved(tokens, 0, 1, 0), moved(tokens, 0, 3, 0)
    scalars, picks, positions = lax.optimization_barrier((scalars, picks, positions))
    cosine, sine = turns(positions)
    plus, minus, up, down, near = called(
        join_kernel,
        (wide, wide, half, half, four),
        scalars,
        partner_tokens,
        last_tokens,
        next_tokens,
        streamed=(tokens,),
        scratch=(pltpu.SemaphoreType.DMA(()),),
        flops=LONG,
    )
    from_last, from_next = moved(plus, 0, 1, 0), moved(minus, 0, 3, 0)
    far_upper, far_lower = moved(down, 1, 3, 0), moved(up, 1, 1, 0)
    scalars, cut_out = lax.optimization_barrier((scalars, cut_out))
    *part, mark = called(
        near_kernel,
        sums + (((8, HD), jnp.float32),),
        scalars,
        *weights,
        near,
        core_swap(near),
        flops=2 * TOK * 8 * SHARD * 3 * HD,
    )
    (sides,) = called(
        sides_kernel,
        (four,),
        None,
        from_last,
        from_next,
        far_upper,
        far_lower,
        streamed=(mark,),
    )
    other_sides = core_swap(sides)
    part = called(
        far_kernel,
        sums,
        scalars,
        *weights,
        *part,
        sides,
        flops=2 * TOK * 4 * SHARD * 3 * HD,
    )
    query_local, pair_local = called(
        last_kernel,
        tuple((shape, jnp.bfloat16) for shape, _ in sums),
        scalars,
        *weights,
        *part,
        other_sides,
        cosine,
        sine,
        flops=2 * TOK * 4 * SHARD * 3 * HD,
    )
    pair_local, cut_out = lax.optimization_barrier((pair_local, cut_out))
    query_other = core_swap(query_local)
    pair_held = lax.ppermute(
        pair_local, "tp", [(t, 2 * t if t < KVH else 2 * (t - KVH) + 1) for t in range(2 * KVH)]
    )
    swapped_out = core_swap(cut_out)
    cached = lax.cond(
        is_prefill,
        prefill_part,
        decode_part,
        scalars,
        row_lengths,
        query_local,
        query_other,
        cache_keys[0],
        cache_values[0],
    )
    cached, pair_held = lax.optimization_barrier((cached, pair_held))
    pair_other = core_swap(pair_held)
    other_cached = (core_swap(cached[0]), core_swap(cached[1]))
    recent = called(
        recent_kernel,
        (((TOK, GQ * HD), jnp.bfloat16), ((TOK, GQ), jnp.float32)),
        scalars,
        query_local,
        query_other,
        pair_held,
        pair_other,
        flops=LONG,
    )

    product_scratch = (
        pltpu.VMEM((4, out_weight.shape[0], SHARD), jnp.bfloat16),
        pltpu.SemaphoreType.DMA((4,)),
    )
    plus, minus, up, down, attention = called(
        merge_out_kernel,
        (wide, wide, half, half, ((TOK, GQ * HD), jnp.bfloat16)),
        scalars,
        out_weight,
        *cached,
        *other_cached,
        *recent,
        streamed=(swapped_out,),
        scratch=product_scratch,
        flops=2 * TOK * 4 * SHARD * GQ * HD,
    )
    next_part, last_part, partner_part, here_part = called(
        out_kernel,
        (shard,) * 4,
        scalars,
        out_weight,
        attention,
        streamed=(swapped_out,),
        scratch=product_scratch,
        flops=2 * TOK * 4 * SHARD * GQ * HD,
    )
    from_last, from_next = moved(plus, 0, 1, 0), moved(minus, 0, 3, 0)
    up, down = moved(up, 1, 1, 0), moved(down, 1, 3, 0)

    _, late_scalars = lax.optimization_barrier((attention, scalars))
    (blocks,) = called(
        blocks_kernel,
        (((group_count * slot_count, BS // 2, 2 * HD), jnp.bfloat16),),
        late_scalars,
        pair_held,
        pair_other,
        scratch=(pltpu.VMEM((TOK, HD), jnp.float32),) * 2,
    )
    blocks = blocks.reshape(group_count, slot_count, BS // 2, 2 * HD)
    arrived = lax.ppermute(blocks[4:], "group", [(0, 4)])

    plus, minus, partner = called(
        second_message_kernel,
        (shard, shard, shard),
        None,
        next_part,
        last_part,
        partner_part,
        from_last,
        from_next,
        up,
        down,
        streamed=(arrived,),
    )
    from_last, from_next = moved(plus, 0, 1, 0), moved(minus, 0, 3, 0)
    from_partner = moved(partner, 1, 0, 0)

    blocks = jnp.where(picks[0], arrived, blocks[:4])
    sent = lax.ppermute(blocks[2:], "group", [(0, 2), (4, 6)])
    blocks = jnp.where(picks[1], sent, blocks[:2])
    sent = lax.ppermute(blocks[1:], "group", [(0, 1), (2, 3), (4, 5), (6, 7)])
    incoming = jnp.where(picks[2], sent, blocks[:1])
    (projected,) = called(
        total_kernel, (shard,), None, here_part, from_last, from_next, from_partner
    )
    return (projected[None], incoming)


def solution(mesh):
    in_specs = (
        P("group", None, "tp"),
        P(None, "tp"),
        P(None, "tp"),
        P("tp", None),
        P("group", None, "tp", None),
        P("group", None, "tp", None),
        P("group", None),
        P(),
    )
    out_specs = (P("group", None, "tp"), P("group", None, "tp", None))
    return jax.shard_map(
        on_device, mesh=mesh, in_specs=in_specs, out_specs=out_specs, check_vma=False
    )
```

```python
import jax
import jax.numpy as jnp
from jax import lax
from jax.experimental import pallas as pl
from jax.experimental.pallas import tpu as pltpu
from jax.sharding import PartitionSpec as P

HD = 128
KVH = 8
STEPS = 4
NPR = 2
BS = 16
R = 64
GQ = 4
TOK = 256
CH = 128
RP = 32


NEG_FILL = -1e30


def tp_index(x_hi, y, core):
    return x_hi * 8 + (y % 4) * 2 + core


def moved(shard, x_flip, y_step, core_flip):
    pairs = []
    for x_hi in range(2):
        for y in range(4):
            for core in range(2):
                pairs.append(
                    (
                        tp_index(x_hi, y, core),
                        tp_index(x_hi ^ x_flip, y + y_step, core ^ core_flip),
                    )
                )
    return lax.ppermute(shard, "tp", pairs)


def core_swap(shard):
    return moved(shard, 0, 0, 1)


def turns(positions):
    midpoint = HD // 2
    frequency = jnp.exp(
        -jnp.log(500000.0) * jnp.arange(midpoint, dtype=jnp.float32) * 2.0 / HD
    )
    angles = positions.astype(jnp.float32)[:, None] * frequency[None, :]
    cosine = jnp.cos(angles)
    sine = jnp.sin(angles)
    return (
        jnp.concatenate([cosine, cosine], axis=1),
        jnp.concatenate([-sine, sine], axis=1),
    )


SPAN = 256
CHIPS = 8
SHARD = 512
HALF = TOK // 2
PREFILL_CHUNK = 4096
ROWS_AT_ONCE = 4
LOG2_E = 1.4426950408889634
NT = (((1,), (1,)), ((), ()))
LONG = 6 * 10**9

CORE, IS_PREFILL, IS_KEY, NEAR_ROWS, FAR_ROWS, PLACE, CELLS = 0, 1, 2, 3, 11, 19, 27


def stacked_heads(*parts):
    return jnp.concatenate(
        [part[:, j * HD : (j + 1) * HD] for part in parts for j in range(part.shape[1] // HD)],
        axis=0,
    )


def length_bias(scalar_ref, length_ref, first, count):
    place = lax.broadcasted_iota(jnp.int32, (1, SPAN), 1) + scalar_ref[CORE] * SPAN
    return jnp.concatenate(
        [jnp.where(place < length_ref[first + row], 0.0, NEG_FILL) for row in range(count)],
        axis=1,
    )


def weights_of(scores, largest):
    return jnp.exp2((scores - largest) * (HD**-0.5 * LOG2_E)).astype(jnp.bfloat16)


def with_ones(values):
    return jnp.concatenate([values, jnp.ones_like(values)], axis=1)


def write_heads(mixed_ref, level_ref, rows, mixed, largest):
    count = mixed.shape[0] // GQ
    total = mixed[:, HD : HD + 1]
    normal = (mixed[:, :HD] / total).astype(jnp.bfloat16)
    level = largest * HD**-0.5 + jnp.log(total)
    lane = lax.broadcasted_iota(jnp.int32, (count, GQ), 1)
    levels = jnp.zeros((count, GQ), jnp.float32)
    for j in range(GQ):
        part = slice(j * count, (j + 1) * count)
        mixed_ref[rows, j * HD : (j + 1) * HD] = normal[part]
        levels = jnp.where(lane == j, level[part], levels)
    level_ref[rows, :] = levels


def prefill_kernel(
    scalar_ref,
    length_ref,
    own_ref,
    other_ref,
    key_ref,
    value_ref,
    mixed_ref,
    level_ref,
    keys,
    values,
    score_ref,
    sems,
):
    rows = PREFILL_CHUNK // SPAN
    chunks = RP // rows

    def fetches(prompt, step):
        part = pl.ds(prompt * RP + step * rows, rows)
        index = prompt * chunks + step
        return (
            pltpu.make_async_copy(key_ref.at[part], keys.at[part], sems.at[0, index]),
            pltpu.make_async_copy(value_ref.at[part], values.at[part], sems.at[1, index]),
        )

    for prompt in range(NPR):
        for kind in range(2):
            for step in range(chunks):
                fetches(prompt, step)[kind].start()

    def one_prompt(prompt, carry):
        tokens = pl.ds(pl.multiple_of(prompt * CH, CH), CH)
        queries = stacked_heads(own_ref[tokens, :], other_ref[tokens, :])

        def score_step(step, peak):
            fetches(prompt, step)[0].wait()
            part = keys[pl.ds(prompt * RP + step * rows, rows)].reshape(PREFILL_CHUNK, HD)
            scores = lax.dot_general(queries, part, NT, preferred_element_type=jnp.float32)
            scores = scores + length_bias(scalar_ref, length_ref, prompt * RP + step * rows, rows)
            score_ref[step] = scores
            for lanes in range(PREFILL_CHUNK // HD):
                peak = jnp.maximum(peak, scores[:, lanes * HD : (lanes + 1) * HD])
            return peak

        peak = lax.fori_loop(
            0, chunks, score_step, jnp.full((GQ * CH, HD), NEG_FILL, jnp.float32)
        )
        largest = jnp.max(peak, axis=1, keepdims=True)
        level = jnp.broadcast_to(largest, (GQ * CH, HD))

        def mix_step(step, mixed):
            fetches(prompt, step)[1].wait()
            weights = jnp.concatenate(
                [
                    weights_of(score_ref[step, :, lanes * HD : (lanes + 1) * HD], level)
                    for lanes in range(PREFILL_CHUNK // HD)
                ],
                axis=1,
            )
            part = values[pl.ds(prompt * RP + step * rows, rows)].reshape(PREFILL_CHUNK, HD)
            return mixed + jnp.dot(weights, with_ones(part), preferred_element_type=jnp.float32)

        mixed = lax.fori_loop(0, chunks, mix_step, jnp.zeros((GQ * CH, 2 * HD), jnp.float32))
        write_heads(mixed_ref, level_ref, tokens, mixed, largest)
        return carry

    lax.fori_loop(0, NPR, one_prompt, 0)


def decode_kernel(
    scalar_ref, length_ref, query_ref, key_ref, value_ref, mixed_ref, level_ref
):
    width = ROWS_AT_ONCE * SPAN
    tokens = ROWS_AT_ONCE * STEPS
    owner = lax.broadcasted_iota(jnp.int32, (GQ * tokens, width), 0) % tokens // STEPS
    holder = lax.broadcasted_iota(jnp.int32, (GQ * tokens, width), 1) // SPAN
    for part in range(query_ref.shape[0] // tokens):
        rows = slice(part * tokens, (part + 1) * tokens)
        cached = slice(part * ROWS_AT_ONCE, (part + 1) * ROWS_AT_ONCE)
        queries = stacked_heads(query_ref[rows, :])
        keys = key_ref[cached].reshape(width, HD)
        values = value_ref[cached].reshape(width, HD)
        scores = lax.dot_general(queries, keys, NT, preferred_element_type=jnp.float32)
        first = (pl.program_id(0) * (query_ref.shape[0] // tokens) + part) * ROWS_AT_ONCE
        bias = length_bias(scalar_ref, length_ref, first, ROWS_AT_ONCE)
        scores = jnp.where(owner == holder, scores + bias, NEG_FILL)
        largest = jnp.max(scores, axis=1, keepdims=True)
        mixed = jnp.dot(
            weights_of(scores, largest), with_ones(values), preferred_element_type=jnp.float32
        )
        write_heads(mixed_ref, level_ref, rows, mixed, largest)


def sort_pair(scalar_ref, held_ref, swapped_ref, keys, values):
    @pl.when(scalar_ref[CORE] == 0)
    def _():
        keys[...] = held_ref[...].astype(keys.dtype)
        values[...] = swapped_ref[...].astype(values.dtype)

    @pl.when(scalar_ref[CORE] != 0)
    def _():
        keys[...] = swapped_ref[...].astype(keys.dtype)
        values[...] = held_ref[...].astype(values.dtype)


def recent_kernel(scalar_ref, own_ref, other_ref, held_ref, swapped_ref, mixed_ref, level_ref):
    row = lax.broadcasted_iota(jnp.int32, (TOK, TOK), 0)
    column = lax.broadcasted_iota(jnp.int32, (TOK, TOK), 1)
    is_prefill = scalar_ref[IS_PREFILL] != 0
    together = jnp.where(is_prefill, row // CH - column // CH, row % R - column % R) == 0
    allowed = together & (column <= row)
    lane = lax.broadcasted_iota(jnp.int32, (TOK, GQ), 1)

    held = held_ref[...].astype(jnp.float32)
    swapped = swapped_ref[...].astype(jnp.float32)
    first = scalar_ref[CORE] == 0
    keys = jnp.where(first, held, swapped).astype(jnp.bfloat16)
    values = with_ones(jnp.where(first, swapped, held).astype(jnp.bfloat16))
    levels = jnp.zeros((TOK, GQ), jnp.float32)
    for j in range(GQ):
        source = own_ref if j < GQ // 2 else other_ref
        part = slice(j % (GQ // 2) * HD, (j % (GQ // 2) + 1) * HD)
        scores = lax.dot_general(
            source[:, part], keys, NT, preferred_element_type=jnp.float32
        )
        scores = jnp.where(allowed, scores, NEG_FILL)
        largest = jnp.max(scores, axis=1, keepdims=True)
        mixed = jnp.dot(
            weights_of(scores, largest), values, preferred_element_type=jnp.float32
        )
        total = mixed[:, HD : HD + 1]
        mixed_ref[:, j * HD : (j + 1) * HD] = (mixed[:, :HD] / total).astype(mixed_ref.dtype)
        levels = jnp.where(lane == j, largest * HD**-0.5 + jnp.log(total), levels)
    level_ref[...] = levels


def merged(parts, levels):
    half = GQ // 2
    turned = jnp.concatenate([levels[1][:, half:], levels[1][:, :half]], axis=1)
    levels = [levels[0], turned, levels[2]]
    top = jnp.maximum(jnp.maximum(levels[0], levels[1]), levels[2])
    shares = [jnp.exp(level - top) for level in levels]
    total = shares[0] + shares[1] + shares[2]
    shares = [share / total for share in shares]
    heads = []
    for j in range(GQ):
        mixed = jnp.zeros((TOK, HD), jnp.float32)
        for part, share, place in zip(parts, shares, (j, (j + half) % GQ, j)):
            values = part[:, place * HD : (place + 1) * HD].astype(jnp.float32)
            mixed = mixed + values * share[:, j : j + 1]
        heads.append(mixed.astype(jnp.bfloat16))
    return jnp.concatenate(heads, axis=1)


def swapped_copies(scalar_ref, first, swapped_ref, held_ref, sems):
    copies = []
    for index in range(4):
        columns = pl.ds(pl.multiple_of(scalar_ref[PLACE + first + index] * SHARD, SHARD), SHARD)
        copies.append(
            pltpu.make_async_copy(
                swapped_ref.at[:, columns], held_ref.at[index], sems.at[index]
            )
        )
        copies[-1].start()
    return copies


def product(scalar_ref, chip, joined, copy, weight_ref, held_ref, index):
    column = 2 * scalar_ref[PLACE + chip] + scalar_ref[CORE]
    own = weight_ref[:, pl.ds(pl.multiple_of(column * SHARD, SHARD), SHARD)]
    copy.wait()
    weights = jnp.concatenate([own, held_ref[index]], axis=0)
    return jnp.dot(joined, weights, preferred_element_type=jnp.float32).astype(jnp.bfloat16)


def merge_out_kernel(
    scalar_ref,
    swapped_ref,
    weight_ref,
    own_ref,
    own_level,
    other_ref,
    other_level,
    recent_ref,
    recent_level,
    plus,
    minus,
    up,
    down,
    attention,
    held_ref,
    sems,
):
    copies = swapped_copies(scalar_ref, 0, swapped_ref, held_ref, sems)
    joined = merged(
        (own_ref, other_ref, recent_ref), (own_level[...], other_level[...], recent_level[...])
    )
    attention[...] = joined
    parts = [
        product(scalar_ref, index, joined, copies[index], weight_ref, held_ref, index)
        for index in range(4)
    ]
    plus[:TOK] = parts[0]
    minus[:TOK] = parts[1]
    plus[TOK:] = parts[2][:HALF]
    minus[TOK:] = parts[2][HALF:]
    up[...] = parts[3][:HALF]
    down[...] = parts[3][HALF:]


def out_kernel(scalar_ref, swapped_ref, weight_ref, attention, *refs):
    *out_refs, held_ref, sems = refs
    copies = swapped_copies(scalar_ref, 4, swapped_ref, held_ref, sems)
    joined = attention[...]
    for index, ref in enumerate(out_refs):
        ref[...] = product(
            scalar_ref, 4 + index, joined, copies[index], weight_ref, held_ref, index
        )


def total_of(*parts):
    total = parts[0].astype(jnp.float32)
    for part in parts[1:]:
        total = total + part.astype(jnp.float32)
    return total.astype(jnp.bfloat16)


def second_message_kernel(
    arrived_ref,
    next_ref,
    last_ref,
    partner_ref,
    from_last,
    from_next,
    up,
    down,
    plus,
    minus,
    partner,
):
    plus[:HALF] = total_of(next_ref[:HALF], from_last[TOK:], up[...])
    plus[HALF:] = next_ref[HALF:]
    minus[:HALF] = last_ref[:HALF]
    minus[HALF:] = total_of(last_ref[HALF:], from_next[TOK:], down[...])
    partner[...] = total_of(partner_ref[...], from_last[:TOK], from_next[:TOK])


def total_kernel(here_ref, from_last, from_next, from_partner, out_ref):
    out_ref[...] = total_of(here_ref[...], from_last[...], from_next[...], from_partner[...])


def join_kernel(
    scalar_ref, own_ref, partner_ref, last_ref, next_ref, plus, minus, up, down, near, sem
):
    own = pltpu.make_async_copy(own_ref, near.at[:TOK], sem)
    own.start()
    plus[:TOK] = partner_ref[...]
    plus[TOK:] = last_ref[:HALF]
    minus[:TOK] = partner_ref[...]
    minus[TOK:] = next_ref[HALF:]
    up[...] = last_ref[HALF:]
    down[...] = next_ref[:HALF]
    for index, ref in enumerate((last_ref, next_ref, partner_ref)):
        near[(index + 1) * TOK : (index + 2) * TOK] = ref[...]
    own.wait()


def sides_kernel(mark_ref, last_ref, next_ref, upper_ref, lower_ref, sides):
    sides[:TOK] = last_ref[:TOK]
    sides[TOK : 2 * TOK] = next_ref[:TOK]
    sides[2 * TOK : 2 * TOK + HALF] = last_ref[TOK:]
    sides[2 * TOK + HALF : 3 * TOK] = next_ref[TOK:]
    sides[3 * TOK : 3 * TOK + HALF] = upper_ref[...]
    sides[3 * TOK + HALF :] = lower_ref[...]


def projected_parts(scalar_ref, first, shards, query_weight, pair_weight):
    joined = jnp.concatenate(shards, axis=1)
    rows = [
        pl.ds(pl.multiple_of(scalar_ref[first + index], SHARD), SHARD)
        for index in range(len(shards))
    ]
    return [
        jnp.dot(
            joined,
            jnp.concatenate([weight[part, :] for part in rows], axis=0),
            preferred_element_type=jnp.float32,
        )
        for weight in (query_weight, pair_weight)
    ]


def four_shards(ref):
    return [ref[index * TOK : (index + 1) * TOK] for index in range(4)]


def near_kernel(scalar_ref, query_weight, pair_weight, near_ref, other_ref, query, pair, mark):
    mark[...] = jnp.zeros_like(mark)
    query[...], pair[...] = projected_parts(
        scalar_ref,
        NEAR_ROWS,
        four_shards(near_ref) + four_shards(other_ref),
        query_weight,
        pair_weight,
    )


def far_kernel(
    scalar_ref,
    cosine_ref,
    sine_ref,
    query_weight,
    pair_weight,
    query_in,
    pair_in,
    far_ref,
    query,
    pair,
):
    sums = projected_parts(scalar_ref, FAR_ROWS, four_shards(far_ref), query_weight, pair_weight)
    query[...] = query_in[...] + sums[0]
    pair[...] = pair_in[...] + sums[1]


def last_kernel(
    scalar_ref,
    query_weight,
    pair_weight,
    query_in,
    pair_in,
    far_ref,
    cosine_ref,
    sine_ref,
    query_out,
    pair_out,
):
    sums = projected_parts(
        scalar_ref, FAR_ROWS + 4, four_shards(far_ref), query_weight, pair_weight
    )
    query = query_in[...] + sums[0]
    pair = pair_in[...] + sums[1]
    cosine = cosine_ref[...]
    sine = sine_ref[...]

    def rotated(values):
        return values * cosine + pltpu.roll(values, HD // 2, 1) * sine

    for head in range(query.shape[1] // HD):
        part = slice(head * HD, (head + 1) * HD)
        query_out[:, part] = rotated(query[:, part]).astype(jnp.bfloat16)
    is_key = scalar_ref[IS_KEY] != 0
    pair_out[...] = jnp.where(is_key, rotated(pair), pair).astype(jnp.bfloat16)


def blocks_kernel(scalar_ref, held_ref, swapped_ref, out_ref, keys, values):
    sliver = out_ref.shape[1]
    out_ref[...] = jnp.zeros_like(out_ref)

    @pl.when(scalar_ref[IS_PREFILL] != 0)
    def _():
        sort_pair(scalar_ref, held_ref, swapped_ref, keys, values)
        for block in range(TOK // BS):
            start = pl.multiple_of(scalar_ref[CORE] * sliver, sliver) + block * BS
            cell = scalar_ref[CELLS + block]
            out_ref[cell, :, :HD] = keys[pl.ds(start, sliver), :].astype(jnp.bfloat16)
            out_ref[cell, :, HD:] = values[pl.ds(start, sliver), :].astype(jnp.bfloat16)


def called(kernel, shapes, scalars, *arrays, streamed=(), scratch=(), flops=0, grant=12):
    whole = pl.BlockSpec(memory_space=pltpu.VMEM)
    specs = [pl.BlockSpec(memory_space=pl.ANY)] * len(streamed) + [whole] * len(arrays)
    arrays = tuple(streamed) + arrays
    if scalars is not None:
        specs = [pl.BlockSpec(memory_space=pltpu.SMEM)] + specs
        arrays = (scalars,) + arrays
    return pl.pallas_call(
        kernel,
        in_specs=specs,
        out_specs=tuple(whole for _ in shapes),
        out_shape=tuple(jax.ShapeDtypeStruct(shape, kind) for shape, kind in shapes),
        scratch_shapes=scratch,
        compiler_params=pltpu.CompilerParams(vmem_limit_bytes=grant * 2**20),
        cost_estimate=pl.CostEstimate(flops=flops, transcendentals=0, bytes_accessed=2**21),
    )(*arrays)


def outputs_of(kind):
    return (
        jax.ShapeDtypeStruct((TOK, GQ * HD), kind),
        jax.ShapeDtypeStruct((TOK, GQ), jnp.float32),
    )


def prefill_part(scalars, lengths, own, other, keys, values):
    chunks = RP * SPAN // PREFILL_CHUNK
    whole = pl.BlockSpec(memory_space=pltpu.VMEM)
    there = pl.BlockSpec(memory_space=pl.ANY)
    small = pl.BlockSpec(memory_space=pltpu.SMEM)
    return pl.pallas_call(
        prefill_kernel,
        in_specs=[small, small, whole, whole, there, there],
        out_specs=(whole, whole),
        out_shape=outputs_of(jnp.bfloat16),
        scratch_shapes=[
            pltpu.VMEM((R, SPAN, HD), jnp.bfloat16),
            pltpu.VMEM((R, SPAN, HD), jnp.bfloat16),
            pltpu.VMEM((chunks, GQ * CH, PREFILL_CHUNK), jnp.float32),
            pltpu.SemaphoreType.DMA((2, NPR * chunks)),
        ],
        compiler_params=pltpu.CompilerParams(vmem_limit_bytes=44 * 2**20),
    )(scalars, lengths, own, other, keys, values)


def decode_part(scalars, lengths, own, other, keys, values):
    def by_row(array):
        return array.reshape(STEPS, R, -1).transpose(1, 0, 2).reshape(TOK, -1)

    def by_step(array):
        return array.reshape(R, STEPS, -1).transpose(1, 0, 2).reshape(TOK, -1)

    rows = 8 * ROWS_AT_ONCE
    mixed, level = pl.pallas_call(
        decode_kernel,
        grid=(R // rows,),
        in_specs=[
            pl.BlockSpec(memory_space=pltpu.SMEM),
            pl.BlockSpec(memory_space=pltpu.SMEM),
            pl.BlockSpec((rows * STEPS, GQ * HD), lambda i: (i, 0)),
            pl.BlockSpec((rows, SPAN, HD), lambda i: (i, 0, 0)),
            pl.BlockSpec((rows, SPAN, HD), lambda i: (i, 0, 0)),
        ],
        out_specs=(
            pl.BlockSpec((rows * STEPS, GQ * HD), lambda i: (i, 0)),
            pl.BlockSpec((rows * STEPS, GQ), lambda i: (i, 0)),
        ),
        out_shape=outputs_of(jnp.bfloat16),
        compiler_params=pltpu.CompilerParams(vmem_limit_bytes=40 * 2**20),
    )(scalars, lengths, by_row(jnp.concatenate([own, other], axis=1)), keys, values)
    return by_step(mixed), by_step(level)


def cut_kernel(scalar_ref, weight_ref, out_ref, held_ref, in_sems, out_sems):
    fetches = []
    stores = []
    for chip in range(CHIPS):
        columns = pl.ds(pl.multiple_of((2 * chip + 1 - scalar_ref[CORE]) * SHARD, SHARD), SHARD)
        fetches.append(
            pltpu.make_async_copy(weight_ref.at[:, columns], held_ref.at[chip], in_sems.at[chip])
        )
        stores.append(
            pltpu.make_async_copy(
                held_ref.at[chip],
                out_ref.at[:, chip * SHARD : (chip + 1) * SHARD],
                out_sems.at[chip],
            )
        )
    for fetch in fetches:
        fetch.start()
    for fetch, store in zip(fetches, stores):
        fetch.wait()
        store.start()
    for store in stores:
        store.wait()


def cut_columns(scalars, out_weight):
    return pl.pallas_call(
        cut_kernel,
        in_specs=[
            pl.BlockSpec(memory_space=pltpu.SMEM),
            pl.BlockSpec(memory_space=pl.ANY),
        ],
        out_specs=pl.BlockSpec(memory_space=pl.ANY),
        out_shape=jax.ShapeDtypeStruct((out_weight.shape[0], CHIPS * SHARD), jnp.bfloat16),
        scratch_shapes=[
            pltpu.VMEM((CHIPS, out_weight.shape[0], SHARD), jnp.bfloat16),
            pltpu.SemaphoreType.DMA((CHIPS,)),
            pltpu.SemaphoreType.DMA((CHIPS,)),
        ],
        compiler_params=pltpu.CompilerParams(vmem_limit_bytes=12 * 2**20),
    )(scalars, out_weight)


def on_device(
    layer_input, query_weight, kv_weight, out_weight, cache_keys, cache_values, lengths, placement
):
    group_count = lax.axis_size("group")
    tp_rank = lax.axis_index("tp")
    group_rank = lax.axis_index("group")
    core = tp_rank % 2
    y = (tp_rank // 2) % 4
    x_hi = tp_rank // 8
    is_prefill = group_rank == 0
    tokens = layer_input[0]
    row_lengths = lengths[0]
    slot_count = 2 * (TOK // BS) // (group_count - 1)

    def rows_of(*owners):
        firsts = [tp_index(x_hi ^ flip, y + step, core) for flip, step in owners]
        return [first * SHARD for first in firsts] + [(first ^ 1) * SHARD for first in firsts]

    places = ((1, 1), (1, 3), (0, 2), (1, 2), (0, 1), (0, 3), (1, 0), (0, 0))
    single = (
        [core, is_prefill, tp_rank < KVH]
        + rows_of((0, 0), (0, 3), (0, 1), (1, 0))
        + rows_of((1, 3), (1, 1), (0, 2), (1, 2))
        + [(x_hi ^ flip) * 4 + (y + step) % 4 for flip, step in places]
    )
    picks = [group_rank >= 4, group_rank // 2 % 2 == 1, group_rank % 2 == 1]
    scalars = jnp.concatenate(
        [
            jnp.stack([jnp.asarray(one, jnp.int32) for one in single]),
            placement[:, 0] * slot_count + placement[:, 1],
        ]
    )
    prefix = jnp.sum(row_lengths.reshape(NPR, RP), axis=1)
    prompt_positions = (prefix[:, None] + jnp.arange(CH, dtype=jnp.int32)[None, :]).reshape(TOK)
    decode_step_positions = (
        row_lengths[None, :] + jnp.arange(STEPS, dtype=jnp.int32)[:, None]
    ).reshape(TOK)
    positions = jnp.where(is_prefill, prompt_positions, decode_step_positions)

    cut_out = cut_columns(scalars, out_weight)

    wide = ((TOK + HALF, SHARD), jnp.bfloat16)
    half = ((HALF, SHARD), jnp.bfloat16)
    shard = ((TOK, SHARD), jnp.bfloat16)
    four = ((4 * TOK, SHARD), jnp.bfloat16)
    weights = (query_weight, kv_weight)
    sums = (((TOK, query_weight.shape[1]), jnp.float32), ((TOK, kv_weight.shape[1]), jnp.float32))
    partner_tokens = moved(tokens, 1, 0, 0)
    last_tokens, next_tokens = moved(tokens, 0, 1, 0), moved(tokens, 0, 3, 0)
    scalars, picks, positions = lax.optimization_barrier((scalars, picks, positions))
    cosine, sine = turns(positions)
    plus, minus, up, down, near = called(
        join_kernel,
        (wide, wide, half, half, four),
        scalars,
        partner_tokens,
        last_tokens,
        next_tokens,
        streamed=(tokens,),
        scratch=(pltpu.SemaphoreType.DMA(()),),
        flops=LONG,
    )
    from_last, from_next = moved(plus, 0, 1, 0), moved(minus, 0, 3, 0)
    far_upper, far_lower = moved(down, 1, 3, 0), moved(up, 1, 1, 0)
    scalars, cut_out = lax.optimization_barrier((scalars, cut_out))
    *part, mark = called(
        near_kernel,
        sums + (((8, HD), jnp.float32),),
        scalars,
        *weights,
        near,
        core_swap(near),
        flops=2 * TOK * 8 * SHARD * 3 * HD,
    )
    (sides,) = called(
        sides_kernel,
        (four,),
        None,
        from_last,
        from_next,
        far_upper,
        far_lower,
        streamed=(mark,),
    )
    other_sides = core_swap(sides)
    part = called(
        far_kernel,
        sums,
        scalars,
        *weights,
        *part,
        sides,
        streamed=(cosine, sine),
        flops=2 * TOK * 4 * SHARD * 3 * HD,
    )
    _, _, cut_out = lax.optimization_barrier((other_sides, part[1], cut_out))
    swapped_out = core_swap(cut_out)
    query_local, pair_local = called(
        last_kernel,
        tuple((shape, jnp.bfloat16) for shape, _ in sums),
        scalars,
        *weights,
        *part,
        other_sides,
        cosine,
        sine,
        flops=2 * TOK * 4 * SHARD * 3 * HD,
    )
    query_other = core_swap(query_local)
    pair_held = lax.ppermute(
        pair_local, "tp", [(t, 2 * t if t < KVH else 2 * (t - KVH) + 1) for t in range(2 * KVH)]
    )
    cached = lax.cond(
        is_prefill,
        prefill_part,
        decode_part,
        scalars,
        row_lengths,
        query_local,
        query_other,
        cache_keys[0],
        cache_values[0],
    )
    cached, pair_held = lax.optimization_barrier((cached, pair_held))
    pair_other = core_swap(pair_held)
    other_cached = (core_swap(cached[0]), core_swap(cached[1]))
    recent = called(
        recent_kernel,
        (((TOK, GQ * HD), jnp.bfloat16), ((TOK, GQ), jnp.float32)),
        scalars,
        query_local,
        query_other,
        pair_held,
        pair_other,
        flops=LONG,
    )

    product_scratch = (
        pltpu.VMEM((4, out_weight.shape[0], SHARD), jnp.bfloat16),
        pltpu.SemaphoreType.DMA((4,)),
    )
    plus, minus, up, down, attention = called(
        merge_out_kernel,
        (wide, wide, half, half, ((TOK, GQ * HD), jnp.bfloat16)),
        scalars,
        out_weight,
        *cached,
        *other_cached,
        *recent,
        streamed=(swapped_out,),
        scratch=product_scratch,
        flops=2 * TOK * 4 * SHARD * GQ * HD,
    )
    next_part, last_part, partner_part, here_part = called(
        out_kernel,
        (shard,) * 4,
        scalars,
        out_weight,
        attention,
        streamed=(swapped_out,),
        scratch=product_scratch,
        flops=2 * TOK * 4 * SHARD * GQ * HD,
    )
    from_last, from_next = moved(plus, 0, 1, 0), moved(minus, 0, 3, 0)
    up, down = moved(up, 1, 1, 0), moved(down, 1, 3, 0)

    _, late_scalars = lax.optimization_barrier((attention, scalars))
    (blocks,) = called(
        blocks_kernel,
        (((group_count * slot_count, BS // 2, 2 * HD), jnp.bfloat16),),
        late_scalars,
        pair_held,
        pair_other,
        scratch=(pltpu.VMEM((TOK, HD), jnp.float32),) * 2,
    )
    blocks = blocks.reshape(group_count, slot_count, BS // 2, 2 * HD)
    arrived = lax.ppermute(blocks[4:], "group", [(0, 4)])

    plus, minus, partner = called(
        second_message_kernel,
        (shard, shard, shard),
        None,
        next_part,
        last_part,
        partner_part,
        from_last,
        from_next,
        up,
        down,
        streamed=(arrived,),
    )
    from_last, from_next = moved(plus, 0, 1, 0), moved(minus, 0, 3, 0)
    from_partner = moved(partner, 1, 0, 0)

    blocks = jnp.where(picks[0], arrived, blocks[:4])
    sent = lax.ppermute(blocks[2:], "group", [(0, 2), (4, 6)])
    blocks = jnp.where(picks[1], sent, blocks[:2])
    sent = lax.ppermute(blocks[1:], "group", [(0, 1), (2, 3), (4, 5), (6, 7)])
    incoming = jnp.where(picks[2], sent, blocks[:1])
    (projected,) = called(
        total_kernel, (shard,), None, here_part, from_last, from_next, from_partner
    )
    return (projected[None], incoming)


def solution(mesh):
    in_specs = (
        P("group", None, "tp"),
        P(None, "tp"),
        P(None, "tp"),
        P("tp", None),
        P("group", None, "tp", None),
        P("group", None, "tp", None),
        P("group", None),
        P(),
    )
    out_specs = (P("group", None, "tp"), P("group", None, "tp", None))
    return jax.shard_map(
        on_device, mesh=mesh, in_specs=in_specs, out_specs=out_specs, check_vma=False
    )
```

```python
import jax
import jax.numpy as jnp
from jax import lax
from jax.experimental import pallas as pl
from jax.experimental.pallas import tpu as pltpu
from jax.sharding import PartitionSpec as P

HD = 128
KVH = 8
STEPS = 4
NPR = 2
BS = 16
R = 64
GQ = 4
TOK = 256
CH = 128
RP = 32


NEG_FILL = -1e30


def tp_index(x_hi, y, core):
    return x_hi * 8 + (y % 4) * 2 + core


def moved(shard, x_flip, y_step, core_flip):
    pairs = []
    for x_hi in range(2):
        for y in range(4):
            for core in range(2):
                pairs.append(
                    (
                        tp_index(x_hi, y, core),
                        tp_index(x_hi ^ x_flip, y + y_step, core ^ core_flip),
                    )
                )
    return lax.ppermute(shard, "tp", pairs)


def core_swap(shard):
    return moved(shard, 0, 0, 1)


def turns(positions):
    midpoint = HD // 2
    frequency = jnp.exp(
        -jnp.log(500000.0) * jnp.arange(midpoint, dtype=jnp.float32) * 2.0 / HD
    )
    angles = positions.astype(jnp.float32)[:, None] * frequency[None, :]
    cosine = jnp.cos(angles)
    sine = jnp.sin(angles)
    return (
        jnp.concatenate([cosine, cosine], axis=1),
        jnp.concatenate([-sine, sine], axis=1),
    )


SPAN = 256
CHIPS = 8
SHARD = 512
HALF = TOK // 2
PREFILL_CHUNK = 4096
ROWS_AT_ONCE = 4
LOG2_E = 1.4426950408889634
NT = (((1,), (1,)), ((), ()))
LONG = 6 * 10**9

CORE, IS_PREFILL, IS_KEY, NEAR_ROWS, FAR_ROWS, PLACE, CELLS = 0, 1, 2, 3, 11, 19, 27


def stacked_heads(*parts):
    return jnp.concatenate(
        [part[:, j * HD : (j + 1) * HD] for part in parts for j in range(part.shape[1] // HD)],
        axis=0,
    )


def length_bias(scalar_ref, length_ref, first, count):
    place = lax.broadcasted_iota(jnp.int32, (1, SPAN), 1) + scalar_ref[CORE] * SPAN
    return jnp.concatenate(
        [jnp.where(place < length_ref[first + row], 0.0, NEG_FILL) for row in range(count)],
        axis=1,
    )


def weights_of(scores, largest):
    return jnp.exp2((scores - largest) * (HD**-0.5 * LOG2_E)).astype(jnp.bfloat16)


def with_ones(values):
    return jnp.concatenate([values, jnp.ones_like(values)], axis=1)


def write_heads(mixed_ref, level_ref, rows, mixed, largest):
    count = mixed.shape[0] // GQ
    total = mixed[:, HD : HD + 1]
    normal = (mixed[:, :HD] / total).astype(jnp.bfloat16)
    level = largest * HD**-0.5 + jnp.log(total)
    lane = lax.broadcasted_iota(jnp.int32, (count, GQ), 1)
    levels = jnp.zeros((count, GQ), jnp.float32)
    for j in range(GQ):
        part = slice(j * count, (j + 1) * count)
        mixed_ref[rows, j * HD : (j + 1) * HD] = normal[part]
        levels = jnp.where(lane == j, level[part], levels)
    level_ref[rows, :] = levels


def prefill_kernel(
    scalar_ref,
    length_ref,
    own_ref,
    other_ref,
    key_ref,
    value_ref,
    mixed_ref,
    level_ref,
    keys,
    values,
    score_ref,
    sems,
):
    rows = PREFILL_CHUNK // SPAN
    chunks = RP // rows

    def fetches(prompt, step):
        part = pl.ds(prompt * RP + step * rows, rows)
        index = prompt * chunks + step
        return (
            pltpu.make_async_copy(key_ref.at[part], keys.at[part], sems.at[0, index]),
            pltpu.make_async_copy(value_ref.at[part], values.at[part], sems.at[1, index]),
        )

    for prompt in range(NPR):
        for kind in range(2):
            for step in range(chunks):
                fetches(prompt, step)[kind].start()

    def one_prompt(prompt, carry):
        tokens = pl.ds(pl.multiple_of(prompt * CH, CH), CH)
        queries = stacked_heads(own_ref[tokens, :], other_ref[tokens, :])

        def score_step(step, peak):
            fetches(prompt, step)[0].wait()
            part = keys[pl.ds(prompt * RP + step * rows, rows)].reshape(PREFILL_CHUNK, HD)
            scores = lax.dot_general(queries, part, NT, preferred_element_type=jnp.float32)
            scores = scores + length_bias(scalar_ref, length_ref, prompt * RP + step * rows, rows)
            score_ref[step] = scores
            for lanes in range(PREFILL_CHUNK // HD):
                peak = jnp.maximum(peak, scores[:, lanes * HD : (lanes + 1) * HD])
            return peak

        peak = lax.fori_loop(
            0, chunks, score_step, jnp.full((GQ * CH, HD), NEG_FILL, jnp.float32)
        )
        largest = jnp.max(peak, axis=1, keepdims=True)
        level = jnp.broadcast_to(largest, (GQ * CH, HD))

        def mix_step(step, mixed):
            fetches(prompt, step)[1].wait()
            weights = jnp.concatenate(
                [
                    weights_of(score_ref[step, :, lanes * HD : (lanes + 1) * HD], level)
                    for lanes in range(PREFILL_CHUNK // HD)
                ],
                axis=1,
            )
            part = values[pl.ds(prompt * RP + step * rows, rows)].reshape(PREFILL_CHUNK, HD)
            return mixed + jnp.dot(weights, with_ones(part), preferred_element_type=jnp.float32)

        mixed = lax.fori_loop(0, chunks, mix_step, jnp.zeros((GQ * CH, 2 * HD), jnp.float32))
        write_heads(mixed_ref, level_ref, tokens, mixed, largest)
        return carry

    lax.fori_loop(0, NPR, one_prompt, 0)


def decode_kernel(
    scalar_ref, length_ref, query_ref, key_ref, value_ref, mixed_ref, level_ref
):
    width = ROWS_AT_ONCE * SPAN
    tokens = ROWS_AT_ONCE * STEPS
    owner = lax.broadcasted_iota(jnp.int32, (GQ * tokens, width), 0) % tokens // STEPS
    holder = lax.broadcasted_iota(jnp.int32, (GQ * tokens, width), 1) // SPAN
    for part in range(query_ref.shape[0] // tokens):
        rows = slice(part * tokens, (part + 1) * tokens)
        cached = slice(part * ROWS_AT_ONCE, (part + 1) * ROWS_AT_ONCE)
        queries = stacked_heads(query_ref[rows, :])
        keys = key_ref[cached].reshape(width, HD)
        values = value_ref[cached].reshape(width, HD)
        scores = lax.dot_general(queries, keys, NT, preferred_element_type=jnp.float32)
        first = (pl.program_id(0) * (query_ref.shape[0] // tokens) + part) * ROWS_AT_ONCE
        bias = length_bias(scalar_ref, length_ref, first, ROWS_AT_ONCE)
        scores = jnp.where(owner == holder, scores + bias, NEG_FILL)
        largest = jnp.max(scores, axis=1, keepdims=True)
        mixed = jnp.dot(
            weights_of(scores, largest), with_ones(values), preferred_element_type=jnp.float32
        )
        write_heads(mixed_ref, level_ref, rows, mixed, largest)


def sort_pair(scalar_ref, held_ref, swapped_ref, keys, values):
    @pl.when(scalar_ref[CORE] == 0)
    def _():
        keys[...] = held_ref[...].astype(keys.dtype)
        values[...] = swapped_ref[...].astype(values.dtype)

    @pl.when(scalar_ref[CORE] != 0)
    def _():
        keys[...] = swapped_ref[...].astype(keys.dtype)
        values[...] = held_ref[...].astype(values.dtype)


def recent_kernel(scalar_ref, own_ref, other_ref, held_ref, swapped_ref, mixed_ref, level_ref):
    row = lax.broadcasted_iota(jnp.int32, (TOK, TOK), 0)
    column = lax.broadcasted_iota(jnp.int32, (TOK, TOK), 1)
    is_prefill = scalar_ref[IS_PREFILL] != 0
    together = jnp.where(is_prefill, row // CH - column // CH, row % R - column % R) == 0
    allowed = together & (column <= row)
    lane = lax.broadcasted_iota(jnp.int32, (TOK, GQ), 1)

    held = held_ref[...].astype(jnp.float32)
    swapped = swapped_ref[...].astype(jnp.float32)
    first = scalar_ref[CORE] == 0
    keys = jnp.where(first, held, swapped).astype(jnp.bfloat16)
    values = with_ones(jnp.where(first, swapped, held).astype(jnp.bfloat16))
    levels = jnp.zeros((TOK, GQ), jnp.float32)
    for j in range(GQ):
        source = own_ref if j < GQ // 2 else other_ref
        part = slice(j % (GQ // 2) * HD, (j % (GQ // 2) + 1) * HD)
        scores = lax.dot_general(
            source[:, part], keys, NT, preferred_element_type=jnp.float32
        )
        scores = jnp.where(allowed, scores, NEG_FILL)
        largest = jnp.max(scores, axis=1, keepdims=True)
        mixed = jnp.dot(
            weights_of(scores, largest), values, preferred_element_type=jnp.float32
        )
        total = mixed[:, HD : HD + 1]
        mixed_ref[:, j * HD : (j + 1) * HD] = (mixed[:, :HD] / total).astype(mixed_ref.dtype)
        levels = jnp.where(lane == j, largest * HD**-0.5 + jnp.log(total), levels)
    level_ref[...] = levels


def merged(parts, levels):
    half = GQ // 2
    turned = jnp.concatenate([levels[1][:, half:], levels[1][:, :half]], axis=1)
    levels = [levels[0], turned, levels[2]]
    top = jnp.maximum(jnp.maximum(levels[0], levels[1]), levels[2])
    shares = [jnp.exp(level - top) for level in levels]
    total = shares[0] + shares[1] + shares[2]
    shares = [share / total for share in shares]
    heads = []
    for j in range(GQ):
        mixed = jnp.zeros((TOK, HD), jnp.float32)
        for part, share, place in zip(parts, shares, (j, (j + half) % GQ, j)):
            values = part[:, place * HD : (place + 1) * HD].astype(jnp.float32)
            mixed = mixed + values * share[:, j : j + 1]
        heads.append(mixed.astype(jnp.bfloat16))
    return jnp.concatenate(heads, axis=1)


def swapped_copies(scalar_ref, first, swapped_ref, held_ref, sems):
    copies = []
    for index in range(4):
        columns = pl.ds(pl.multiple_of(scalar_ref[PLACE + first + index] * SHARD, SHARD), SHARD)
        copies.append(
            pltpu.make_async_copy(
                swapped_ref.at[:, columns], held_ref.at[index], sems.at[index]
            )
        )
        copies[-1].start()
    return copies


def product(scalar_ref, chip, joined, copy, weight_ref, held_ref, index):
    column = 2 * scalar_ref[PLACE + chip] + scalar_ref[CORE]
    own = weight_ref[:, pl.ds(pl.multiple_of(column * SHARD, SHARD), SHARD)]
    copy.wait()
    weights = jnp.concatenate([own, held_ref[index]], axis=0)
    return jnp.dot(joined, weights, preferred_element_type=jnp.float32).astype(jnp.bfloat16)


def merge_out_kernel(
    scalar_ref,
    swapped_ref,
    weight_ref,
    own_ref,
    own_level,
    other_ref,
    other_level,
    recent_ref,
    recent_level,
    plus,
    minus,
    up,
    down,
    attention,
    held_ref,
    sems,
):
    copies = swapped_copies(scalar_ref, 0, swapped_ref, held_ref, sems)
    joined = merged(
        (own_ref, other_ref, recent_ref), (own_level[...], other_level[...], recent_level[...])
    )
    attention[...] = joined
    parts = [
        product(scalar_ref, index, joined, copies[index], weight_ref, held_ref, index)
        for index in range(4)
    ]
    plus[:TOK] = parts[0]
    minus[:TOK] = parts[1]
    plus[TOK:] = parts[2][:HALF]
    minus[TOK:] = parts[2][HALF:]
    up[...] = parts[3][:HALF]
    down[...] = parts[3][HALF:]


def out_kernel(scalar_ref, swapped_ref, weight_ref, attention, *refs):
    *out_refs, held_ref, sems = refs
    copies = swapped_copies(scalar_ref, 4, swapped_ref, held_ref, sems)
    joined = attention[...]
    for index, ref in enumerate(out_refs):
        ref[...] = product(
            scalar_ref, 4 + index, joined, copies[index], weight_ref, held_ref, index
        )


def total_of(*parts):
    total = parts[0].astype(jnp.float32)
    for part in parts[1:]:
        total = total + part.astype(jnp.float32)
    return total.astype(jnp.bfloat16)


def second_message_kernel(
    arrived_ref,
    next_ref,
    last_ref,
    partner_ref,
    from_last,
    from_next,
    up,
    down,
    plus,
    minus,
    partner,
):
    plus[:HALF] = total_of(next_ref[:HALF], from_last[TOK:], up[...])
    plus[HALF:] = next_ref[HALF:]
    minus[:HALF] = last_ref[:HALF]
    minus[HALF:] = total_of(last_ref[HALF:], from_next[TOK:], down[...])
    partner[...] = total_of(partner_ref[...], from_last[:TOK], from_next[:TOK])


def total_kernel(here_ref, from_last, from_next, from_partner, out_ref):
    out_ref[...] = total_of(here_ref[...], from_last[...], from_next[...], from_partner[...])


def fetch_kernel(source_ref, out_ref, sem):
    copy = pltpu.make_async_copy(source_ref, out_ref, sem)
    copy.start()
    copy.wait()


def join_kernel(
    scalar_ref, own_ref, partner_ref, last_ref, next_ref, plus, minus, up, down, near
):
    plus[:TOK] = partner_ref[...]
    plus[TOK:] = last_ref[:HALF]
    minus[:TOK] = partner_ref[...]
    minus[TOK:] = next_ref[HALF:]
    up[...] = last_ref[HALF:]
    down[...] = next_ref[:HALF]
    for index, ref in enumerate((own_ref, last_ref, next_ref, partner_ref)):
        near[index * TOK : (index + 1) * TOK] = ref[...]


def sides_kernel(mark_ref, last_ref, next_ref, upper_ref, lower_ref, sides):
    sides[:TOK] = last_ref[:TOK]
    sides[TOK : 2 * TOK] = next_ref[:TOK]
    sides[2 * TOK : 2 * TOK + HALF] = last_ref[TOK:]
    sides[2 * TOK + HALF : 3 * TOK] = next_ref[TOK:]
    sides[3 * TOK : 3 * TOK + HALF] = upper_ref[...]
    sides[3 * TOK + HALF :] = lower_ref[...]


def projected_parts(scalar_ref, first, shards, query_weight, pair_weight):
    joined = jnp.concatenate(shards, axis=1)
    rows = [
        pl.ds(pl.multiple_of(scalar_ref[first + index], SHARD), SHARD)
        for index in range(len(shards))
    ]
    return [
        jnp.dot(
            joined,
            jnp.concatenate([weight[part, :] for part in rows], axis=0),
            preferred_element_type=jnp.float32,
        )
        for weight in (query_weight, pair_weight)
    ]


def four_shards(ref):
    return [ref[index * TOK : (index + 1) * TOK] for index in range(4)]


def near_kernel(scalar_ref, query_weight, pair_weight, near_ref, other_ref, query, pair, mark):
    mark[...] = jnp.zeros_like(mark)
    query[...], pair[...] = projected_parts(
        scalar_ref,
        NEAR_ROWS,
        four_shards(near_ref) + four_shards(other_ref),
        query_weight,
        pair_weight,
    )


def far_kernel(
    scalar_ref,
    cosine_ref,
    sine_ref,
    query_weight,
    pair_weight,
    query_in,
    pair_in,
    far_ref,
    query,
    pair,
):
    sums = projected_parts(scalar_ref, FAR_ROWS, four_shards(far_ref), query_weight, pair_weight)
    query[...] = query_in[...] + sums[0]
    pair[...] = pair_in[...] + sums[1]


def last_kernel(
    scalar_ref,
    query_weight,
    pair_weight,
    query_in,
    pair_in,
    far_ref,
    cosine_ref,
    sine_ref,
    query_out,
    pair_out,
):
    sums = projected_parts(
        scalar_ref, FAR_ROWS + 4, four_shards(far_ref), query_weight, pair_weight
    )
    query = query_in[...] + sums[0]
    pair = pair_in[...] + sums[1]
    cosine = cosine_ref[...]
    sine = sine_ref[...]

    def rotated(values):
        return values * cosine + pltpu.roll(values, HD // 2, 1) * sine

    for head in range(query.shape[1] // HD):
        part = slice(head * HD, (head + 1) * HD)
        query_out[:, part] = rotated(query[:, part]).astype(jnp.bfloat16)
    is_key = scalar_ref[IS_KEY] != 0
    pair_out[...] = jnp.where(is_key, rotated(pair), pair).astype(jnp.bfloat16)


def blocks_kernel(scalar_ref, held_ref, swapped_ref, out_ref, keys, values):
    sliver = out_ref.shape[1]
    out_ref[...] = jnp.zeros_like(out_ref)

    @pl.when(scalar_ref[IS_PREFILL] != 0)
    def _():
        sort_pair(scalar_ref, held_ref, swapped_ref, keys, values)
        for block in range(TOK // BS):
            start = pl.multiple_of(scalar_ref[CORE] * sliver, sliver) + block * BS
            cell = scalar_ref[CELLS + block]
            out_ref[cell, :, :HD] = keys[pl.ds(start, sliver), :].astype(jnp.bfloat16)
            out_ref[cell, :, HD:] = values[pl.ds(start, sliver), :].astype(jnp.bfloat16)


def called(kernel, shapes, scalars, *arrays, streamed=(), scratch=(), flops=0, grant=12):
    whole = pl.BlockSpec(memory_space=pltpu.VMEM)
    specs = [pl.BlockSpec(memory_space=pl.ANY)] * len(streamed) + [whole] * len(arrays)
    arrays = tuple(streamed) + arrays
    if scalars is not None:
        specs = [pl.BlockSpec(memory_space=pltpu.SMEM)] + specs
        arrays = (scalars,) + arrays
    return pl.pallas_call(
        kernel,
        in_specs=specs,
        out_specs=tuple(whole for _ in shapes),
        out_shape=tuple(jax.ShapeDtypeStruct(shape, kind) for shape, kind in shapes),
        scratch_shapes=scratch,
        compiler_params=pltpu.CompilerParams(vmem_limit_bytes=grant * 2**20),
        cost_estimate=pl.CostEstimate(flops=flops, transcendentals=0, bytes_accessed=2**21),
    )(*arrays)


def outputs_of(kind):
    return (
        jax.ShapeDtypeStruct((TOK, GQ * HD), kind),
        jax.ShapeDtypeStruct((TOK, GQ), jnp.float32),
    )


def prefill_part(scalars, lengths, own, other, keys, values):
    chunks = RP * SPAN // PREFILL_CHUNK
    whole = pl.BlockSpec(memory_space=pltpu.VMEM)
    there = pl.BlockSpec(memory_space=pl.ANY)
    small = pl.BlockSpec(memory_space=pltpu.SMEM)
    return pl.pallas_call(
        prefill_kernel,
        in_specs=[small, small, whole, whole, there, there],
        out_specs=(whole, whole),
        out_shape=outputs_of(jnp.bfloat16),
        scratch_shapes=[
            pltpu.VMEM((R, SPAN, HD), jnp.bfloat16),
            pltpu.VMEM((R, SPAN, HD), jnp.bfloat16),
            pltpu.VMEM((chunks, GQ * CH, PREFILL_CHUNK), jnp.float32),
            pltpu.SemaphoreType.DMA((2, NPR * chunks)),
        ],
        compiler_params=pltpu.CompilerParams(vmem_limit_bytes=44 * 2**20),
    )(scalars, lengths, own, other, keys, values)


def decode_part(scalars, lengths, own, other, keys, values):
    def by_row(array):
        return array.reshape(STEPS, R, -1).transpose(1, 0, 2).reshape(TOK, -1)

    def by_step(array):
        return array.reshape(R, STEPS, -1).transpose(1, 0, 2).reshape(TOK, -1)

    rows = 8 * ROWS_AT_ONCE
    mixed, level = pl.pallas_call(
        decode_kernel,
        grid=(R // rows,),
        in_specs=[
            pl.BlockSpec(memory_space=pltpu.SMEM),
            pl.BlockSpec(memory_space=pltpu.SMEM),
            pl.BlockSpec((rows * STEPS, GQ * HD), lambda i: (i, 0)),
            pl.BlockSpec((rows, SPAN, HD), lambda i: (i, 0, 0)),
            pl.BlockSpec((rows, SPAN, HD), lambda i: (i, 0, 0)),
        ],
        out_specs=(
            pl.BlockSpec((rows * STEPS, GQ * HD), lambda i: (i, 0)),
            pl.BlockSpec((rows * STEPS, GQ), lambda i: (i, 0)),
        ),
        out_shape=outputs_of(jnp.bfloat16),
        compiler_params=pltpu.CompilerParams(vmem_limit_bytes=40 * 2**20),
    )(scalars, lengths, by_row(jnp.concatenate([own, other], axis=1)), keys, values)
    return by_step(mixed), by_step(level)


def cut_kernel(scalar_ref, weight_ref, out_ref, held_ref, in_sems, out_sems):
    fetches = []
    stores = []
    for chip in range(CHIPS):
        columns = pl.ds(pl.multiple_of((2 * chip + 1 - scalar_ref[CORE]) * SHARD, SHARD), SHARD)
        fetches.append(
            pltpu.make_async_copy(weight_ref.at[:, columns], held_ref.at[chip], in_sems.at[chip])
        )
        stores.append(
            pltpu.make_async_copy(
                held_ref.at[chip],
                out_ref.at[:, chip * SHARD : (chip + 1) * SHARD],
                out_sems.at[chip],
            )
        )
    for fetch in fetches:
        fetch.start()
    for fetch, store in zip(fetches, stores):
        fetch.wait()
        store.start()
    for store in stores:
        store.wait()


def cut_columns(scalars, out_weight):
    return pl.pallas_call(
        cut_kernel,
        in_specs=[
            pl.BlockSpec(memory_space=pltpu.SMEM),
            pl.BlockSpec(memory_space=pl.ANY),
        ],
        out_specs=pl.BlockSpec(memory_space=pl.ANY),
        out_shape=jax.ShapeDtypeStruct((out_weight.shape[0], CHIPS * SHARD), jnp.bfloat16),
        scratch_shapes=[
            pltpu.VMEM((CHIPS, out_weight.shape[0], SHARD), jnp.bfloat16),
            pltpu.SemaphoreType.DMA((CHIPS,)),
            pltpu.SemaphoreType.DMA((CHIPS,)),
        ],
        compiler_params=pltpu.CompilerParams(vmem_limit_bytes=12 * 2**20),
    )(scalars, out_weight)


def on_device(
    layer_input, query_weight, kv_weight, out_weight, cache_keys, cache_values, lengths, placement
):
    group_count = lax.axis_size("group")
    tp_rank = lax.axis_index("tp")
    group_rank = lax.axis_index("group")
    core = tp_rank % 2
    y = (tp_rank // 2) % 4
    x_hi = tp_rank // 8
    is_prefill = group_rank == 0
    tokens = layer_input[0]
    row_lengths = lengths[0]
    slot_count = 2 * (TOK // BS) // (group_count - 1)

    def rows_of(*owners):
        firsts = [tp_index(x_hi ^ flip, y + step, core) for flip, step in owners]
        return [first * SHARD for first in firsts] + [(first ^ 1) * SHARD for first in firsts]

    places = ((1, 1), (1, 3), (0, 2), (1, 2), (0, 1), (0, 3), (1, 0), (0, 0))
    single = (
        [core, is_prefill, tp_rank < KVH]
        + rows_of((0, 0), (0, 3), (0, 1), (1, 0))
        + rows_of((1, 3), (1, 1), (0, 2), (1, 2))
        + [(x_hi ^ flip) * 4 + (y + step) % 4 for flip, step in places]
    )
    picks = [group_rank >= 4, group_rank // 2 % 2 == 1, group_rank % 2 == 1]
    scalars = jnp.concatenate(
        [
            jnp.stack([jnp.asarray(one, jnp.int32) for one in single]),
            placement[:, 0] * slot_count + placement[:, 1],
        ]
    )
    prefix = jnp.sum(row_lengths.reshape(NPR, RP), axis=1)
    prompt_positions = (prefix[:, None] + jnp.arange(CH, dtype=jnp.int32)[None, :]).reshape(TOK)
    decode_step_positions = (
        row_lengths[None, :] + jnp.arange(STEPS, dtype=jnp.int32)[:, None]
    ).reshape(TOK)
    positions = jnp.where(is_prefill, prompt_positions, decode_step_positions)

    cut_out = cut_columns(scalars, out_weight)

    wide = ((TOK + HALF, SHARD), jnp.bfloat16)
    half = ((HALF, SHARD), jnp.bfloat16)
    shard = ((TOK, SHARD), jnp.bfloat16)
    four = ((4 * TOK, SHARD), jnp.bfloat16)
    weights = (query_weight, kv_weight)
    sums = (((TOK, query_weight.shape[1]), jnp.float32), ((TOK, kv_weight.shape[1]), jnp.float32))
    partner_tokens = moved(tokens, 1, 0, 0)
    last_tokens, next_tokens = moved(tokens, 0, 1, 0), moved(tokens, 0, 3, 0)
    scalars, picks, positions = lax.optimization_barrier((scalars, picks, positions))
    cosine, sine = turns(positions)
    (own_tokens,) = called(
        fetch_kernel,
        (shard,),
        None,
        streamed=(tokens,),
        scratch=(pltpu.SemaphoreType.DMA(()),),
    )
    plus, minus, up, down, near = called(
        join_kernel,
        (wide, wide, half, half, four),
        scalars,
        own_tokens,
        partner_tokens,
        last_tokens,
        next_tokens,
        flops=LONG,
    )
    from_last, from_next = moved(plus, 0, 1, 0), moved(minus, 0, 3, 0)
    far_upper, far_lower = moved(down, 1, 3, 0), moved(up, 1, 1, 0)
    scalars, cut_out = lax.optimization_barrier((scalars, cut_out))
    *part, mark = called(
        near_kernel,
        sums + (((8, HD), jnp.float32),),
        scalars,
        *weights,
        near,
        core_swap(near),
        flops=2 * TOK * 8 * SHARD * 3 * HD,
    )
    (sides,) = called(
        sides_kernel,
        (four,),
        None,
        from_last,
        from_next,
        far_upper,
        far_lower,
        streamed=(mark,),
    )
    other_sides = core_swap(sides)
    part = called(
        far_kernel,
        sums,
        scalars,
        *weights,
        *part,
        sides,
        streamed=(cosine, sine),
        flops=2 * TOK * 4 * SHARD * 3 * HD,
    )
    _, _, cut_out = lax.optimization_barrier((other_sides, part[1], cut_out))
    swapped_out = core_swap(cut_out)
    query_local, pair_local = called(
        last_kernel,
        tuple((shape, jnp.bfloat16) for shape, _ in sums),
        scalars,
        *weights,
        *part,
        other_sides,
        cosine,
        sine,
        flops=2 * TOK * 4 * SHARD * 3 * HD,
    )
    query_other = core_swap(query_local)
    pair_held = lax.ppermute(
        pair_local, "tp", [(t, 2 * t if t < KVH else 2 * (t - KVH) + 1) for t in range(2 * KVH)]
    )
    cached = lax.cond(
        is_prefill,
        prefill_part,
        decode_part,
        scalars,
        row_lengths,
        query_local,
        query_other,
        cache_keys[0],
        cache_values[0],
    )
    cached, pair_held = lax.optimization_barrier((cached, pair_held))
    pair_other = core_swap(pair_held)
    other_cached = (core_swap(cached[0]), core_swap(cached[1]))
    recent = called(
        recent_kernel,
        (((TOK, GQ * HD), jnp.bfloat16), ((TOK, GQ), jnp.float32)),
        scalars,
        query_local,
        query_other,
        pair_held,
        pair_other,
        flops=LONG,
    )

    product_scratch = (
        pltpu.VMEM((4, out_weight.shape[0], SHARD), jnp.bfloat16),
        pltpu.SemaphoreType.DMA((4,)),
    )
    plus, minus, up, down, attention = called(
        merge_out_kernel,
        (wide, wide, half, half, ((TOK, GQ * HD), jnp.bfloat16)),
        scalars,
        out_weight,
        *cached,
        *other_cached,
        *recent,
        streamed=(swapped_out,),
        scratch=product_scratch,
        flops=2 * TOK * 4 * SHARD * GQ * HD,
    )
    next_part, last_part, partner_part, here_part = called(
        out_kernel,
        (shard,) * 4,
        scalars,
        out_weight,
        attention,
        streamed=(swapped_out,),
        scratch=product_scratch,
        flops=2 * TOK * 4 * SHARD * GQ * HD,
    )
    from_last, from_next = moved(plus, 0, 1, 0), moved(minus, 0, 3, 0)
    up, down = moved(up, 1, 1, 0), moved(down, 1, 3, 0)

    _, late_scalars = lax.optimization_barrier((attention, scalars))
    (blocks,) = called(
        blocks_kernel,
        (((group_count * slot_count, BS // 2, 2 * HD), jnp.bfloat16),),
        late_scalars,
        pair_held,
        pair_other,
        scratch=(pltpu.VMEM((TOK, HD), jnp.float32),) * 2,
    )
    blocks = blocks.reshape(group_count, slot_count, BS // 2, 2 * HD)
    arrived = lax.ppermute(blocks[4:], "group", [(0, 4)])

    plus, minus, partner = called(
        second_message_kernel,
        (shard, shard, shard),
        None,
        next_part,
        last_part,
        partner_part,
        from_last,
        from_next,
        up,
        down,
        streamed=(arrived,),
    )
    from_last, from_next = moved(plus, 0, 1, 0), moved(minus, 0, 3, 0)
    from_partner = moved(partner, 1, 0, 0)

    blocks = jnp.where(picks[0], arrived, blocks[:4])
    sent = lax.ppermute(blocks[2:], "group", [(0, 2), (4, 6)])
    blocks = jnp.where(picks[1], sent, blocks[:2])
    sent = lax.ppermute(blocks[1:], "group", [(0, 1), (2, 3), (4, 5), (6, 7)])
    incoming = jnp.where(picks[2], sent, blocks[:1])
    (projected,) = called(
        total_kernel, (shard,), None, here_part, from_last, from_next, from_partner
    )
    return (projected[None], incoming)


def solution(mesh):
    in_specs = (
        P("group", None, "tp"),
        P(None, "tp"),
        P(None, "tp"),
        P("tp", None),
        P("group", None, "tp", None),
        P("group", None, "tp", None),
        P("group", None),
        P(),
    )
    out_specs = (P("group", None, "tp"), P("group", None, "tp", None))
    return jax.shard_map(
        on_device, mesh=mesh, in_specs=in_specs, out_specs=out_specs, check_vma=False
    )
```

```python
import jax
import jax.numpy as jnp
from jax import lax
from jax.experimental import pallas as pl
from jax.experimental.pallas import tpu as pltpu
from jax.sharding import PartitionSpec as P

HD = 128
KVH = 8
STEPS = 4
NPR = 2
BS = 16
R = 64
GQ = 4
TOK = 256
CH = 128
RP = 32


NEG_FILL = -1e30


def tp_index(x_hi, y, core):
    return x_hi * 8 + (y % 4) * 2 + core


def moved(shard, x_flip, y_step, core_flip):
    pairs = []
    for x_hi in range(2):
        for y in range(4):
            for core in range(2):
                pairs.append(
                    (
                        tp_index(x_hi, y, core),
                        tp_index(x_hi ^ x_flip, y + y_step, core ^ core_flip),
                    )
                )
    return lax.ppermute(shard, "tp", pairs)


def core_swap(shard):
    return moved(shard, 0, 0, 1)


def turns(positions):
    midpoint = HD // 2
    frequency = jnp.exp(
        -jnp.log(500000.0) * jnp.arange(midpoint, dtype=jnp.float32) * 2.0 / HD
    )
    angles = positions.astype(jnp.float32)[:, None] * frequency[None, :]
    cosine = jnp.cos(angles)
    sine = jnp.sin(angles)
    return (
        jnp.concatenate([cosine, cosine], axis=1),
        jnp.concatenate([-sine, sine], axis=1),
    )


SPAN = 256
CHIPS = 8
SHARD = 512
HALF = TOK // 2
PREFILL_CHUNK = 4096
ROWS_AT_ONCE = 4
LOG2_E = 1.4426950408889634
NT = (((1,), (1,)), ((), ()))
LONG = 6 * 10**9

CORE, IS_PREFILL, IS_KEY, NEAR_ROWS, FAR_ROWS, PLACE, CELLS = 0, 1, 2, 3, 11, 19, 27


def stacked_heads(*parts):
    return jnp.concatenate(
        [part[:, j * HD : (j + 1) * HD] for part in parts for j in range(part.shape[1] // HD)],
        axis=0,
    )


def length_bias(scalar_ref, length_ref, first, count):
    place = lax.broadcasted_iota(jnp.int32, (1, SPAN), 1) + scalar_ref[CORE] * SPAN
    return jnp.concatenate(
        [jnp.where(place < length_ref[first + row], 0.0, NEG_FILL) for row in range(count)],
        axis=1,
    )


def weights_of(scores, largest):
    return jnp.exp2((scores - largest) * (HD**-0.5 * LOG2_E)).astype(jnp.bfloat16)


def with_ones(values):
    return jnp.concatenate([values, jnp.ones_like(values)], axis=1)


def write_heads(mixed_ref, level_ref, rows, mixed, largest):
    count = mixed.shape[0] // GQ
    total = mixed[:, HD : HD + 1]
    normal = (mixed[:, :HD] / total).astype(jnp.bfloat16)
    level = largest * HD**-0.5 + jnp.log(total)
    lane = lax.broadcasted_iota(jnp.int32, (count, GQ), 1)
    levels = jnp.zeros((count, GQ), jnp.float32)
    for j in range(GQ):
        part = slice(j * count, (j + 1) * count)
        mixed_ref[rows, j * HD : (j + 1) * HD] = normal[part]
        levels = jnp.where(lane == j, level[part], levels)
    level_ref[rows, :] = levels


def prefill_kernel(
    scalar_ref,
    length_ref,
    own_ref,
    other_ref,
    key_ref,
    value_ref,
    mixed_ref,
    level_ref,
    keys,
    values,
    score_ref,
    sems,
):
    rows = PREFILL_CHUNK // SPAN
    chunks = RP // rows

    def fetches(prompt, step):
        part = pl.ds(prompt * RP + step * rows, rows)
        index = prompt * chunks + step
        return (
            pltpu.make_async_copy(key_ref.at[part], keys.at[part], sems.at[0, index]),
            pltpu.make_async_copy(value_ref.at[part], values.at[part], sems.at[1, index]),
        )

    for prompt in range(NPR):
        for kind in range(2):
            for step in range(chunks):
                fetches(prompt, step)[kind].start()

    def one_prompt(prompt, carry):
        tokens = pl.ds(pl.multiple_of(prompt * CH, CH), CH)
        queries = stacked_heads(own_ref[tokens, :], other_ref[tokens, :])

        def score_step(step, peak):
            fetches(prompt, step)[0].wait()
            part = keys[pl.ds(prompt * RP + step * rows, rows)].reshape(PREFILL_CHUNK, HD)
            scores = lax.dot_general(queries, part, NT, preferred_element_type=jnp.float32)
            scores = scores + length_bias(scalar_ref, length_ref, prompt * RP + step * rows, rows)
            score_ref[step] = scores
            for lanes in range(PREFILL_CHUNK // HD):
                peak = jnp.maximum(peak, scores[:, lanes * HD : (lanes + 1) * HD])
            return peak

        peak = lax.fori_loop(
            0, chunks, score_step, jnp.full((GQ * CH, HD), NEG_FILL, jnp.float32)
        )
        largest = jnp.max(peak, axis=1, keepdims=True)
        level = jnp.broadcast_to(largest, (GQ * CH, HD))

        def mix_step(step, mixed):
            fetches(prompt, step)[1].wait()
            weights = jnp.concatenate(
                [
                    weights_of(score_ref[step, :, lanes * HD : (lanes + 1) * HD], level)
                    for lanes in range(PREFILL_CHUNK // HD)
                ],
                axis=1,
            )
            part = values[pl.ds(prompt * RP + step * rows, rows)].reshape(PREFILL_CHUNK, HD)
            return mixed + jnp.dot(weights, with_ones(part), preferred_element_type=jnp.float32)

        mixed = lax.fori_loop(0, chunks, mix_step, jnp.zeros((GQ * CH, 2 * HD), jnp.float32))
        write_heads(mixed_ref, level_ref, tokens, mixed, largest)
        return carry

    lax.fori_loop(0, NPR, one_prompt, 0)


def decode_kernel(
    scalar_ref, length_ref, query_ref, key_ref, value_ref, mixed_ref, level_ref
):
    width = ROWS_AT_ONCE * SPAN
    tokens = ROWS_AT_ONCE * STEPS
    owner = lax.broadcasted_iota(jnp.int32, (GQ * tokens, width), 0) % tokens // STEPS
    holder = lax.broadcasted_iota(jnp.int32, (GQ * tokens, width), 1) // SPAN
    for part in range(query_ref.shape[0] // tokens):
        rows = slice(part * tokens, (part + 1) * tokens)
        cached = slice(part * ROWS_AT_ONCE, (part + 1) * ROWS_AT_ONCE)
        queries = stacked_heads(query_ref[rows, :])
        keys = key_ref[cached].reshape(width, HD)
        values = value_ref[cached].reshape(width, HD)
        scores = lax.dot_general(queries, keys, NT, preferred_element_type=jnp.float32)
        first = (pl.program_id(0) * (query_ref.shape[0] // tokens) + part) * ROWS_AT_ONCE
        bias = length_bias(scalar_ref, length_ref, first, ROWS_AT_ONCE)
        scores = jnp.where(owner == holder, scores + bias, NEG_FILL)
        largest = jnp.max(scores, axis=1, keepdims=True)
        mixed = jnp.dot(
            weights_of(scores, largest), with_ones(values), preferred_element_type=jnp.float32
        )
        write_heads(mixed_ref, level_ref, rows, mixed, largest)


def sort_pair(scalar_ref, held_ref, swapped_ref, keys, values):
    @pl.when(scalar_ref[CORE] == 0)
    def _():
        keys[...] = held_ref[...].astype(keys.dtype)
        values[...] = swapped_ref[...].astype(values.dtype)

    @pl.when(scalar_ref[CORE] != 0)
    def _():
        keys[...] = swapped_ref[...].astype(keys.dtype)
        values[...] = held_ref[...].astype(values.dtype)


def recent_kernel(scalar_ref, own_ref, other_ref, held_ref, swapped_ref, mixed_ref, level_ref):
    row = lax.broadcasted_iota(jnp.int32, (TOK, TOK), 0)
    column = lax.broadcasted_iota(jnp.int32, (TOK, TOK), 1)
    is_prefill = scalar_ref[IS_PREFILL] != 0
    together = jnp.where(is_prefill, row // CH - column // CH, row % R - column % R) == 0
    allowed = together & (column <= row)
    lane = lax.broadcasted_iota(jnp.int32, (TOK, GQ), 1)

    held = held_ref[...].astype(jnp.float32)
    swapped = swapped_ref[...].astype(jnp.float32)
    first = scalar_ref[CORE] == 0
    keys = jnp.where(first, held, swapped).astype(jnp.bfloat16)
    values = with_ones(jnp.where(first, swapped, held).astype(jnp.bfloat16))
    levels = jnp.zeros((TOK, GQ), jnp.float32)
    for j in range(GQ):
        source = own_ref if j < GQ // 2 else other_ref
        part = slice(j % (GQ // 2) * HD, (j % (GQ // 2) + 1) * HD)
        scores = lax.dot_general(
            source[:, part], keys, NT, preferred_element_type=jnp.float32
        )
        scores = jnp.where(allowed, scores, NEG_FILL)
        largest = jnp.max(scores, axis=1, keepdims=True)
        mixed = jnp.dot(
            weights_of(scores, largest), values, preferred_element_type=jnp.float32
        )
        total = mixed[:, HD : HD + 1]
        mixed_ref[:, j * HD : (j + 1) * HD] = (mixed[:, :HD] / total).astype(mixed_ref.dtype)
        levels = jnp.where(lane == j, largest * HD**-0.5 + jnp.log(total), levels)
    level_ref[...] = levels


def merged(parts, levels):
    half = GQ // 2
    turned = jnp.concatenate([levels[1][:, half:], levels[1][:, :half]], axis=1)
    levels = [levels[0], turned, levels[2]]
    top = jnp.maximum(jnp.maximum(levels[0], levels[1]), levels[2])
    shares = [jnp.exp(level - top) for level in levels]
    total = shares[0] + shares[1] + shares[2]
    shares = [share / total for share in shares]
    heads = []
    for j in range(GQ):
        mixed = jnp.zeros((TOK, HD), jnp.float32)
        for part, share, place in zip(parts, shares, (j, (j + half) % GQ, j)):
            values = part[:, place * HD : (place + 1) * HD].astype(jnp.float32)
            mixed = mixed + values * share[:, j : j + 1]
        heads.append(mixed.astype(jnp.bfloat16))
    return jnp.concatenate(heads, axis=1)


def swapped_copies(scalar_ref, first, swapped_ref, held_ref, sems):
    copies = []
    for index in range(4):
        columns = pl.ds(pl.multiple_of(scalar_ref[PLACE + first + index] * SHARD, SHARD), SHARD)
        copies.append(
            pltpu.make_async_copy(
                swapped_ref.at[:, columns], held_ref.at[index], sems.at[index]
            )
        )
        copies[-1].start()
    return copies


def product(scalar_ref, chip, joined, copy, weight_ref, held_ref, index):
    column = 2 * scalar_ref[PLACE + chip] + scalar_ref[CORE]
    own = weight_ref[:, pl.ds(pl.multiple_of(column * SHARD, SHARD), SHARD)]
    copy.wait()
    weights = jnp.concatenate([own, held_ref[index]], axis=0)
    return jnp.dot(joined, weights, preferred_element_type=jnp.float32).astype(jnp.bfloat16)


def merge_out_kernel(
    scalar_ref,
    swapped_ref,
    weight_ref,
    own_ref,
    own_level,
    other_ref,
    other_level,
    recent_ref,
    recent_level,
    plus,
    minus,
    up,
    down,
    attention,
    held_ref,
    sems,
):
    copies = swapped_copies(scalar_ref, 0, swapped_ref, held_ref, sems)
    joined = merged(
        (own_ref, other_ref, recent_ref), (own_level[...], other_level[...], recent_level[...])
    )
    attention[...] = joined
    parts = [
        product(scalar_ref, index, joined, copies[index], weight_ref, held_ref, index)
        for index in range(4)
    ]
    plus[:TOK] = parts[0]
    minus[:TOK] = parts[1]
    plus[TOK:] = parts[2][:HALF]
    minus[TOK:] = parts[2][HALF:]
    up[...] = parts[3][:HALF]
    down[...] = parts[3][HALF:]


def out_kernel(scalar_ref, swapped_ref, weight_ref, attention, *refs):
    *out_refs, held_ref, sems = refs
    copies = swapped_copies(scalar_ref, 4, swapped_ref, held_ref, sems)
    joined = attention[...]
    for index, ref in enumerate(out_refs):
        ref[...] = product(
            scalar_ref, 4 + index, joined, copies[index], weight_ref, held_ref, index
        )


def total_of(*parts):
    total = parts[0].astype(jnp.float32)
    for part in parts[1:]:
        total = total + part.astype(jnp.float32)
    return total.astype(jnp.bfloat16)


def partner_kernel(partner_ref, from_last, from_next, partner):
    partner[...] = total_of(partner_ref[...], from_last[:TOK], from_next[:TOK])


def second_message_kernel(
    arrived_ref, sent_ref, next_ref, last_ref, from_last, from_next, up, down, plus, minus
):
    plus[:HALF] = total_of(next_ref[:HALF], from_last[TOK:], up[...])
    plus[HALF:] = next_ref[HALF:]
    minus[:HALF] = last_ref[:HALF]
    minus[HALF:] = total_of(last_ref[HALF:], from_next[TOK:], down[...])


def total_kernel(here_ref, from_last, from_next, from_partner, out_ref):
    out_ref[...] = total_of(here_ref[...], from_last[...], from_next[...], from_partner[...])


def fetch_kernel(source_ref, out_ref, sem):
    copy = pltpu.make_async_copy(source_ref, out_ref, sem)
    copy.start()
    copy.wait()


def join_kernel(
    scalar_ref, own_ref, partner_ref, last_ref, next_ref, plus, minus, up, down, near
):
    plus[:TOK] = partner_ref[...]
    plus[TOK:] = last_ref[:HALF]
    minus[:TOK] = partner_ref[...]
    minus[TOK:] = next_ref[HALF:]
    up[...] = last_ref[HALF:]
    down[...] = next_ref[:HALF]
    for index, ref in enumerate((own_ref, last_ref, next_ref, partner_ref)):
        near[index * TOK : (index + 1) * TOK] = ref[...]


def sides_kernel(mark_ref, last_ref, next_ref, upper_ref, lower_ref, sides):
    sides[:TOK] = last_ref[:TOK]
    sides[TOK : 2 * TOK] = next_ref[:TOK]
    sides[2 * TOK : 2 * TOK + HALF] = last_ref[TOK:]
    sides[2 * TOK + HALF : 3 * TOK] = next_ref[TOK:]
    sides[3 * TOK : 3 * TOK + HALF] = upper_ref[...]
    sides[3 * TOK + HALF :] = lower_ref[...]


def projected_parts(scalar_ref, first, shards, query_weight, pair_weight):
    joined = jnp.concatenate(shards, axis=1)
    rows = [
        pl.ds(pl.multiple_of(scalar_ref[first + index], SHARD), SHARD)
        for index in range(len(shards))
    ]
    return [
        jnp.dot(
            joined,
            jnp.concatenate([weight[part, :] for part in rows], axis=0),
            preferred_element_type=jnp.float32,
        )
        for weight in (query_weight, pair_weight)
    ]


def four_shards(ref):
    return [ref[index * TOK : (index + 1) * TOK] for index in range(4)]


def near_kernel(scalar_ref, query_weight, pair_weight, near_ref, other_ref, query, pair, mark):
    mark[...] = jnp.zeros_like(mark)
    query[...], pair[...] = projected_parts(
        scalar_ref,
        NEAR_ROWS,
        four_shards(near_ref) + four_shards(other_ref),
        query_weight,
        pair_weight,
    )


def far_kernel(
    scalar_ref,
    cosine_ref,
    sine_ref,
    query_weight,
    pair_weight,
    query_in,
    pair_in,
    far_ref,
    query,
    pair,
):
    sums = projected_parts(scalar_ref, FAR_ROWS, four_shards(far_ref), query_weight, pair_weight)
    query[...] = query_in[...] + sums[0]
    pair[...] = pair_in[...] + sums[1]


def last_kernel(
    scalar_ref,
    query_weight,
    pair_weight,
    query_in,
    pair_in,
    far_ref,
    cosine_ref,
    sine_ref,
    query_out,
    pair_out,
):
    sums = projected_parts(
        scalar_ref, FAR_ROWS + 4, four_shards(far_ref), query_weight, pair_weight
    )
    query = query_in[...] + sums[0]
    pair = pair_in[...] + sums[1]
    cosine = cosine_ref[...]
    sine = sine_ref[...]

    def rotated(values):
        return values * cosine + pltpu.roll(values, HD // 2, 1) * sine

    for head in range(query.shape[1] // HD):
        part = slice(head * HD, (head + 1) * HD)
        query_out[:, part] = rotated(query[:, part]).astype(jnp.bfloat16)
    is_key = scalar_ref[IS_KEY] != 0
    pair_out[...] = jnp.where(is_key, rotated(pair), pair).astype(jnp.bfloat16)


def blocks_kernel(scalar_ref, held_ref, swapped_ref, out_ref, keys, values):
    sliver = out_ref.shape[1]
    out_ref[...] = jnp.zeros_like(out_ref)

    @pl.when(scalar_ref[IS_PREFILL] != 0)
    def _():
        sort_pair(scalar_ref, held_ref, swapped_ref, keys, values)
        for block in range(TOK // BS):
            start = pl.multiple_of(scalar_ref[CORE] * sliver, sliver) + block * BS
            cell = scalar_ref[CELLS + block]
            out_ref[cell, :, :HD] = keys[pl.ds(start, sliver), :].astype(jnp.bfloat16)
            out_ref[cell, :, HD:] = values[pl.ds(start, sliver), :].astype(jnp.bfloat16)


def called(kernel, shapes, scalars, *arrays, streamed=(), scratch=(), flops=0, grant=12):
    whole = pl.BlockSpec(memory_space=pltpu.VMEM)
    specs = [pl.BlockSpec(memory_space=pl.ANY)] * len(streamed) + [whole] * len(arrays)
    arrays = tuple(streamed) + arrays
    if scalars is not None:
        specs = [pl.BlockSpec(memory_space=pltpu.SMEM)] + specs
        arrays = (scalars,) + arrays
    return pl.pallas_call(
        kernel,
        in_specs=specs,
        out_specs=tuple(whole for _ in shapes),
        out_shape=tuple(jax.ShapeDtypeStruct(shape, kind) for shape, kind in shapes),
        scratch_shapes=scratch,
        compiler_params=pltpu.CompilerParams(vmem_limit_bytes=grant * 2**20),
        cost_estimate=pl.CostEstimate(flops=flops, transcendentals=0, bytes_accessed=2**21),
    )(*arrays)


def outputs_of(kind):
    return (
        jax.ShapeDtypeStruct((TOK, GQ * HD), kind),
        jax.ShapeDtypeStruct((TOK, GQ), jnp.float32),
    )


def prefill_part(scalars, lengths, own, other, keys, values):
    chunks = RP * SPAN // PREFILL_CHUNK
    whole = pl.BlockSpec(memory_space=pltpu.VMEM)
    there = pl.BlockSpec(memory_space=pl.ANY)
    small = pl.BlockSpec(memory_space=pltpu.SMEM)
    return pl.pallas_call(
        prefill_kernel,
        in_specs=[small, small, whole, whole, there, there],
        out_specs=(whole, whole),
        out_shape=outputs_of(jnp.bfloat16),
        scratch_shapes=[
            pltpu.VMEM((R, SPAN, HD), jnp.bfloat16),
            pltpu.VMEM((R, SPAN, HD), jnp.bfloat16),
            pltpu.VMEM((chunks, GQ * CH, PREFILL_CHUNK), jnp.float32),
            pltpu.SemaphoreType.DMA((2, NPR * chunks)),
        ],
        compiler_params=pltpu.CompilerParams(vmem_limit_bytes=44 * 2**20),
    )(scalars, lengths, own, other, keys, values)


def decode_part(scalars, lengths, own, other, keys, values):
    def by_row(array):
        return array.reshape(STEPS, R, -1).transpose(1, 0, 2).reshape(TOK, -1)

    def by_step(array):
        return array.reshape(R, STEPS, -1).transpose(1, 0, 2).reshape(TOK, -1)

    rows = 8 * ROWS_AT_ONCE
    mixed, level = pl.pallas_call(
        decode_kernel,
        grid=(R // rows,),
        in_specs=[
            pl.BlockSpec(memory_space=pltpu.SMEM),
            pl.BlockSpec(memory_space=pltpu.SMEM),
            pl.BlockSpec((rows * STEPS, GQ * HD), lambda i: (i, 0)),
            pl.BlockSpec((rows, SPAN, HD), lambda i: (i, 0, 0)),
            pl.BlockSpec((rows, SPAN, HD), lambda i: (i, 0, 0)),
        ],
        out_specs=(
            pl.BlockSpec((rows * STEPS, GQ * HD), lambda i: (i, 0)),
            pl.BlockSpec((rows * STEPS, GQ), lambda i: (i, 0)),
        ),
        out_shape=outputs_of(jnp.bfloat16),
        compiler_params=pltpu.CompilerParams(vmem_limit_bytes=40 * 2**20),
    )(scalars, lengths, by_row(jnp.concatenate([own, other], axis=1)), keys, values)
    return by_step(mixed), by_step(level)


def cut_kernel(scalar_ref, weight_ref, out_ref, held_ref, in_sems, out_sems):
    fetches = []
    stores = []
    for chip in range(CHIPS):
        columns = pl.ds(pl.multiple_of((2 * chip + 1 - scalar_ref[CORE]) * SHARD, SHARD), SHARD)
        fetches.append(
            pltpu.make_async_copy(weight_ref.at[:, columns], held_ref.at[chip], in_sems.at[chip])
        )
        stores.append(
            pltpu.make_async_copy(
                held_ref.at[chip],
                out_ref.at[:, chip * SHARD : (chip + 1) * SHARD],
                out_sems.at[chip],
            )
        )
    for fetch in fetches:
        fetch.start()
    for fetch, store in zip(fetches, stores):
        fetch.wait()
        store.start()
    for store in stores:
        store.wait()


def cut_columns(scalars, out_weight):
    return pl.pallas_call(
        cut_kernel,
        in_specs=[
            pl.BlockSpec(memory_space=pltpu.SMEM),
            pl.BlockSpec(memory_space=pl.ANY),
        ],
        out_specs=pl.BlockSpec(memory_space=pl.ANY),
        out_shape=jax.ShapeDtypeStruct((out_weight.shape[0], CHIPS * SHARD), jnp.bfloat16),
        scratch_shapes=[
            pltpu.VMEM((CHIPS, out_weight.shape[0], SHARD), jnp.bfloat16),
            pltpu.SemaphoreType.DMA((CHIPS,)),
            pltpu.SemaphoreType.DMA((CHIPS,)),
        ],
        compiler_params=pltpu.CompilerParams(vmem_limit_bytes=12 * 2**20),
    )(scalars, out_weight)


def on_device(
    layer_input, query_weight, kv_weight, out_weight, cache_keys, cache_values, lengths, placement
):
    group_count = lax.axis_size("group")
    tp_rank = lax.axis_index("tp")
    group_rank = lax.axis_index("group")
    core = tp_rank % 2
    y = (tp_rank // 2) % 4
    x_hi = tp_rank // 8
    is_prefill = group_rank == 0
    tokens = layer_input[0]
    row_lengths = lengths[0]
    slot_count = 2 * (TOK // BS) // (group_count - 1)

    def rows_of(*owners):
        firsts = [tp_index(x_hi ^ flip, y + step, core) for flip, step in owners]
        return [first * SHARD for first in firsts] + [(first ^ 1) * SHARD for first in firsts]

    places = ((1, 1), (1, 3), (0, 2), (1, 2), (0, 1), (0, 3), (1, 0), (0, 0))
    single = (
        [core, is_prefill, tp_rank < KVH]
        + rows_of((0, 0), (0, 3), (0, 1), (1, 0))
        + rows_of((1, 3), (1, 1), (0, 2), (1, 2))
        + [(x_hi ^ flip) * 4 + (y + step) % 4 for flip, step in places]
    )
    picks = [group_rank >= 4, group_rank // 2 % 2 == 1, group_rank % 2 == 1]
    scalars = jnp.concatenate(
        [
            jnp.stack([jnp.asarray(one, jnp.int32) for one in single]),
            placement[:, 0] * slot_count + placement[:, 1],
        ]
    )
    prefix = jnp.sum(row_lengths.reshape(NPR, RP), axis=1)
    prompt_positions = (prefix[:, None] + jnp.arange(CH, dtype=jnp.int32)[None, :]).reshape(TOK)
    decode_step_positions = (
        row_lengths[None, :] + jnp.arange(STEPS, dtype=jnp.int32)[:, None]
    ).reshape(TOK)
    positions = jnp.where(is_prefill, prompt_positions, decode_step_positions)

    cut_out = cut_columns(scalars, out_weight)

    wide = ((TOK + HALF, SHARD), jnp.bfloat16)
    half = ((HALF, SHARD), jnp.bfloat16)
    shard = ((TOK, SHARD), jnp.bfloat16)
    four = ((4 * TOK, SHARD), jnp.bfloat16)
    weights = (query_weight, kv_weight)
    sums = (((TOK, query_weight.shape[1]), jnp.float32), ((TOK, kv_weight.shape[1]), jnp.float32))
    partner_tokens = moved(tokens, 1, 0, 0)
    last_tokens, next_tokens = moved(tokens, 0, 1, 0), moved(tokens, 0, 3, 0)
    scalars, picks, positions = lax.optimization_barrier((scalars, picks, positions))
    cosine, sine = turns(positions)
    (own_tokens,) = called(
        fetch_kernel,
        (shard,),
        None,
        streamed=(tokens,),
        scratch=(pltpu.SemaphoreType.DMA(()),),
    )
    plus, minus, up, down, near = called(
        join_kernel,
        (wide, wide, half, half, four),
        scalars,
        own_tokens,
        partner_tokens,
        last_tokens,
        next_tokens,
        flops=LONG,
    )
    from_last, from_next = moved(plus, 0, 1, 0), moved(minus, 0, 3, 0)
    far_upper, far_lower = moved(down, 1, 3, 0), moved(up, 1, 1, 0)
    scalars, cut_out = lax.optimization_barrier((scalars, cut_out))
    *part, mark = called(
        near_kernel,
        sums + (((8, HD), jnp.float32),),
        scalars,
        *weights,
        near,
        core_swap(near),
        flops=2 * TOK * 8 * SHARD * 3 * HD,
    )
    (sides,) = called(
        sides_kernel,
        (four,),
        None,
        from_last,
        from_next,
        far_upper,
        far_lower,
        streamed=(mark,),
    )
    other_sides = core_swap(sides)
    part = called(
        far_kernel,
        sums,
        scalars,
        *weights,
        *part,
        sides,
        streamed=(cosine, sine),
        flops=2 * TOK * 4 * SHARD * 3 * HD,
    )
    _, _, cut_out = lax.optimization_barrier((other_sides, part[1], cut_out))
    swapped_out = core_swap(cut_out)
    query_local, pair_local = called(
        last_kernel,
        tuple((shape, jnp.bfloat16) for shape, _ in sums),
        scalars,
        *weights,
        *part,
        other_sides,
        cosine,
        sine,
        flops=2 * TOK * 4 * SHARD * 3 * HD,
    )
    query_other = core_swap(query_local)
    pair_held = lax.ppermute(
        pair_local, "tp", [(t, 2 * t if t < KVH else 2 * (t - KVH) + 1) for t in range(2 * KVH)]
    )
    cached = lax.cond(
        is_prefill,
        prefill_part,
        decode_part,
        scalars,
        row_lengths,
        query_local,
        query_other,
        cache_keys[0],
        cache_values[0],
    )
    cached, pair_held = lax.optimization_barrier((cached, pair_held))
    pair_other = core_swap(pair_held)
    other_cached = (core_swap(cached[0]), core_swap(cached[1]))
    recent = called(
        recent_kernel,
        (((TOK, GQ * HD), jnp.bfloat16), ((TOK, GQ), jnp.float32)),
        scalars,
        query_local,
        query_other,
        pair_held,
        pair_other,
        flops=LONG,
    )

    product_scratch = (
        pltpu.VMEM((4, out_weight.shape[0], SHARD), jnp.bfloat16),
        pltpu.SemaphoreType.DMA((4,)),
    )
    plus, minus, up, down, attention = called(
        merge_out_kernel,
        (wide, wide, half, half, ((TOK, GQ * HD), jnp.bfloat16)),
        scalars,
        out_weight,
        *cached,
        *other_cached,
        *recent,
        streamed=(swapped_out,),
        scratch=product_scratch,
        flops=2 * TOK * 4 * SHARD * GQ * HD,
    )
    next_part, last_part, partner_part, here_part = called(
        out_kernel,
        (shard,) * 4,
        scalars,
        out_weight,
        attention,
        streamed=(swapped_out,),
        scratch=product_scratch,
        flops=2 * TOK * 4 * SHARD * GQ * HD,
    )
    from_last, from_next = moved(plus, 0, 1, 0), moved(minus, 0, 3, 0)
    up, down = moved(up, 1, 1, 0), moved(down, 1, 3, 0)

    _, late_scalars = lax.optimization_barrier((attention, scalars))
    (blocks,) = called(
        blocks_kernel,
        (((group_count * slot_count, BS // 2, 2 * HD), jnp.bfloat16),),
        late_scalars,
        pair_held,
        pair_other,
        scratch=(pltpu.VMEM((TOK, HD), jnp.float32),) * 2,
    )
    blocks = blocks.reshape(group_count, slot_count, BS // 2, 2 * HD)
    arrived = lax.ppermute(blocks[4:], "group", [(0, 4)])

    (partner,) = called(partner_kernel, (shard,), None, partner_part, from_last, from_next)
    plus, minus = called(
        second_message_kernel,
        (shard, shard),
        None,
        next_part,
        last_part,
        from_last,
        from_next,
        up,
        down,
        streamed=(arrived, partner),
    )
    from_last, from_next = moved(plus, 0, 1, 0), moved(minus, 0, 3, 0)
    from_partner = moved(partner, 1, 0, 0)

    blocks = jnp.where(picks[0], arrived, blocks[:4])
    sent = lax.ppermute(blocks[2:], "group", [(0, 2), (4, 6)])
    blocks = jnp.where(picks[1], sent, blocks[:2])
    sent = lax.ppermute(blocks[1:], "group", [(0, 1), (2, 3), (4, 5), (6, 7)])
    incoming = jnp.where(picks[2], sent, blocks[:1])
    (projected,) = called(
        total_kernel, (shard,), None, here_part, from_last, from_next, from_partner
    )
    return (projected[None], incoming)


def solution(mesh):
    in_specs = (
        P("group", None, "tp"),
        P(None, "tp"),
        P(None, "tp"),
        P("tp", None),
        P("group", None, "tp", None),
        P("group", None, "tp", None),
        P("group", None),
        P(),
    )
    out_specs = (P("group", None, "tp"), P("group", None, "tp", None))
    return jax.shard_map(
        on_device, mesh=mesh, in_specs=in_specs, out_specs=out_specs, check_vma=False
    )
```
